32 devices in a mesh: gx: 2 (over y), gy: 4 (over z), gz: 4 (over x, core).
Axes of the slice: x: 2, y: 2, z: 4, core: 2. Of those that a mesh axis runs over, the one named last changes fastest.
Arguments:
- right_side: float32 [32, 64, 1024], P('gx', 'gy', 'gz'), may hold values from -8 to 8
- conductance: float32 [3, 32, 64, 1024], P(None, 'gx', 'gy', 'gz'), may hold values from 0.2 to 5
- storage: float32 [32, 64, 1024], P('gx', 'gy', 'gz'), may hold values from 0.05 to 0.8
- dirichlet: int32 [32, 64, 1024], P('gx', 'gy', 'gz'), may hold values 0 or 1
- basis: float32 [16, 32, 64, 1024], P(None, 'gx', 'gy', 'gz'), may hold values from -2 to 2
- coarse_inverse: float32 [512, 512], P(('gx', 'gy', 'gz')), may hold values from 0 to 2, as said below
Outputs:
- solution_field: float32 [32, 64, 1024], P('gx', 'gy', 'gz')
- residual: float32 [32, 64, 1024], P('gx', 'gy', 'gz')
The draws below stay inside these ranges and needn't reach their ends.
Inputs may be any that keep to these rules, and one draw needn't show every extreme that they name: `coarse_inverse`: symmetric positive definite.
All inputs are finite; a program needn't handle non-finite values. No bound on the sum of `dirichlet` on one device may be relied on, other than what follows from the above.
Results may differ from the reference program's by a relative error of at most 0.0003.
Values sent between devices are 32-bit elements; how exact they have to be, the bound alone decides.
No kernel may reach another device: no remote copies, remote signals or barrier semaphores. Data moves between devices by JAX's collectives and lax.ppermute only.
A program may use at most 128 MiB of HBM per device.

```python
import math
import jax
import jax.numpy as jnp
from jax import lax

CX = 16
CY = 16
CZ = 256
VECS = 16
SWEEPS = 4
ITERS = 2
NX = 32
NY = 64
NZ = 1024
NC = 512
N_GX = 2
N_GY = 4
N_GZ = 4


def draw_right_side(key, part):
    pos_x = (jnp.arange(NX, dtype=jnp.float32) + 0.5) / NX
    pos_y = (jnp.arange(NY, dtype=jnp.float32) + 0.5) / NY
    pos_z = (jnp.arange(NZ, dtype=jnp.float32) + 0.5) / NZ
    smooth = 1.0 + 0.5 * jnp.sin(2.0 * math.pi * pos_x)[:, None, None] * jnp.cos(math.pi * pos_y)[None, :, None] + 0.3 * jnp.cos(2.0 * math.pi * pos_z)[None, None, :]
    rough = jax.random.truncated_normal(key, -4.0, 4.0, (NX, NY, NZ), jnp.float32)
    return rough + 0.5 * smooth


def draw_basis(key, part):
    local_x = ((jnp.arange(NX) % CX).astype(jnp.float32) + 0.5) / CX
    local_y = ((jnp.arange(NY) % CY).astype(jnp.float32) + 0.5) / CY
    local_z = ((jnp.arange(NZ) % CZ).astype(jnp.float32) + 0.5) / CZ
    order = jnp.arange(VECS)
    first = (order // 8).astype(jnp.float32)
    second = (order // 4 % 2).astype(jnp.float32)
    third = (order % 4).astype(jnp.float32)
    mode = jnp.cos(math.pi * first[:, None, None, None] * local_x[None, :, None, None]) * jnp.cos(math.pi * second[:, None, None, None] * local_y[None, None, :, None]) * jnp.cos(math.pi * third[:, None, None, None] * local_z[None, None, None, :])
    noise = jax.random.uniform(key, (VECS, NX, NY, NZ), jnp.float32, -1.0, 1.0)
    rough = 1.0 + 0.3 * noise
    return mode * rough / math.sqrt(CX * CY * CZ)


def draw_coarse_inverse(key, part):
    key_scale = jax.random.fold_in(key, 11)
    key_diag = jax.random.fold_in(key, 12)
    rows = jnp.arange(NC)
    owner = rows // VECS
    vector = rows % VECS
    sub_x = owner // (N_GY * N_GZ)
    sub_y = owner // N_GZ % N_GY
    sub_z = owner % N_GZ
    reach = 2.0
    scales = jnp.exp(jax.random.uniform(key_scale, (NC,), jnp.float32, math.log(0.3), 0.0))
    gap = jnp.abs(sub_x[:, None] - sub_x[None, :]) + jnp.abs(sub_y[:, None] - sub_y[None, :]) + jnp.abs(sub_z[:, None] - sub_z[None, :])
    spread = jnp.abs(vector[:, None] - vector[None, :])
    kernel = jnp.exp(-gap.astype(jnp.float32) / reach) * jnp.exp(-spread.astype(jnp.float32) / 3.0)
    coupled = 0.06 * scales[:, None] * scales[None, :] * kernel
    diag = 0.5 + jax.random.uniform(key_diag, (NC,), jnp.float32)
    same = rows[:, None] == rows[None, :]
    return coupled + jnp.where(same, diag[:, None], 0.0)


def touch_ends(result, stream_key, low, largest):
    shape = result.shape
    place = [jax.random.randint(jax.random.fold_in(stream_key, axis), (), 0, shape[axis]) for axis in range(len(shape))]
    result = result.at[tuple(place)].set(low)
    longest = shape.index(max(shape))
    place[longest] = (place[longest] + 1) % shape[longest]
    return result.at[tuple(place)].set(largest)


def block_levels(key, dims, cuts, smallest, largest):
    def one(dim, blocks):
        steps = jax.random.uniform(jax.random.fold_in(jax.random.fold_in(key, 6), dim), (blocks,), jnp.float32, smallest / len(cuts), largest / len(cuts))
        return jnp.repeat(jnp.exp(steps), dims[dim] // blocks).reshape((-1,) + (1,) * (len(dims) - dim - 1))

    loudness = one(*cuts[0])
    for cut in cuts[1:]:
        loudness = loudness * one(*cut)
    return loudness


def setup_inputs(seed: int = 0) -> dict:
    key_of = jax.random.split(jax.random.key(seed), 7)
    right_side = draw_right_side(jax.random.fold_in(key_of[6], 71), 0)
    conductance = jnp.clip(jnp.exp(math.log(5.0) - 3.218876 * jax.random.uniform(key_of[1], (3, NX, NY, NZ), jnp.float32) ** block_levels(key_of[1], (3, NX, NY, NZ), ((1, 2), (2, 4), (3, 4)), -0.2, 0.2)), 0.2, 5.0)
    storage = jnp.clip(jnp.exp(math.log(0.8) - 2.7725887 * jax.random.uniform(key_of[2], (NX, NY, NZ), jnp.float32) ** block_levels(key_of[2], (NX, NY, NZ), ((0, 2), (1, 4), (2, 4)), -0.2, 0.2)), 0.05, 0.8)
    dirichlet = touch_ends((jax.random.randint(key_of[3], (NX, NY, NZ), 0, 16) < 1).astype(jnp.int32), jax.random.fold_in(key_of[3], 1), 0, 1)
    basis = draw_basis(jax.random.fold_in(key_of[6], 71), 0)
    coarse_inverse = draw_coarse_inverse(jax.random.fold_in(key_of[6], 71), 0)
    return dict(right_side=right_side, conductance=conductance, storage=storage, dirichlet=dirichlet, basis=basis, coarse_inverse=coarse_inverse)


RELAX = 2.0 / 3.0


def pad_cond(cond):
    return jnp.pad(cond, ((0, 0), (1, 1), (1, 1), (1, 1)))


def stencil(padded_free, padded_cond, field, storage, free):
    middle = padded_free[1:-1, 1:-1, 1:-1]
    total = storage * middle
    total = total + padded_cond[0, 1:-1, 1:-1, 1:-1] * (middle - padded_free[2:, 1:-1, 1:-1]) + padded_cond[0, :-2, 1:-1, 1:-1] * (middle - padded_free[:-2, 1:-1, 1:-1])
    total = total + padded_cond[1, 1:-1, 1:-1, 1:-1] * (middle - padded_free[1:-1, 2:, 1:-1]) + padded_cond[1, 1:-1, :-2, 1:-1] * (middle - padded_free[1:-1, :-2, 1:-1])
    total = total + padded_cond[2, 1:-1, 1:-1, 1:-1] * (middle - padded_free[1:-1, 1:-1, 2:]) + padded_cond[2, 1:-1, 1:-1, :-2] * (middle - padded_free[1:-1, 1:-1, :-2])
    return free * total + (1.0 - free) * field


def diagonal_of(padded_cond, storage, free):
    total = storage + padded_cond[0, 1:-1, 1:-1, 1:-1] + padded_cond[0, :-2, 1:-1, 1:-1]
    total = total + padded_cond[1, 1:-1, 1:-1, 1:-1] + padded_cond[1, 1:-1, :-2, 1:-1]
    total = total + padded_cond[2, 1:-1, 1:-1, 1:-1] + padded_cond[2, 1:-1, 1:-1, :-2]
    return free * total + (1.0 - free)


def jacobi(rhs_box, padded_cond, diagonal, storage_box, free_box):
    guess = jnp.zeros_like(rhs_box)
    for sweep in range(SWEEPS):
        image = stencil(jnp.pad(free_box * guess, 1), padded_cond, guess, storage_box, free_box)
        guess = guess + RELAX * (rhs_box - image) / diagonal
    return guess


def reference(right_side, conductance, storage, dirichlet, basis, coarse_inverse):
    free = 1.0 - dirichlet.astype(jnp.float32)
    cond_pad = pad_cond(conductance)

    def apply(field):
        return stencil(jnp.pad(free * field, 1), cond_pad, field, storage, free)

    cond_two = jnp.pad(conductance, ((0, 0), (2, 2), (2, 2), (2, 2)))
    store_two = jnp.pad(storage, 2)
    free_two = jnp.pad(free, 2)
    count = N_GX * N_GY * N_GZ
    box_shape = (CX + 4, CY + 4, CZ + 4)

    def schwarz(residual):
        rhs_two = jnp.pad(residual, 2)

        def one(index):
            first = (index // (N_GY * N_GZ)) * CX
            second = ((index // N_GZ) % N_GY) * CY
            third = (index % N_GZ) * CZ
            rhs_box = lax.dynamic_slice(rhs_two, (first, second, third), box_shape)
            cond_box = lax.dynamic_slice(cond_two, (jnp.zeros((), jnp.int32), first, second, third), (3,) + box_shape)
            store_box = lax.dynamic_slice(store_two, (first, second, third), box_shape)
            free_box = lax.dynamic_slice(free_two, (first, second, third), box_shape)
            padded = pad_cond(cond_box)
            diagonal = diagonal_of(padded, store_box, free_box)
            return jacobi(rhs_box, padded, diagonal, store_box, free_box)[2:-2, 2:-2, 2:-2]

        blocks = lax.map(one, jnp.arange(count, dtype=jnp.int32))
        return blocks.reshape(N_GX, N_GY, N_GZ, CX, CY, CZ).transpose(0, 3, 1, 4, 2, 5).reshape(NX, NY, NZ)

    basis_six = basis.reshape(VECS, N_GX, CX, N_GY, CY, N_GZ, CZ)

    def coarse(residual):
        res_six = residual.reshape(N_GX, CX, N_GY, CY, N_GZ, CZ)
        parts = jnp.einsum('kaxbycz,axbycz->abck', basis_six, res_six, precision=lax.Precision.HIGHEST).reshape(-1)
        weights = jnp.dot(coarse_inverse, parts, precision=lax.Precision.HIGHEST).reshape(N_GX, N_GY, N_GZ, VECS)
        return jnp.einsum('abck,kaxbycz->axbycz', weights, basis_six, precision=lax.Precision.HIGHEST).reshape(NX, NY, NZ)

    def precondition(residual):
        return schwarz(residual) + coarse(residual)

    solution = jnp.zeros_like(right_side)
    residual = right_side
    precond = precondition(residual)
    norm_now = jnp.sum(residual * precond)
    direction = precond
    for step in range(ITERS):
        image = apply(direction)
        alpha = norm_now / jnp.sum(direction * image)
        solution = solution + alpha * direction
        residual = residual - alpha * image
        if step + 1 < ITERS:
            precond = precondition(residual)
            norm_next = jnp.sum(residual * precond)
            direction = precond + (norm_next / norm_now) * direction
            norm_now = norm_next
    return solution, residual
```

```python
import functools

import jax
import jax.numpy as jnp
from jax import lax
from jax.experimental import pallas as pl
from jax.experimental.pallas import tpu as pltpu
from jax.sharding import PartitionSpec as P

SWEEPS = 4
RELAX = 2.0 / 3.0
AXES = ("gx", "gy", "gz")
LANES = 128
COARSE_LANE = 96
VMEM_LIMIT = 40 * 1024 * 1024
F32 = jnp.float32


def rounds_of(count):
    return (0, 1)[: 1 if count <= 2 else 2]


def mate(index, odd, count):
    other = index + 1 if index % 2 == odd else index - 1
    return other if 0 <= other < count else None


def swap(value, sizes, along):
    pairs = []
    nx, ny, nz = sizes
    for ix in range(nx):
        for iy in range(ny):
            for iz in range(nz):
                here = [ix, iy, iz]
                there = [
                    mate(here[a], along[a], sizes[a]) if a in along else here[a] for a in range(3)
                ]
                if None in there:
                    if 2 in along:
                        spare = nz - 1 - iz if iz in (0, nz - 1) else None
                    else:
                        spare = iz ^ 1 if nz % 2 == 0 else None
                    if spare is None:
                        continue
                    there = [ix, iy, spare]
                pairs.append(
                    ((ix * ny + iy) * nz + iz, (there[0] * ny + there[1]) * nz + there[2])
                )
    return lax.ppermute(value, AXES, pairs)


def upward(index, odd):
    return lax.rem(index, 2) == odd


def where_am_i():
    return [lax.axis_index(a) for a in AXES]


def lane_iota(shape):
    return lax.broadcasted_iota(jnp.int32, shape, len(shape) - 1)


def pack_x(out, fields, odd, index, width):
    nx = fields[0].shape[0]
    high = upward(index, odd)
    for cond, first in ((high, nx - width), (jnp.logical_not(high), 0)):

        @pl.when(cond)
        def _(first=first):
            for k, field in enumerate(fields):
                out[k * width : (k + 1) * width] = field[first : first + width]


def pack_y(out, fields, odd, index, width):
    ny = fields[0].shape[1]
    high = upward(index, odd)
    for cond, first in ((high, ny - width), (jnp.logical_not(high), 0)):

        @pl.when(cond)
        def _(first=first):
            for k, field in enumerate(fields):
                for j in range(width):
                    out[k * width + j] = field[:, first + j, :]


def pack_xy(out, fields, rx, ry, ix, iy):
    nx, ny, _ = fields[0].shape
    for xhigh in (False, True):
        for yhigh in (False, True):

            @pl.when((upward(ix, rx) == xhigh) & (upward(iy, ry) == yhigh))
            def _(x0=(nx - 2 if xhigh else 0), y0=(ny - 2 if yhigh else 0)):
                for k, field in enumerate(fields):
                    for i in range(2):
                        out[4 * k + 2 * i : 4 * k + 2 * i + 2, :] = field[x0 + i, y0 : y0 + 2, :]


def pack_z(fields):
    nx, ny, nz = fields[0].shape
    lane = lane_iota((nx, ny, LANES))
    total = jnp.zeros((nx, ny, LANES), F32)
    for k, field in enumerate(fields):
        ends = jnp.where(lane < 64, field[:, :, 0:LANES], field[:, :, nz - LANES : nz])
        turned = pltpu.roll(ends, 4 * k + 2, 2)
        total = jnp.where((lane >= 4 * k) & (lane < 4 * k + 4), turned, total)
    return total


def edge_tiles(ends, count):
    nx, ny, _ = ends.shape
    rows = jnp.concatenate(
        [
            ends[0:2].reshape(2 * ny, LANES),
            ends[nx - 2 : nx].reshape(2 * ny, LANES),
            ends[:, 0, :],
            ends[:, 1, :],
            ends[:, ny - 2, :],
            ends[:, ny - 1, :],
        ],
        axis=0,
    )
    turned = rows.T
    lane = lane_iota((8, LANES))
    tiles = []
    for t in range(4):
        tile = jnp.zeros((8, LANES), F32)
        for q in range((4 * count + 7) // 8):
            part = pltpu.roll(turned[8 * q : 8 * q + 8, :], (32 * q - 32 * t) % LANES, 1)
            tile = jnp.where((lane >= 32 * q) & (lane < 32 * q + 32), part, tile)
        tiles.append(tile)
    return tiles


def project(basis_ref, field):
    vecs, nx, ny, nz = basis_ref.shape
    row = lax.broadcasted_iota(jnp.int32, (8, LANES), 0)
    lane = lane_iota((8, LANES))
    tile = jnp.zeros((8, LANES), F32)
    for k in range(vecs):
        prod = jnp.sum(basis_ref[k] * field, axis=0)
        part = jnp.zeros((8, LANES), F32)
        for y in range(ny // 8):
            for z in range(nz // LANES):
                part = part + prod[8 * y : 8 * y + 8, LANES * z : LANES * (z + 1)]
        value = jnp.sum(part)
        tile = jnp.where((row == 0) & (lane == COARSE_LANE + k), value, tile)
    return tile


def put_scalars(tile, values):
    row = lax.broadcasted_iota(jnp.int32, (8, LANES), 0)
    lane = lane_iota((8, LANES))
    for i, value in enumerate(values):
        tile = jnp.where((row == 1) & (lane == COARSE_LANE + i), value, tile)
    return tile


def fill_rows(out, sizes, tiles, common):
    ix, iy, _ = where_am_i()
    nx, ny, nz = sizes
    low_x, high_x, low_y, high_y = [t + common for t in tiles]
    for jx in range(nx):
        for jy in range(ny):
            tile = jnp.where(
                jx > ix, high_x, jnp.where(jx < ix, low_x, jnp.where(jy > iy, high_y, low_y))
            )
            for jz in range(nz):
                out[(jx * ny + jy) * nz + jz] = tile


def box_shape(shape):
    nx, ny, nz = shape
    return (nx + 6, ny + 8, nz + LANES)


def clear(box):
    def body(x, carry):
        box[x] = jnp.zeros(box.shape[1:], F32)
        return carry

    lax.fori_loop(0, box.shape[0], body, 0)


def each_round(sizes, a, index, act):
    for r in rounds_of(sizes[a]):
        high = upward(index, r)

        @pl.when(high & (index + 1 < sizes[a]))
        def _(r=r):
            act(r, True)

        @pl.when(jnp.logical_not(high) & (index > 0))
        def _(r=r):
            act(r, False)


def unpack_faces(boxes, owns, xs, ys, sizes, width):
    nx, ny, nz = owns[0].shape
    ix, iy, _ = where_am_i()
    for k, (box, own) in enumerate(zip(boxes, owns)):
        box[3 : 3 + nx, 0:ny, 0:nz] = own[...]

    def put_x(r, above):
        first = 3 + nx if above else 3 - width
        for k, box in enumerate(boxes):
            box[first : first + width, 0:ny, 0:nz] = xs[r][k * width : (k + 1) * width]

    each_round(sizes, 0, ix, put_x)

    def put_y(r, above):
        first = ny if above else ny + 8 - width
        for k, box in enumerate(boxes):
            for j in range(width):
                box[3 : 3 + nx, first + j, 0:nz] = ys[r][k * width + j]

    each_round(sizes, 1, iy, put_y)


def unpack_xy(boxes, shape, xys, sizes):
    nx, ny, nz = shape
    ix, iy, _ = where_am_i()

    def put(rx, xabove):
        x0 = 3 + nx if xabove else 1

        def inner(ry, yabove):
            y0 = ny if yabove else ny + 6
            for k, box in enumerate(boxes):
                for i in range(2):
                    box[x0 + i, y0 : y0 + 2, 0:nz] = xys[(rx, ry)][
                        4 * k + 2 * i : 4 * k + 2 * i + 2, :
                    ]

        each_round(sizes, 1, iy, inner)

    each_round(sizes, 0, ix, put)


def pick_z(zs, sizes, iz, shape):
    count = sizes[2]
    lane = lane_iota(shape)
    first = lax.rem(lane, 4) < 2
    total = jnp.zeros(shape, F32)
    for r in rounds_of(count):
        high = upward(iz, r)
        below = jnp.logical_not(high) & (iz > 0)
        above = high & (iz + 1 < count)
        total = jnp.where((first & below) | (jnp.logical_not(first) & above), zs[r][...], total)
    return total


def halo_lanes(tile, k):
    lane = lane_iota(tile.shape)
    axis = len(tile.shape) - 1
    turned = pltpu.roll(tile, (-(4 * k + 2)) % LANES, axis)
    return jnp.where((lane < 2) | (lane >= LANES - 2), turned, 0.0)


def unpack_z(boxes, shape, zs, sizes):
    nx, ny, nz = shape
    iz = lax.axis_index("gz")
    tile = pick_z(zs, sizes, iz, (nx, ny, LANES))
    for k, box in enumerate(boxes):
        box[3 : 3 + nx, 0:ny, nz : nz + LANES] = halo_lanes(tile, k)


def unpack_edges(boxes, shape, rows_ref, sizes):
    nx, ny, nz = shape
    here = where_am_i()
    combos = [(dx, dy) for dx in (-1, 0, 1) for dy in (-1, 0, 1) if dx or dy]
    row = lax.broadcasted_iota(jnp.int32, (8, LANES), 0)
    first = lax.rem(row, 4) < 2
    merged = []
    for dx, dy in combos:
        parts = []
        for dz in (-1, 1):
            spot = [h + d for h, d in zip(here, (dx, dy, dz))]
            valid = True
            for s, n in zip(spot, sizes):
                valid = valid & (s >= 0) & (s < n)
            spot = [jnp.clip(s, 0, n - 1) for s, n in zip(spot, sizes)]
            j = (spot[0] * sizes[1] + spot[1]) * sizes[2] + spot[2]
            parts.append(jnp.where(valid, rows_ref[j], 0.0))
        merged.append(jnp.where(first, parts[0], parts[1]))
    merged += [jnp.zeros((8, LANES), F32)] * (LANES // 8 - len(merged))
    turned = jnp.concatenate(merged, axis=0).T
    lane = lane_iota((32, LANES))
    for c, (dx, dy) in enumerate(combos):
        tile = jnp.zeros((32, LANES), F32)
        for q in range((4 * len(boxes) + 7) // 8):
            part = pltpu.roll(turned[32 * q : 32 * q + 32, :], (8 * q - 8 * c) % LANES, 1)
            tile = jnp.where((lane >= 8 * q) & (lane < 8 * q + 8), part, tile)
        for k, box in enumerate(boxes):
            piece = halo_lanes(tile, k)
            x0 = 1 if dx < 0 else 3 + nx
            y0 = ny + 6 if dy < 0 else ny
            if dx and dy:
                inside = ny - 2 if dy < 0 else 0
                for i in range(2):
                    box[x0 + i, y0 : y0 + 2, nz : nz + LANES] = piece[
                        i * ny + inside : i * ny + inside + 2
                    ]
            elif dx:
                box[x0 : x0 + 2, 0:ny, nz : nz + LANES] = piece.reshape(2, ny, LANES)
            else:
                for j in range(2):
                    box[3 : 3 + nx, y0 + j, nz : nz + LANES] = piece[j * nx : (j + 1) * nx]


def ahead(plane, axis):
    return pltpu.roll(plane, plane.shape[axis] - 1, axis)


def behind(plane, axis):
    return pltpu.roll(plane, 1, axis)


def neighbours(g, links, x):
    lx, ly, lz = links
    mid = g[x]
    y = ly[x]
    z = lz[x]
    total = lx[x] * g[x + 1] + lx[x - 1] * g[x - 1]
    total = total + y * ahead(mid, 0) + behind(y * mid, 0)
    return total + z * ahead(mid, 1) + behind(z * mid, 1)


def coefficients(fields, links, diag, step):
    tx, ty, tz, store, free, _ = fields
    lx, ly, lz = links
    last = tx.shape[0] - 1
    for ref in (lx, ly, lz, diag, step):
        ref[0] = jnp.zeros(ref.shape[1:], F32)
        ref[last] = jnp.zeros(ref.shape[1:], F32)

    def body(x, carry):
        f = free[x]
        a, b, c = tx[x], ty[x], tz[x]
        total = store[x] + a + tx[x - 1] + b + behind(b, 0) + c + behind(c, 1)
        d = f * total + (1.0 - f)
        diag[x] = d
        step[x] = RELAX / d
        lx[x] = a * f * free[x + 1]
        ly[x] = b * f * ahead(f, 0)
        lz[x] = c * f * ahead(f, 1)
        return carry

    lax.fori_loop(1, last, body, 0)


def jacobi(rhs, step, links, ga, gb, source):
    planes = rhs.shape[0]
    for g in (ga, gb):
        g[0] = jnp.zeros(g.shape[1:], F32)
        g[planes - 1] = jnp.zeros(g.shape[1:], F32)

    def first(x, carry):
        value = step[x] * rhs[x]
        source[x] = value
        ga[x] = value
        return carry

    lax.fori_loop(1, planes - 1, first, 0)
    now, then = ga, gb
    for sweep in range(1, SWEEPS):
        low, high = (3, planes - 3) if sweep == SWEEPS - 1 else (1, planes - 1)

        def body(x, carry, now=now, then=then):
            then[x] = (1.0 - RELAX) * now[x] + source[x] + step[x] * neighbours(now, links, x)
            return carry

        lax.fori_loop(low, high, body, 0)
        now, then = then, now
    return now


def coarse_sum(rows_ref):
    count = rows_ref.shape[0]
    each = 16
    per = LANES // each
    lane = lane_iota((count, LANES))
    row = lax.broadcasted_iota(jnp.int32, (count, LANES), 0)
    all_rows = rows_ref[:, 0, :]
    total = jnp.zeros((count, LANES), F32)
    for m in range(per):
        turned = pltpu.roll(all_rows, (each * m - COARSE_LANE) % LANES, 1)
        keep = (lax.rem(row, per) == m) & (lane >= each * m) & (lane < each * (m + 1))
        total = jnp.where(keep, turned, total)
    return jnp.sum(total.reshape(count // per, per, LANES), axis=1)


def scalar_sums(rows_ref, count):
    total = jnp.sum(rows_ref[:, 1, :], axis=0, keepdims=True)
    return [total[0:1, COARSE_LANE + i : COARSE_LANE + i + 1] for i in range(count)]


def coarse_weights(inverse_ref, sums):
    total = jnp.zeros((inverse_ref.shape[0], LANES), F32)
    for g in range(sums.shape[0]):
        total = total + inverse_ref[:, LANES * g : LANES * (g + 1)] * sums[g : g + 1, :]
    return jnp.sum(total, axis=1, keepdims=True)


def add_coarse(out, smooth, basis_ref, weights):
    vecs, nx, ny, nz = basis_ref.shape
    scale = [jnp.broadcast_to(weights[k : k + 1, 0:1], (8, LANES)) for k in range(vecs)]
    scale = [jnp.tile(s, (ny // 8, nz // LANES)) for s in scale]

    def body(x, carry):
        total = smooth[x + 3, 0:ny, 0:nz]
        for k in range(vecs):
            total = total + scale[k] * basis_ref[k, x]
        out[x] = total
        return carry

    lax.fori_loop(0, nx, body, 0)


def full_sum(value):
    return jnp.sum(value)


def call(kernel, outs, args, scratch=(), flops=0):
    whole = pl.BlockSpec(memory_space=pltpu.VMEM)
    size = sum(a.size * 4 for a in jax.tree.leaves(args)) + sum(
        o.size * 4 for o in jax.tree.leaves(outs)
    )
    return pl.pallas_call(
        kernel,
        out_shape=outs,
        in_specs=jax.tree.map(lambda _: whole, list(args)),
        out_specs=jax.tree.map(lambda _: whole, outs),
        scratch_shapes=list(scratch),
        compiler_params=pltpu.CompilerParams(vmem_limit_bytes=VMEM_LIMIT),
        cost_estimate=pl.CostEstimate(flops=flops, bytes_accessed=size, transcendentals=0),
    )(*args)


def shaped(*shape):
    return jax.ShapeDtypeStruct(shape, F32)


def face_shapes(shape, sizes, count, width):
    nx, ny, nz = shape
    outs = {
        "x": {r: shaped(count * width, ny, nz) for r in rounds_of(sizes[0])},
        "y": {r: shaped(count * width, nx, nz) for r in rounds_of(sizes[1])},
        "z": shaped(nx, ny, LANES),
    }
    if width == 2:
        outs["xy"] = {
            (rx, ry): shaped(max(8, 4 * count), nz)
            for rx in rounds_of(sizes[0])
            for ry in rounds_of(sizes[1])
        }
    return outs


def pack_faces(out, fields, sizes, width):
    ix, iy, _ = where_am_i()
    out["z"][...] = pack_z(fields)
    for r, ref in out["x"].items():
        pack_x(ref, fields, r, ix, width)
    for r, ref in out["y"].items():
        pack_y(ref, fields, r, iy, width)
    for (rx, ry), ref in out.get("xy", {}).items():
        pack_xy(ref, fields, rx, ry, ix, iy)


def send_faces(faces, sizes):
    got = {
        "x": {r: swap(v, sizes, {0: r}) for r, v in faces["x"].items()},
        "y": {r: swap(v, sizes, {1: r}) for r, v in faces["y"].items()},
        "z": {r: swap(faces["z"], sizes, {2: r}) for r in rounds_of(sizes[2])},
    }
    if "xy" in faces:
        got["xy"] = {(rx, ry): swap(v, sizes, {0: rx, 1: ry}) for (rx, ry), v in faces["xy"].items()}
    return got


def spread(rows):
    return lax.all_to_all(rows, AXES, 0, 0, tiled=True)


def shards(sizes, right_side, conductance, storage, dirichlet, basis, coarse_inverse):
    shape = right_side.shape
    nx, ny, nz = shape
    boxed = box_shape(shape)
    devices = sizes[0] * sizes[1] * sizes[2]
    row_shape = shaped(devices, 8, LANES)
    box = shaped(*boxed)
    vbox = pltpu.VMEM(boxed, F32)

    def pack_all(cond, store, fixed, rhs, out, free):
        free[...] = 1.0 - fixed[...].astype(F32)
        pack_faces(out, [cond.at[0], cond.at[1], cond.at[2], store, free, rhs], sizes, 2)

    faces = call(
        pack_all,
        face_shapes(shape, sizes, 6, 2),
        (conductance, storage, dirichlet, right_side),
        [pltpu.VMEM(shape, F32)],
    )

    def first_rows(ends, base, rhs, out):
        fill_rows(out, sizes, edge_tiles(ends, 6), project(base, rhs[...]))

    rows = call(first_rows, row_shape, (faces["z"], basis, right_side))
    got = send_faces(faces, sizes)
    rows_a = spread(rows)

    def first_solve(cond, store, fixed, rhs, base, inverse, got, rows, outs, scr, *work):
        (ga, gb, source), boxes = work[:3], list(work[3:]) + [outs["rhs"]]
        free = scr
        free[...] = 1.0 - fixed[...].astype(F32)
        owns = [cond.at[0], cond.at[1], cond.at[2], store, free, rhs]
        for b in boxes:
            clear(b)
        unpack_faces(boxes, owns, got["x"], got["y"], sizes, 2)
        unpack_xy(boxes, shape, got["xy"], sizes)
        unpack_z(boxes, shape, got["z"], sizes)
        unpack_edges(boxes, shape, rows, sizes)
        links = outs["links"]
        coefficients(boxes, links, outs["diag"], outs["step"])
        smooth = jacobi(outs["rhs"], outs["step"], links, ga, gb, source)
        weights = coarse_weights(inverse, coarse_sum(rows))
        add_coarse(outs["z"], smooth, base, weights)
        pack_faces(outs["faces"], [outs["z"]], sizes, 1)

    solved = call(
        first_solve,
        {
            "z": shaped(*shape),
            "links": [box, box, box],
            "diag": box,
            "step": box,
            "rhs": box,
            "faces": face_shapes(shape, sizes, 1, 1),
        },
        (conductance, storage, dirichlet, right_side, basis, coarse_inverse, got, rows_a),
        [pltpu.VMEM(shape, F32)] + [vbox] * 8,
    )
    links, diag, step = solved["links"], solved["diag"], solved["step"]
    direction = solved["z"]
    got = send_faces(solved["faces"], sizes)

    def apply(field, got, links, diag, out, vb):
        clear(vb)
        unpack_faces([vb], [field], got["x"], got["y"], sizes, 1)
        unpack_z([vb], shape, got["z"], sizes)

        def body(x, carry):
            whole = diag[x + 3] * vb[x + 3] - neighbours(vb, links, x + 3)
            out[x] = whole[0:ny, 0:nz]
            return carry

        lax.fori_loop(0, nx, body, 0)

    def first_image(field, got, links, diag, rhs, outs, vb):
        apply(field, got, links, diag, outs["image"], vb)
        pack_faces(outs["faces"], [outs["image"]], sizes, 2)
        tile = jnp.zeros((8, LANES), F32)
        values = [full_sum(rhs[...] * field[...]), full_sum(field[...] * outs["image"][...])]
        outs["sums"][...] = put_scalars(tile, values)

    imaged = call(
        first_image,
        {
            "image": shaped(*shape),
            "faces": face_shapes(shape, sizes, 1, 2),
            "sums": shaped(8, LANES),
        },
        (direction, got, links, diag, right_side),
        [vbox],
    )
    image = imaged["image"]

    def second_rows(ends, base, field, sums, out):
        fill_rows(out, sizes, edge_tiles(ends, 1), project(base, field[...]) + sums[...])

    rows = call(second_rows, row_shape, (imaged["faces"]["z"], basis, image, imaged["sums"]))
    got = send_faces(imaged["faces"], sizes)
    rows_c = spread(rows)

    def second_solve(
        field, rhs, rhs_box, base, inverse, links, step, got, rows_a, rows, outs, *work
    ):
        ga, gb, source, vb = work
        clear(vb)
        unpack_faces([vb], [field], got["x"], got["y"], sizes, 2)
        unpack_xy([vb], shape, got["xy"], sizes)
        unpack_z([vb], shape, got["z"], sizes)
        unpack_edges([vb], shape, rows, sizes)
        norm, curve = scalar_sums(rows, 2)
        alpha = norm / curve

        def body(x, carry):
            vb[x] = rhs_box[x] - alpha * vb[x]
            return carry

        lax.fori_loop(0, boxed[0], body, 0)
        outs["residual"][...] = vb[3 : 3 + nx, 0:ny, 0:nz]
        smooth = jacobi(vb, step, links, ga, gb, source)
        sums = coarse_sum(rows_a) - alpha * coarse_sum(rows)
        add_coarse(outs["z"], smooth, base, coarse_weights(inverse, sums))
        pack_faces(outs["faces"], [outs["z"]], sizes, 1)
        outs["scalars"][...] = jnp.concatenate(
            [jnp.broadcast_to(norm, (8, LANES)), jnp.broadcast_to(curve, (8, LANES))], axis=0
        )

    solved = call(
        second_solve,
        {
            "z": shaped(*shape),
            "residual": shaped(*shape),
            "scalars": shaped(16, LANES),
            "faces": face_shapes(shape, sizes, 1, 1),
        },
        (
            image,
            right_side,
            solved["rhs"],
            basis,
            coarse_inverse,
            links,
            step,
            got,
            rows_a,
            rows_c,
        ),
        [vbox] * 4,
    )
    precond, residual = solved["z"], solved["residual"]
    got = send_faces(solved["faces"], sizes)

    def second_image(field, got, links, diag, image, residual, outs, vb):
        apply(field, got, links, diag, outs["image"], vb)
        values = [
            full_sum(residual[...] * field[...]),
            full_sum(field[...] * outs["image"][...]),
            full_sum(field[...] * image[...]),
        ]
        tile = put_scalars(jnp.zeros((8, LANES), F32), values)
        outs["rows"][...] = jnp.broadcast_to(tile[None], outs["rows"].shape)

    last = call(
        second_image,
        {"image": shaped(*shape), "rows": row_shape},
        (precond, got, links, diag, image, residual),
        [vbox],
    )
    rows_e = spread(last["rows"])

    def finish(rows, scalars, direction, image, precond, precond_image, residual, out_field, out_rest):
        norm = scalars[0:1, 0:1]
        curve = scalars[8:9, 0:1]
        norm_next, curve_z, curve_mixed = scalar_sums(rows, 3)
        alpha = norm / curve
        beta = norm_next / norm
        curve_next = curve_z + 2.0 * beta * curve_mixed + beta * beta * curve
        alpha_next = norm_next / curve_next
        out_field[...] = alpha * direction[...] + alpha_next * (
            precond[...] + beta * direction[...]
        )
        out_rest[...] = residual[...] - alpha_next * (precond_image[...] + beta * image[...])

    return call(
        finish,
        (shaped(*shape), shaped(*shape)),
        (rows_e, solved["scalars"], direction, image, precond, last["image"], residual),
    )


def solution(mesh):
    sizes = tuple(mesh.shape[a] for a in AXES)
    placed = (
        P("gx", "gy", "gz"),
        P(None, "gx", "gy", "gz"),
        P("gx", "gy", "gz"),
        P("gx", "gy", "gz"),
        P(None, "gx", "gy", "gz"),
        P(("gx", "gy", "gz"), None),
    )
    return jax.shard_map(
        functools.partial(shards, sizes),
        mesh=mesh,
        in_specs=placed,
        out_specs=(P("gx", "gy", "gz"), P("gx", "gy", "gz")),
        check_vma=False,
    )
```

```python
import functools
import math

import jax
import jax.numpy as jnp
from jax import lax
from jax.experimental import pallas as pl
from jax.experimental.pallas import tpu as pltpu
from jax.sharding import PartitionSpec as P

SWEEPS = 4
RELAX = 2.0 / 3.0
AXES = ("gx", "gy", "gz")
LANES = 128
VMEM_LIMIT = 24 * 1024 * 1024
F32 = jnp.float32
UNROLL = 4
PARTS = 4
SMOOTH_FLOPS = 10**9


def rounds_of(count):
    return (0, 1)[: 1 if count <= 2 else 2]


def mate(index, odd, count):
    other = index + 1 if index % 2 == odd else index - 1
    return other if 0 <= other < count else None


def swap(value, sizes, along):
    pairs = []
    nx, ny, nz = sizes
    for ix in range(nx):
        for iy in range(ny):
            for iz in range(nz):
                here = [ix, iy, iz]
                there = [
                    mate(here[a], along[a], sizes[a]) if a in along else here[a] for a in range(3)
                ]
                if None in there:
                    if 2 in along:
                        spare = nz - 1 - iz if iz in (0, nz - 1) else None
                    else:
                        spare = iz ^ 1 if nz % 2 == 0 else None
                    if spare is None:
                        continue
                    there = [ix, iy, spare]
                pairs.append(
                    ((ix * ny + iy) * nz + iz, (there[0] * ny + there[1]) * nz + there[2])
                )
    return lax.ppermute(value, AXES, pairs)


def upward(index, odd):
    return lax.rem(index, 2) == odd


def where_am_i():
    return [lax.axis_index(a) for a in AXES]


def lane_iota(shape):
    return lax.broadcasted_iota(jnp.int32, shape, len(shape) - 1)


def pack_x(out, fields, odd, index, width, ends=None):
    nx, _, nz = fields[0].shape
    count = len(fields) * width
    high = upward(index, odd)
    for cond, first in ((high, nx - width), (jnp.logical_not(high), 0)):

        @pl.when(cond)
        def _(first=first):
            for k, field in enumerate(fields):
                out[k * width : (k + 1) * width] = field[first : first + width]
            if ends is not None:
                for i in range(width):
                    out[count, :, LANES * i : LANES * (i + 1)] = ends[first + i]


def pack_y(out, fields, odd, index, width, ends=None):
    _, ny, nz = fields[0].shape
    count = len(fields) * width
    high = upward(index, odd)
    for cond, first in ((high, ny - width), (jnp.logical_not(high), 0)):

        @pl.when(cond)
        def _(first=first):
            for j in range(width):
                for k, field in enumerate(fields):
                    out[k * width + j] = field[:, first + j, :]
                if ends is not None:
                    out[count, :, LANES * j : LANES * (j + 1)] = ends[:, first + j, :]


def pack_xy(out, fields, rx, ry, ix, iy, ends):
    nx, ny, _ = fields[0].shape
    count = len(fields)
    for xhigh in (False, True):
        for yhigh in (False, True):

            @pl.when((upward(ix, rx) == xhigh) & (upward(iy, ry) == yhigh))
            def _(x0=(nx - 2 if xhigh else 0), y0=(ny - 2 if yhigh else 0)):
                for i in range(2):
                    for k, field in enumerate(fields):
                        out[4 * k + 2 * i : 4 * k + 2 * i + 2, :] = field[x0 + i, y0 : y0 + 2, :]
                    out[4 * count + 2 * i : 4 * count + 2 * i + 2, 0:LANES] = ends[
                        x0 + i, y0 : y0 + 2, :
                    ]


def z_rows(count):
    return (4 * count + 7) // 8 * 8


def pack_z(fields):
    nx, ny, nz = fields[0].shape
    lane = lane_iota((nx, ny, LANES))
    total = jnp.zeros((nx, ny, LANES), F32)
    for k, field in enumerate(fields):
        ends = jnp.where(lane < 64, field[:, :, 0:LANES], field[:, :, nz - LANES : nz])
        turned = pltpu.roll(ends, 4 * k + 2, 2)
        total = jnp.where((lane >= 4 * k) & (lane < 4 * k + 4), turned, total)
    return total.reshape(nx * ny, LANES).T[0 : z_rows(len(fields))]


def project(basis, field):
    nx, ny, nz = field.shape
    rows = []
    for piece in basis:
        vectors = piece.get()
        for k in range(vectors.shape[0]):
            prod = jnp.sum(vectors[k] * field, axis=0)
            part = jnp.zeros((8, LANES), F32)
            for y in range(ny // 8):
                for z in range(nz // LANES):
                    part = part + prod[8 * y : 8 * y + 8, LANES * z : LANES * (z + 1)]
            rows.append(jnp.sum(part, axis=0, keepdims=True))
    vecs = len(rows)
    totals = jnp.sum(jnp.concatenate(rows, axis=0), axis=1, keepdims=True)
    row = lax.broadcasted_iota(jnp.int32, (vecs, LANES), 0)
    return jnp.sum(jnp.where(lane_iota((vecs, LANES)) == row, totals, 0.0), axis=0, keepdims=True)


def put_scalars(row, first, values):
    lane = lane_iota(row.shape)
    for i, value in enumerate(values):
        row = jnp.where(lane == first + i, value, row)
    return row


def box_shape(shape):
    nx, ny, nz = shape
    return (nx + 6, ny + 8, nz + LANES)


def clear(box):
    def body(x, carry):
        box[x] = jnp.zeros(box.shape[1:], F32)
        return carry

    loop(0, box.shape[0], body)


def each_round(sizes, a, index, act):
    for r in rounds_of(sizes[a]):
        high = upward(index, r)

        @pl.when(high & (index + 1 < sizes[a]))
        def _(r=r):
            act(r, True)

        @pl.when(jnp.logical_not(high) & (index > 0))
        def _(r=r):
            act(r, False)


def unpack_faces(boxes, owns, xs, ys, sizes, width, ends=None):
    nx, ny, nz = owns[0].shape
    count = len(boxes) * width
    ix, iy, _ = where_am_i()
    for k, (box, own) in enumerate(zip(boxes, owns)):
        box[3 : 3 + nx, 0:ny, 0:nz] = own[...]
        if ends is not None:
            box[3 : 3 + nx, 0:ny, nz : nz + LANES] = halo_lanes(ends, k)

    def put_x(r, above):
        first = 3 + nx if above else 3 - width
        for k, box in enumerate(boxes):
            box[first : first + width, 0:ny, 0:nz] = xs[r][k * width : (k + 1) * width]
            if ends is not None:
                for i in range(width):
                    tile = xs[r][count, :, LANES * i : LANES * (i + 1)]
                    box[first + i, 0:ny, nz : nz + LANES] = halo_lanes(tile, k)

    each_round(sizes, 0, ix, put_x)

    def put_y(r, above):
        first = ny if above else ny + 8 - width
        for k, box in enumerate(boxes):
            for j in range(width):
                box[3 : 3 + nx, first + j, 0:nz] = ys[r][k * width + j]
                if ends is not None:
                    tile = ys[r][count, :, LANES * j : LANES * (j + 1)]
                    box[3 : 3 + nx, first + j, nz : nz + LANES] = halo_lanes(tile, k)

    each_round(sizes, 1, iy, put_y)


def unpack_xy(boxes, shape, xys, sizes):
    nx, ny, nz = shape
    count = len(boxes)
    ix, iy, _ = where_am_i()

    def put(rx, xabove):
        x0 = 3 + nx if xabove else 1

        def inner(ry, yabove):
            y0 = ny if yabove else ny + 6
            rows = xys[(rx, ry)]
            tile = rows[4 * count : 4 * count + 4, 0:LANES]
            for k, box in enumerate(boxes):
                turned = halo_lanes(tile, k)
                for i in range(2):
                    box[x0 + i, y0 : y0 + 2, 0:nz] = rows[4 * k + 2 * i : 4 * k + 2 * i + 2, :]
                    box[x0 + i, y0 : y0 + 2, nz : nz + LANES] = turned[2 * i : 2 * i + 2]

        each_round(sizes, 1, iy, inner)

    each_round(sizes, 0, ix, put)


def pick_z(zs, sizes, shape):
    count = sizes[2]
    iz = lax.axis_index("gz")
    rows, cells = zs[0].shape
    first = lax.rem(lax.broadcasted_iota(jnp.int32, (rows, cells), 0), 4) < 2
    total = jnp.zeros((rows, cells), F32)
    for r in rounds_of(count):
        high = upward(iz, r)
        below = jnp.logical_not(high) & (iz > 0)
        above = high & (iz + 1 < count)
        total = jnp.where((first & below) | (jnp.logical_not(first) & above), zs[r][...], total)
    filled = jnp.concatenate([total, jnp.zeros((LANES - rows, cells), F32)], axis=0)
    return filled.T.reshape(shape)


def halo_lanes(tile, k):
    lane = lane_iota(tile.shape)
    axis = len(tile.shape) - 1
    turned = pltpu.roll(tile, (-(4 * k + 2)) % LANES, axis)
    return jnp.where((lane < 2) | (lane >= LANES - 2), turned, 0.0)


def ahead(plane, axis):
    return pltpu.roll(plane, plane.shape[axis] - 1, axis)


def behind(plane, axis):
    return pltpu.roll(plane, 1, axis)


def neighbours(g, links, x):
    lx, ly, lz = links
    mid = g[x]
    y = ly[x]
    z = lz[x]
    total = lx[x] * g[x + 1] + lx[x - 1] * g[x - 1]
    total = total + y * ahead(mid, 0) + behind(y * mid, 0)
    return total + z * ahead(mid, 1) + behind(z * mid, 1)


def coefficients(fields, links, diag, step):
    tx, ty, tz, store, free, _ = fields
    lx, ly, lz = links
    last = tx.shape[0] - 1
    for ref in (lx, ly, lz, diag, step):
        ref[0] = jnp.zeros(ref.shape[1:], F32)
        ref[last] = jnp.zeros(ref.shape[1:], F32)

    def body(x, carry):
        f = free[x]
        a, b, c = tx[x], ty[x], tz[x]
        total = store[x] + a + tx[x - 1] + b + behind(b, 0) + c + behind(c, 1)
        d = f * total + (1.0 - f)
        diag[x] = d
        step[x] = RELAX / d
        lx[x] = a * f * free[x + 1]
        ly[x] = b * f * ahead(f, 0)
        lz[x] = c * f * ahead(f, 1)
        return carry

    loop(1, last, body)


def jacobi(rhs, step, links, ga, gb, source, out):
    planes = rhs.shape[0]
    nx, ny, nz = out.shape
    for g in (ga, gb, source):
        g[0] = jnp.zeros(g.shape[1:], F32)
        g[planes - 1] = jnp.zeros(g.shape[1:], F32)

    def first(x, carry):
        source[x] = step[x] * rhs[x]
        return carry

    loop(1, planes - 1, first)

    def swept(now, x):
        return (1.0 - RELAX) * now[x] + source[x] + step[x] * neighbours(now, links, x)

    now, then, spare = source, ga, gb
    for sweep in range(1, SWEEPS - 1):
        edge = max(1, 3 - (SWEEPS - 1 - sweep))

        def body(x, carry, now=now, then=then):
            then[x] = swept(now, x)
            return carry

        loop(edge, planes - edge, body)
        now, then, spare = then, spare, then

    def final(x, carry):
        out[x] = swept(now, x + 3)[0:ny, 0:nz]
        return carry

    loop(0, nx, final)


def coarse_sum(rows_ref, vecs):
    count = rows_ref.shape[0]
    per = LANES // vecs
    lane = lane_iota((count, LANES))
    row = lax.broadcasted_iota(jnp.int32, (count, LANES), 0)
    all_rows = rows_ref[...]
    total = jnp.zeros((count, LANES), F32)
    for m in range(per):
        turned = pltpu.roll(all_rows, vecs * m, 1) if m else all_rows
        keep = (lax.rem(row, per) == m) & (lane >= vecs * m) & (lane < vecs * (m + 1))
        total = jnp.where(keep, turned, total)
    return jnp.sum(total.reshape(count // per, per, LANES), axis=1)


def scalar_sums(rows_ref, first, count):
    total = jnp.sum(rows_ref[...], axis=0, keepdims=True)
    return [total[0:1, first + i : first + i + 1] for i in range(count)]


def coarse_weights(inverse_ref, sums):
    total = jnp.zeros((inverse_ref.shape[0], LANES), F32)
    for g in range(sums.shape[0]):
        total = total + inverse_ref[:, LANES * g : LANES * (g + 1)] * sums[g : g + 1, :]
    return jnp.sum(total, axis=1, keepdims=True)


def add_coarse(out, smooth, basis_ref, weights):
    vecs, nx, ny, nz = basis_ref.shape
    scale = [jnp.broadcast_to(weights[k : k + 1, 0:1], (8, LANES)) for k in range(vecs)]
    scale = [jnp.tile(s, (ny // 8, nz // LANES)) for s in scale]

    def body(x, carry):
        total = smooth[x]
        for k in range(vecs):
            total = total + scale[k] * basis_ref[k, x]
        out[x] = total
        return carry

    loop(0, nx, body)


def full_sum(value):
    return jnp.sum(value)


class Arriving:
    def __init__(self, buffer, copy=None):
        self.copy = copy
        self.buffer = buffer

    def get(self):
        if self.copy is not None:
            self.copy.wait()
            self.copy = None
        return self.buffer


class Far:
    def __init__(self, value, parts=False):
        self.value, self.parts = value, parts


class Stored:
    def __init__(self, *shape):
        self.shape = shape


class Leaving:
    def __init__(self, target, sem):
        self.target, self.sem, self.copy = target, sem, None

    def put(self, source):
        self.copy = pltpu.make_async_copy(source, self.target, self.sem)
        self.copy.start()


def call(kernel, outs, args, scratch=(), flops=0):
    leaves, tree = jax.tree.flatten(list(args), is_leaf=lambda one: isinstance(one, Far))
    out_leaves, out_tree = jax.tree.flatten(outs, is_leaf=lambda one: isinstance(one, Stored))
    count, n_out = len(leaves), len(out_leaves)
    far = [i for i, a in enumerate(leaves) if isinstance(a, Far)]
    stored = [i for i, a in enumerate(out_leaves) if isinstance(a, Stored)]
    parts = [i for i in far if leaves[i].parts]
    leaves = [
        pltpu.with_memory_space_constraint(a.value, pltpu.HBM) if isinstance(a, Far) else a
        for a in leaves
    ]

    def body(*refs):
        sources, results = refs[:count], list(refs[count : count + n_out])
        rest = refs[count + n_out :]
        sems, rest = rest[0], rest[1:]
        coming = [Arriving(a) for a in sources]
        used = 0
        for n, i in enumerate(far):
            pieces = [(sources[i], rest[n])]
            if i in parts:
                pieces = [(sources[i].at[p], rest[n].at[p]) for p in chunks(leaves[i].shape[0])]
            arrivals = []
            for source, target in pieces:
                copy = pltpu.make_async_copy(source, target, sems.at[used])
                copy.start()
                arrivals.append(Arriving(target, copy))
                used += 1
            coming[i] = arrivals if i in parts else arrivals[0]
        for n, i in enumerate(stored):
            results[i] = Leaving(results[i], sems.at[used])
            used += 1
        kernel(
            *jax.tree.unflatten(tree, coming),
            jax.tree.unflatten(out_tree, results),
            *rest[len(far) :],
        )
        fetch(coming)
        for i in stored:
            results[i].copy.wait()

    n_sems = len(far) - len(parts) + len(stored) + len(parts) * PARTS
    size = sum(4 * math.prod(a.shape) for a in leaves + out_leaves)
    given = pl.pallas_call(
        body,
        out_shape=[pltpu.HBM(a.shape, F32) if isinstance(a, Stored) else a for a in out_leaves],
        in_specs=[
            pl.BlockSpec(
                memory_space=pltpu.HBM if i in far else pltpu.VMEM
            )
            for i in range(count)
        ],
        out_specs=[
            pl.BlockSpec(memory_space=pltpu.HBM if i in stored else pltpu.VMEM)
            for i in range(n_out)
        ],
        scratch_shapes=[pltpu.SemaphoreType.DMA((max(1, n_sems),))]
        + [pltpu.VMEM(leaves[i].shape, leaves[i].dtype) for i in far]
        + list(scratch),
        compiler_params=pltpu.CompilerParams(vmem_limit_bytes=VMEM_LIMIT),
        cost_estimate=pl.CostEstimate(flops=flops, bytes_accessed=size, transcendentals=0),
    )(*leaves)
    return jax.tree.unflatten(out_tree, given)


def chunks(count):
    each = count // PARTS
    return [pl.ds(p * each, each) for p in range(PARTS)]


def far(tree):
    return jax.tree.map(Far, tree)


def fetch(tree):
    return jax.tree.map(lambda one: one.get(), tree, is_leaf=lambda one: isinstance(one, Arriving))


def loop(first, last, body):
    lax.fori_loop(first, last, body, 0, unroll=UNROLL)


def shaped(*shape):
    return jax.ShapeDtypeStruct(shape, F32)


def face_shapes(shape, sizes, count, width):
    nx, ny, nz = shape
    blocks = count * width + (1 if width == 2 else 0)
    outs = {
        "x": {r: shaped(blocks, ny, nz) for r in rounds_of(sizes[0])},
        "y": {r: shaped(blocks, nx, nz) for r in rounds_of(sizes[1])},
    }
    if width == 2:
        outs["xy"] = {
            (rx, ry): shaped(4 * count + 4, nz)
            for rx in rounds_of(sizes[0])
            for ry in rounds_of(sizes[1])
        }
    return outs


def pack_faces(out, fields, sizes, width, ends=None):
    ix, iy, _ = where_am_i()
    for r, ref in out["x"].items():
        pack_x(ref, fields, r, ix, width, ends)
    for r, ref in out["y"].items():
        pack_y(ref, fields, r, iy, width, ends)
    for (rx, ry), ref in out.get("xy", {}).items():
        pack_xy(ref, fields, rx, ry, ix, iy, ends)


def send_z(tile, sizes):
    return {r: swap(tile, sizes, {2: r}) for r in rounds_of(sizes[2])}


def send_faces(faces, sizes):
    got = {
        "x": {r: swap(v, sizes, {0: r}) for r, v in faces["x"].items()},
        "y": {r: swap(v, sizes, {1: r}) for r, v in faces["y"].items()},
    }
    if "xy" in faces:
        got["xy"] = {(rx, ry): swap(v, sizes, {0: rx, 1: ry}) for (rx, ry), v in faces["xy"].items()}
    return got


def spread(rows):
    return lax.all_to_all(rows, AXES, 0, 0, tiled=True)


def shards(sizes, right_side, conductance, storage, dirichlet, basis, coarse_inverse):
    shape = right_side.shape
    nx, ny, nz = shape
    vecs = basis.shape[0]
    boxed = box_shape(shape)
    devices = sizes[0] * sizes[1] * sizes[2]
    row_shape = shaped(devices, LANES)
    sum_shape = (devices * vecs // LANES, LANES)
    ends_shape = (nx, ny, LANES)
    box = shaped(*boxed)
    vbox = pltpu.VMEM(boxed, F32)
    inputs = (Far(conductance), Far(storage), Far(dirichlet), Far(right_side))

    def six(cond, store, fixed, rhs, free):
        cond, store, fixed, rhs = fetch((cond, store, fixed, rhs))
        free[...] = 1.0 - fixed[...].astype(F32)
        return [cond.at[0], cond.at[1], cond.at[2], store, free, rhs]

    def pack_first(cond, store, fixed, rhs, out, free):
        out[...] = pack_z(six(cond, store, fixed, rhs, free))

    tile = call(pack_first, shaped(z_rows(6), nx * ny), inputs, [pltpu.VMEM(shape, F32)])
    got_z = send_z(tile, sizes)

    def first_rows(rhs, base, out):
        row = project(base, rhs.get()[...])
        out[...] = jnp.broadcast_to(row, out.shape)

    rows = call(first_rows, row_shape, (Far(right_side), Far(basis, True)))
    rows_a = spread(rows)

    def pack_all(got_z, cond, store, fixed, rhs, rows, outs, free, ends):
        fields = six(cond, store, fixed, rhs, free)
        ends[...] = pick_z(fetch(got_z), sizes, ends_shape)
        outs["ends"].put(ends)
        pack_faces(outs["faces"], fields, sizes, 2, ends)

    packed = call(
        pack_all,
        {"ends": Stored(*ends_shape), "faces": face_shapes(shape, sizes, 6, 2)},
        (got_z,) + inputs + (rows,),
        [pltpu.VMEM(shape, F32), pltpu.VMEM(ends_shape, F32)],
    )
    got = send_faces(packed["faces"], sizes)

    def first_smooth(got, cond, store, fixed, rhs, ends, outs, free, *work):
        ga, gb, source, step = work[:4]
        boxes = list(work[4:])
        for b in boxes:
            clear(b)
        owns = six(cond, store, fixed, rhs, free)
        got = fetch(got)
        unpack_faces(boxes, owns, got["x"], got["y"], sizes, 2, ends.get()[...])
        unpack_xy(boxes, shape, got["xy"], sizes)
        links = outs["links"]
        coefficients(boxes, links, outs["diag"], step)
        for name, value in (("diag", outs["diag"]), ("step", step)):
            outs["kept"][name].put(value)
        for kept, link in zip(outs["kept"]["links"], links):
            kept.put(link)
        jacobi(boxes[-1], step, links, ga, gb, source, outs["smooth"])

    smoothed = call(
        first_smooth,
        {
            "smooth": shaped(*shape),
            "links": [box, box, box],
            "diag": box,
            "kept": {
                "links": [Stored(*boxed), Stored(*boxed), Stored(*boxed)],
                "diag": Stored(*boxed),
                "step": Stored(*boxed),
            },
        },
        (far(got),) + inputs + (Far(packed["ends"]),),
        [pltpu.VMEM(shape, F32)] + [vbox] * 10,
        flops=SMOOTH_FLOPS,
    )
    kept = smoothed["kept"]
    links, diag = smoothed["links"], smoothed["diag"]

    def first_direction(smooth, rows, inverse, base, outs):
        smooth, rows = fetch((smooth, rows))
        weights = coarse_weights(inverse.get(), coarse_sum(rows, vecs))
        add_coarse(outs["z"], smooth, base.get(), weights)
        outs["kept"].put(outs["z"])
        pack_faces(outs["faces"], [outs["z"]], sizes, 1)
        outs["tile"][...] = pack_z([outs["z"]])

    directed = call(
        first_direction,
        {
            "z": shaped(*shape),
            "kept": Stored(*shape),
            "faces": face_shapes(shape, sizes, 1, 1),
            "tile": shaped(z_rows(1), nx * ny),
        },
        (smoothed["smooth"], rows_a, Far(coarse_inverse), Far(basis)),
    )
    direction, kept_z = directed["z"], directed["kept"]
    got = send_faces(directed["faces"], sizes)
    got_z = send_z(directed["tile"], sizes)

    def apply(field, got, got_z, links, diag, out, vb):
        clear(vb)
        field, got, got_z = fetch((field, got, got_z))
        unpack_faces([vb], [field], got["x"], got["y"], sizes, 1)
        vb[3 : 3 + nx, 0:ny, nz : nz + LANES] = halo_lanes(pick_z(got_z, sizes, ends_shape), 0)
        links, diag = fetch((links, diag))

        def body(x, carry):
            whole = diag[x + 3] * vb[x + 3] - neighbours(vb, links, x + 3)
            out[x] = whole[0:ny, 0:nz]
            return carry

        loop(0, nx, body)

    def first_image(got, got_z, field, links, diag, rhs, outs, vb):
        image = outs["image"]
        apply(field, got, got_z, links, diag, image, vb)
        outs["kept"].put(image)
        outs["tile"][...] = pack_z([image])
        field, rhs = fetch((field, rhs))
        values = [full_sum(rhs[...] * field[...]), full_sum(field[...] * image[...])]
        outs["sums"][...] = put_scalars(jnp.zeros((1, LANES), F32), vecs, values)

    imaged = call(
        first_image,
        {
            "image": shaped(*shape),
            "kept": Stored(*shape),
            "tile": shaped(z_rows(1), nx * ny),
            "sums": shaped(1, LANES),
        },
        (far(got), got_z, direction, links, diag, Far(right_side)),
        [vbox],
    )
    got_z = send_z(imaged["tile"], sizes)

    def second_rows(base, field, sums, out):
        row = project(base, field.get()[...]) + sums.get()[...]
        out[...] = jnp.broadcast_to(row, out.shape)

    rows = call(second_rows, row_shape, (Far(basis, True), imaged["image"], imaged["sums"]))
    rows_c = spread(rows)

    def pack_image(got_z, field, rows, outs, ends):
        ends[...] = pick_z(fetch(got_z), sizes, ends_shape)
        outs["ends"].put(ends)
        pack_faces(outs["faces"], [field.get()], sizes, 2, ends)

    packed = call(
        pack_image,
        {"ends": Stored(*ends_shape), "faces": face_shapes(shape, sizes, 1, 2)},
        (got_z, imaged["image"], rows),
        [pltpu.VMEM(ends_shape, F32)],
    )
    got = send_faces(packed["faces"], sizes)

    def second_smooth(got, field, step, links, ends, out, *work):
        ga, gb, source, vb = work
        clear(vb)
        field, got, ends = fetch((field, got, ends))
        unpack_faces([vb], [field], got["x"], got["y"], sizes, 2, ends[...])
        unpack_xy([vb], shape, got["xy"], sizes)
        step, links = fetch((step, links))
        jacobi(vb, step, links, ga, gb, source, out)

    smooth = call(
        second_smooth,
        shaped(*shape),
        (far(got), Far(imaged["kept"]), Far(kept["step"]), far(kept["links"]), Far(packed["ends"])),
        [vbox] * 4,
        flops=SMOOTH_FLOPS,
    )

    def second_direction(smooth, rows, inverse, field, rhs, before, base, outs):
        smooth, rows = fetch((smooth, rows))
        norm, curve = scalar_sums(rows, vecs, 2)
        alpha = norm / curve
        weights = coarse_weights(inverse.get(), coarse_sum(rows, vecs))
        field, rhs, before = fetch((field, rhs, before))
        outs["residual"][...] = rhs[...] - alpha * field[...]
        add_coarse(outs["z"], smooth, base.get(), weights)
        outs["z"][...] = before[...] - alpha * outs["z"][...]
        pack_faces(outs["faces"], [outs["z"]], sizes, 1)
        outs["tile"][...] = pack_z([outs["z"]])
        outs["scalars"][...] = jnp.concatenate(
            [jnp.broadcast_to(norm, (8, LANES)), jnp.broadcast_to(curve, (8, LANES))], axis=0
        )

    directed = call(
        second_direction,
        {
            "z": shaped(*shape),
            "residual": shaped(*shape),
            "scalars": shaped(16, LANES),
            "faces": face_shapes(shape, sizes, 1, 1),
            "tile": shaped(z_rows(1), nx * ny),
        },
        (
            smooth,
            rows_c,
            Far(coarse_inverse),
            Far(imaged["kept"]),
            Far(right_side),
            Far(kept_z),
            Far(basis),
        ),
    )
    precond, residual = directed["z"], directed["residual"]
    got = send_faces(directed["faces"], sizes)
    got_z = send_z(directed["tile"], sizes)
    image, direction = Far(imaged["kept"]), Far(kept_z)

    def second_image(got, got_z, field, links, diag, image, residual, outs, vb):
        apply(field, got, got_z, links, diag, outs["image"], vb)
        field, image, residual = fetch((field, image, residual))
        values = [
            full_sum(residual[...] * field[...]),
            full_sum(field[...] * outs["image"][...]),
            full_sum(field[...] * image[...]),
        ]
        row = put_scalars(jnp.zeros((1, LANES), F32), 0, values)
        outs["rows"][...] = jnp.broadcast_to(row, outs["rows"].shape)

    last = call(
        second_image,
        {"image": shaped(*shape), "rows": row_shape},
        (
            far(got),
            got_z,
            precond,
            far(kept["links"]),
            Far(kept["diag"]),
            image,
            residual,
        ),
        [vbox],
    )
    rows_e = spread(last["rows"])

    def finish(rows, scalars, direction, image, precond, precond_image, residual, outs):
        rows, scalars = fetch((rows, scalars))
        norm = scalars[0:1, 0:1]
        curve = scalars[8:9, 0:1]
        norm_next, curve_z, curve_mixed = scalar_sums(rows, 0, 3)
        alpha = norm / curve
        beta = norm_next / norm
        curve_next = curve_z + 2.0 * beta * curve_mixed + beta * beta * curve
        alpha_next = norm_next / curve_next
        direction, image, precond = fetch((direction, image, precond))
        precond_image, residual = fetch((precond_image, residual))
        outs[0][...] = alpha * direction[...] + alpha_next * (
            precond[...] + beta * direction[...]
        )
        outs[1][...] = residual[...] - alpha_next * (precond_image[...] + beta * image[...])

    return tuple(
        call(
            finish,
            [shaped(*shape), shaped(*shape)],
            (rows_e, directed["scalars"], direction, image, precond, last["image"], residual),
        )
    )


def solution(mesh):
    sizes = tuple(mesh.shape[a] for a in AXES)
    placed = (
        P("gx", "gy", "gz"),
        P(None, "gx", "gy", "gz"),
        P("gx", "gy", "gz"),
        P("gx", "gy", "gz"),
        P(None, "gx", "gy", "gz"),
        P(("gx", "gy", "gz"), None),
    )
    return jax.shard_map(
        functools.partial(shards, sizes),
        mesh=mesh,
        in_specs=placed,
        out_specs=(P("gx", "gy", "gz"), P("gx", "gy", "gz")),
        check_vma=False,
    )
```

```python
import functools
import math

import jax
import jax.numpy as jnp
from jax import lax
from jax.experimental import pallas as pl
from jax.experimental.pallas import tpu as pltpu
from jax.sharding import PartitionSpec as P

SWEEPS = 4
RELAX = 2.0 / 3.0
AXES = ("gx", "gy", "gz")
LANES = 128
VMEM_LIMIT = 24 * 1024 * 1024
F32 = jnp.float32
UNROLL = 4
PARTS = 4
SMOOTH_FLOPS = 10**9


def rounds_of(count):
    return (0, 1)[: 1 if count <= 2 else 2]


def mate(index, odd, count):
    other = index + 1 if index % 2 == odd else index - 1
    return other if 0 <= other < count else None


def swap(value, sizes, along):
    pairs = []
    nx, ny, nz = sizes
    for ix in range(nx):
        for iy in range(ny):
            for iz in range(nz):
                here = [ix, iy, iz]
                there = [
                    mate(here[a], along[a], sizes[a]) if a in along else here[a] for a in range(3)
                ]
                if None in there:
                    if 2 in along:
                        spare = nz - 1 - iz if iz in (0, nz - 1) else None
                    else:
                        spare = iz ^ 1 if nz % 2 == 0 else None
                    if spare is None:
                        continue
                    there = [ix, iy, spare]
                pairs.append(
                    ((ix * ny + iy) * nz + iz, (there[0] * ny + there[1]) * nz + there[2])
                )
    return lax.ppermute(value, AXES, pairs)


def upward(index, odd):
    return lax.rem(index, 2) == odd


def where_am_i():
    return [lax.axis_index(a) for a in AXES]


def lane_iota(shape):
    return lax.broadcasted_iota(jnp.int32, shape, len(shape) - 1)


def pack_x(out, fields, odd, index, width, ends=None):
    nx, _, nz = fields[0].shape
    count = len(fields) * width
    high = upward(index, odd)
    for cond, first in ((high, nx - width), (jnp.logical_not(high), 0)):

        @pl.when(cond)
        def _(first=first):
            for k, field in enumerate(fields):
                out[k * width : (k + 1) * width] = field[first : first + width]
            if ends is not None:
                for i in range(width):
                    out[count, :, LANES * i : LANES * (i + 1)] = ends[first + i]


def pack_y(out, fields, odd, index, width, ends=None):
    _, ny, nz = fields[0].shape
    count = len(fields) * width
    high = upward(index, odd)
    for cond, first in ((high, ny - width), (jnp.logical_not(high), 0)):

        @pl.when(cond)
        def _(first=first):
            for j in range(width):
                for k, field in enumerate(fields):
                    out[k * width + j] = field[:, first + j, :]
                if ends is not None:
                    out[count, :, LANES * j : LANES * (j + 1)] = ends[:, first + j, :]


def pack_xy(out, fields, rx, ry, ix, iy, ends):
    nx, ny, _ = fields[0].shape
    count = len(fields)
    for xhigh in (False, True):
        for yhigh in (False, True):

            @pl.when((upward(ix, rx) == xhigh) & (upward(iy, ry) == yhigh))
            def _(x0=(nx - 2 if xhigh else 0), y0=(ny - 2 if yhigh else 0)):
                for i in range(2):
                    for k, field in enumerate(fields):
                        out[4 * k + 2 * i : 4 * k + 2 * i + 2, :] = field[x0 + i, y0 : y0 + 2, :]
                    out[4 * count + 2 * i : 4 * count + 2 * i + 2, 0:LANES] = ends[
                        x0 + i, y0 : y0 + 2, :
                    ]


def z_rows(count):
    return (4 * count + 7) // 8 * 8


def pack_z(fields):
    nx, ny, nz = fields[0].shape
    lane = lane_iota((nx, ny, LANES))
    total = jnp.zeros((nx, ny, LANES), F32)
    for k, field in enumerate(fields):
        ends = jnp.where(lane < 64, field[:, :, 0:LANES], field[:, :, nz - LANES : nz])
        turned = pltpu.roll(ends, 4 * k + 2, 2)
        total = jnp.where((lane >= 4 * k) & (lane < 4 * k + 4), turned, total)
    return total.reshape(nx * ny, LANES).T[0 : z_rows(len(fields))]


def project(basis, field):
    nx, ny, nz = field.shape
    rows = []
    for piece in basis:
        vectors = piece.get()
        for k in range(vectors.shape[0]):
            prod = jnp.sum(vectors[k] * field, axis=0)
            part = jnp.zeros((8, LANES), F32)
            for y in range(ny // 8):
                for z in range(nz // LANES):
                    part = part + prod[8 * y : 8 * y + 8, LANES * z : LANES * (z + 1)]
            rows.append(jnp.sum(part, axis=0, keepdims=True))
    vecs = len(rows)
    totals = jnp.sum(jnp.concatenate(rows, axis=0), axis=1, keepdims=True)
    row = lax.broadcasted_iota(jnp.int32, (vecs, LANES), 0)
    return jnp.sum(jnp.where(lane_iota((vecs, LANES)) == row, totals, 0.0), axis=0, keepdims=True)


def put_scalars(row, first, values):
    lane = lane_iota(row.shape)
    for i, value in enumerate(values):
        row = jnp.where(lane == first + i, value, row)
    return row


def box_shape(shape):
    nx, ny, nz = shape
    return (nx + 6, ny + 8, nz + LANES)


def clear(box):
    def body(x, carry):
        box[x] = jnp.zeros(box.shape[1:], F32)
        return carry

    loop(0, box.shape[0], body)


def clear_round(box, shape):
    nx, ny, nz = shape
    planes, rows, lanes = box.shape
    for x in (0, 1, 2, planes - 3, planes - 2, planes - 1):
        box[x] = jnp.zeros((rows, lanes), F32)

    def body(x, carry):
        box[x, ny:rows, :] = jnp.zeros((rows - ny, lanes), F32)
        box[x, 0:ny, nz:lanes] = jnp.zeros((ny, lanes - nz), F32)
        return carry

    loop(3, 3 + nx, body)


def own_cells(box, shape):
    nx, ny, nz = shape
    return box.at[3 : 3 + nx, 0:ny, 0:nz]


def each_round(sizes, a, index, act):
    for r in rounds_of(sizes[a]):
        high = upward(index, r)

        @pl.when(high & (index + 1 < sizes[a]))
        def _(r=r):
            act(r, True)

        @pl.when(jnp.logical_not(high) & (index > 0))
        def _(r=r):
            act(r, False)


def unpack_faces(boxes, owns, xs, ys, sizes, width, ends=None):
    nx, ny, nz = boxes[0].shape[0] - 6, boxes[0].shape[1] - 8, boxes[0].shape[2] - LANES
    count = len(boxes) * width
    ix, iy, _ = where_am_i()
    for k, (box, own) in enumerate(zip(boxes, owns)):
        if own is not None:
            box[3 : 3 + nx, 0:ny, 0:nz] = own[...]
        if ends is not None:
            box[3 : 3 + nx, 0:ny, nz : nz + LANES] = halo_lanes(ends, k)

    def put_x(r, above):
        first = 3 + nx if above else 3 - width
        for k, box in enumerate(boxes):
            box[first : first + width, 0:ny, 0:nz] = xs[r][k * width : (k + 1) * width]
            if ends is not None:
                for i in range(width):
                    tile = xs[r][count, :, LANES * i : LANES * (i + 1)]
                    box[first + i, 0:ny, nz : nz + LANES] = halo_lanes(tile, k)

    each_round(sizes, 0, ix, put_x)

    def put_y(r, above):
        first = ny if above else ny + 8 - width
        for k, box in enumerate(boxes):
            for j in range(width):
                box[3 : 3 + nx, first + j, 0:nz] = ys[r][k * width + j]
                if ends is not None:
                    tile = ys[r][count, :, LANES * j : LANES * (j + 1)]
                    box[3 : 3 + nx, first + j, nz : nz + LANES] = halo_lanes(tile, k)

    each_round(sizes, 1, iy, put_y)


def unpack_xy(boxes, shape, xys, sizes):
    nx, ny, nz = shape
    count = len(boxes)
    ix, iy, _ = where_am_i()

    def put(rx, xabove):
        x0 = 3 + nx if xabove else 1

        def inner(ry, yabove):
            y0 = ny if yabove else ny + 6
            rows = xys[(rx, ry)]
            tile = rows[4 * count : 4 * count + 4, 0:LANES]
            for k, box in enumerate(boxes):
                turned = halo_lanes(tile, k)
                for i in range(2):
                    box[x0 + i, y0 : y0 + 2, 0:nz] = rows[4 * k + 2 * i : 4 * k + 2 * i + 2, :]
                    box[x0 + i, y0 : y0 + 2, nz : nz + LANES] = turned[2 * i : 2 * i + 2]

        each_round(sizes, 1, iy, inner)

    each_round(sizes, 0, ix, put)


def pick_z(zs, sizes, shape):
    count = sizes[2]
    iz = lax.axis_index("gz")
    rows, cells = zs[0].shape
    first = lax.rem(lax.broadcasted_iota(jnp.int32, (rows, cells), 0), 4) < 2
    total = jnp.zeros((rows, cells), F32)
    for r in rounds_of(count):
        high = upward(iz, r)
        below = jnp.logical_not(high) & (iz > 0)
        above = high & (iz + 1 < count)
        total = jnp.where((first & below) | (jnp.logical_not(first) & above), zs[r][...], total)
    filled = jnp.concatenate([total, jnp.zeros((LANES - rows, cells), F32)], axis=0)
    return filled.T.reshape(shape)


def halo_lanes(tile, k):
    lane = lane_iota(tile.shape)
    axis = len(tile.shape) - 1
    turned = pltpu.roll(tile, (-(4 * k + 2)) % LANES, axis)
    return jnp.where((lane < 2) | (lane >= LANES - 2), turned, 0.0)


def ahead(plane, axis):
    return pltpu.roll(plane, plane.shape[axis] - 1, axis)


def behind(plane, axis):
    return pltpu.roll(plane, 1, axis)


def neighbours(g, links, x):
    lx, ly, lz = links
    mid = g[x]
    y = ly[x]
    z = lz[x]
    total = lx[x] * g[x + 1] + lx[x - 1] * g[x - 1]
    total = total + y * ahead(mid, 0) + behind(y * mid, 0)
    return total + z * ahead(mid, 1) + behind(z * mid, 1)


def coefficients(fields, links, step, own):
    tx, ty, tz, store, free, _ = fields
    lx, ly, lz = links
    _, nx, ny, nz = own.shape
    last = tx.shape[0] - 1
    for ref in (lx, ly, lz, step):
        ref[0] = jnp.zeros(ref.shape[1:], F32)
        ref[last] = jnp.zeros(ref.shape[1:], F32)

    def body(x, carry, inside):
        f = free[x]
        a, b, c = tx[x], ty[x], tz[x]
        total = store[x] + a + tx[x - 1] + b + behind(b, 0) + c + behind(c, 1)
        d = f * total + (1.0 - f)
        step[x] = RELAX / d
        links_here = (a * f * free[x + 1], b * f * ahead(f, 0), c * f * ahead(f, 1))
        for ref, value in zip(links, links_here):
            ref[x] = value
        if inside:
            x_link, y_link, z_link = links_here
            mine = (
                d,
                x_link,
                lx[x - 1],
                y_link,
                behind(y_link, 0),
                z_link,
                behind(z_link, 1),
            )
            for n, value in enumerate(mine):
                own[n, x - 3] = value[0:ny, 0:nz]
        return carry

    loop(1, 3, functools.partial(body, inside=False))
    loop(3, 3 + nx, functools.partial(body, inside=True))
    loop(3 + nx, last, functools.partial(body, inside=False))


def jacobi(rhs, step, links, ga, gb, source, out):
    planes = rhs.shape[0]
    nx, ny, nz = out.shape
    for g in (ga, gb):
        g[0] = jnp.zeros(g.shape[1:], F32)
        g[planes - 1] = jnp.zeros(g.shape[1:], F32)

    def first(x, carry):
        source[x] = step[x] * rhs[x]
        return carry

    loop(1, planes - 1, first)

    def swept(now, x):
        return (1.0 - RELAX) * now[x] + source[x] + step[x] * neighbours(now, links, x)

    now, then, spare = source, ga, gb
    for sweep in range(1, SWEEPS - 1):
        edge = max(1, 3 - (SWEEPS - 1 - sweep))

        def body(x, carry, now=now, then=then):
            then[x] = swept(now, x)
            return carry

        loop(edge, planes - edge, body)
        now, then, spare = then, spare, then

    def final(x, carry):
        out[x] = swept(now, x + 3)[0:ny, 0:nz]
        return carry

    loop(0, nx, final)


def coarse_sum(rows_ref, vecs):
    count = rows_ref.shape[0]
    per = LANES // vecs
    lane = lane_iota((count, LANES))
    row = lax.broadcasted_iota(jnp.int32, (count, LANES), 0)
    all_rows = rows_ref[...]
    total = jnp.zeros((count, LANES), F32)
    for m in range(per):
        turned = pltpu.roll(all_rows, vecs * m, 1) if m else all_rows
        keep = (lax.rem(row, per) == m) & (lane >= vecs * m) & (lane < vecs * (m + 1))
        total = jnp.where(keep, turned, total)
    return jnp.sum(total.reshape(count // per, per, LANES), axis=1)


def scalar_sums(rows_ref, first, count):
    total = jnp.sum(rows_ref[...], axis=0, keepdims=True)
    return [total[0:1, first + i : first + i + 1] for i in range(count)]


def coarse_weights(inverse_ref, sums):
    total = jnp.zeros((inverse_ref.shape[0], LANES), F32)
    for g in range(sums.shape[0]):
        total = total + inverse_ref[:, LANES * g : LANES * (g + 1)] * sums[g : g + 1, :]
    return jnp.sum(total, axis=1, keepdims=True)


def add_coarse(out, smooth, basis, weights):
    nx, ny, nz = out.shape
    k = 0
    for piece in basis:
        vectors = piece.get()
        count = vectors.shape[0]
        scale = [jnp.broadcast_to(weights[k + i : k + i + 1, 0:1], (8, LANES)) for i in range(count)]
        scale = [jnp.tile(s, (ny // 8, nz // LANES)) for s in scale]
        source = smooth if k == 0 else out

        def body(x, carry, vectors=vectors, scale=scale, source=source):
            total = source[x]
            for i, s in enumerate(scale):
                total = total + s * vectors[i, x]
            out[x] = total
            return carry

        loop(0, nx, body)
        k += count


def full_sum(value):
    return jnp.sum(value)


class Arriving:
    def __init__(self, buffer, copy=None):
        self.copy = copy
        self.buffer = buffer

    def get(self):
        if self.copy is not None:
            self.copy.wait()
            self.copy = None
        return self.buffer


class Far:
    def __init__(self, value, parts=False):
        self.value, self.parts = value, parts


class Raw(Far):
    pass


class Stored:
    def __init__(self, *shape, near=False):
        self.shape, self.near = shape, near


class Leaving:
    def __init__(self, target, sem):
        self.target, self.sem, self.copy = target, sem, None

    def put(self, source):
        self.copy = pltpu.make_async_copy(source, self.target, self.sem)
        self.copy.start()

    def done(self):
        if self.copy is not None:
            self.copy.wait()
            self.copy = None
        return self.target


def call(kernel, outs, args, scratch=(), flops=0):
    leaves, tree = jax.tree.flatten(list(args), is_leaf=lambda one: isinstance(one, Far))
    out_leaves, out_tree = jax.tree.flatten(outs, is_leaf=lambda one: isinstance(one, Stored))
    count, n_out = len(leaves), len(out_leaves)
    raw = [i for i, a in enumerate(leaves) if isinstance(a, Raw)]
    far = [i for i, a in enumerate(leaves) if isinstance(a, Far) and i not in raw]
    distant = [i for i, a in enumerate(out_leaves) if isinstance(a, Stored) and not a.near]
    stored = [i for i, a in enumerate(out_leaves) if isinstance(a, Stored)]
    parts = [i for i in far if leaves[i].parts]
    leaves = [
        pltpu.with_memory_space_constraint(a.value, pltpu.HBM) if isinstance(a, Far) else a
        for a in leaves
    ]

    def body(*refs):
        sources, results = refs[:count], list(refs[count : count + n_out])
        rest = refs[count + n_out :]
        sems, rest = rest[0], rest[1:]
        coming = [Arriving(a) for a in sources]
        used = 0
        for n, i in enumerate(far):
            pieces = [(sources[i], rest[n])]
            if i in parts:
                pieces = [(sources[i].at[p], rest[n].at[p]) for p in chunks(leaves[i].shape[0])]
            arrivals = []
            for source, target in pieces:
                copy = pltpu.make_async_copy(source, target, sems.at[used])
                copy.start()
                arrivals.append(Arriving(target, copy))
                used += 1
            coming[i] = arrivals if i in parts else arrivals[0]
        for n, i in enumerate(stored):
            results[i] = Leaving(results[i], sems.at[used])
            used += 1
        kernel(
            *jax.tree.unflatten(tree, coming),
            jax.tree.unflatten(out_tree, results),
            *rest[len(far) :],
        )
        fetch(coming)
        for i in stored:
            results[i].done()

    n_sems = len(far) - len(parts) + len(stored) + len(parts) * PARTS
    size = sum(4 * math.prod(a.shape) for a in leaves + out_leaves)
    given = pl.pallas_call(
        body,
        out_shape=[
            pltpu.HBM(a.shape, F32) if i in distant else shaped(*a.shape)
            for i, a in enumerate(out_leaves)
        ],
        in_specs=[
            pl.BlockSpec(
                memory_space=pltpu.HBM if i in far + raw else pltpu.VMEM
            )
            for i in range(count)
        ],
        out_specs=[
            pl.BlockSpec(memory_space=pltpu.HBM if i in distant else pltpu.VMEM)
            for i in range(n_out)
        ],
        scratch_shapes=[pltpu.SemaphoreType.DMA((max(1, n_sems),))]
        + [pltpu.VMEM(leaves[i].shape, leaves[i].dtype) for i in far]
        + list(scratch),
        compiler_params=pltpu.CompilerParams(vmem_limit_bytes=VMEM_LIMIT),
        cost_estimate=pl.CostEstimate(flops=flops, bytes_accessed=size, transcendentals=0),
    )(*leaves)
    return jax.tree.unflatten(out_tree, given)


def chunks(count):
    each = count // PARTS
    return [pl.ds(p * each, each) for p in range(PARTS)]


def far(tree):
    return jax.tree.map(Far, tree)


def fetch(tree):
    return jax.tree.map(lambda one: one.get(), tree, is_leaf=lambda one: isinstance(one, Arriving))


def loop(first, last, body):
    lax.fori_loop(first, last, body, 0, unroll=UNROLL)


def shaped(*shape):
    return jax.ShapeDtypeStruct(shape, F32)


def face_shapes(shape, sizes, count, width):
    nx, ny, nz = shape
    blocks = count * width + (1 if width == 2 else 0)
    outs = {
        "x": {r: shaped(blocks, ny, nz) for r in rounds_of(sizes[0])},
        "y": {r: shaped(blocks, nx, nz) for r in rounds_of(sizes[1])},
    }
    if width == 2:
        outs["xy"] = {
            (rx, ry): shaped(4 * count + 4, nz)
            for rx in rounds_of(sizes[0])
            for ry in rounds_of(sizes[1])
        }
    return outs


def pack_faces(out, fields, sizes, width, ends=None):
    ix, iy, _ = where_am_i()
    for r, ref in out["x"].items():
        pack_x(ref, fields, r, ix, width, ends)
    for r, ref in out["y"].items():
        pack_y(ref, fields, r, iy, width, ends)
    for (rx, ry), ref in out.get("xy", {}).items():
        pack_xy(ref, fields, rx, ry, ix, iy, ends)


def send_z(tile, sizes):
    return {r: swap(tile, sizes, {2: r}) for r in rounds_of(sizes[2])}


def send_faces(faces, sizes):
    got = {
        "x": {r: swap(v, sizes, {0: r}) for r, v in faces["x"].items()},
        "y": {r: swap(v, sizes, {1: r}) for r, v in faces["y"].items()},
    }
    if "xy" in faces:
        got["xy"] = {(rx, ry): swap(v, sizes, {0: rx, 1: ry}) for (rx, ry), v in faces["xy"].items()}
    return got


def spread(rows):
    return lax.all_to_all(rows, AXES, 0, 0, tiled=True)


def shards(sizes, right_side, conductance, storage, dirichlet, basis, coarse_inverse):
    shape = right_side.shape
    nx, ny, nz = shape
    vecs = basis.shape[0]
    boxed = box_shape(shape)
    devices = sizes[0] * sizes[1] * sizes[2]
    row_shape = shaped(devices, LANES)
    sum_shape = (devices * vecs // LANES, LANES)
    ends_shape = (nx, ny, LANES)
    vbox = pltpu.VMEM(boxed, F32)
    def pack_first(cond, store, fixed, rhs, outs):
        near, free = outs["near"], outs["free"]
        for target, source in zip(near, (cond, store, rhs)):
            target.put(source.get())
        fixed = fixed.get()
        free[...] = 1.0 - fixed[...].astype(F32)
        cond, store, rhs = [one.done() for one in near]
        outs["tile"][...] = pack_z([cond.at[0], cond.at[1], cond.at[2], store, free, rhs])

    first = call(
        pack_first,
        {
            "near": [Stored(*a.shape, near=True) for a in (conductance, storage, right_side)],
            "free": shaped(*shape),
            "tile": shaped(z_rows(6), nx * ny),
        },
        (Raw(conductance), Raw(storage), Far(dirichlet), Raw(right_side)),
    )
    got_z = send_z(first["tile"], sizes)

    def first_rows(rhs, base, out):
        row = project(base, rhs.get()[...])
        out[...] = jnp.broadcast_to(row, out.shape)

    rows = call(first_rows, row_shape, (Far(right_side), Far(basis, True)))
    rows_a = spread(rows)

    def pack_all(got_z, near, free, rows, outs, ends):
        cond, store, rhs = fetch(near)
        fields = [cond.at[0], cond.at[1], cond.at[2], store, free.get(), rhs]
        ends[...] = pick_z(fetch(got_z), sizes, ends_shape)
        outs["ends"].put(ends)
        pack_faces(outs["faces"], fields, sizes, 2, ends)

    packed = call(
        pack_all,
        {"ends": Stored(*ends_shape), "faces": face_shapes(shape, sizes, 6, 2)},
        (got_z, first["near"], first["free"], rows),
        [pltpu.VMEM(ends_shape, F32)],
    )
    got = send_faces(packed["faces"], sizes)

    def first_smooth(got, cond, store, fixed, rhs, ends, outs, sems, step, *boxes):
        boxes = list(boxes)
        cond, store, rhs = fetch((cond, store, rhs))
        owns = [cond.at[0], cond.at[1], cond.at[2], store, None, rhs]
        copies = []
        for k, own in enumerate(owns):
            if own is not None:
                copies.append(
                    pltpu.make_async_copy(own, own_cells(boxes[k], shape), sems.at[k])
                )
                copies[-1].start()
        for b in boxes[:6]:
            clear_round(b, shape)
        got, fixed = fetch((got, fixed))
        boxes[4][3 : 3 + nx, 0:ny, 0:nz] = 1.0 - fixed[...].astype(F32)
        unpack_faces(boxes[:6], [None] * 6, got["x"], got["y"], sizes, 2, ends.get()[...])
        unpack_xy(boxes[:6], shape, got["xy"], sizes)
        for copy in copies:
            copy.wait()
        links, boxes = boxes[6:], boxes[:6]
        coefficients(boxes, links, step, outs["own"])
        for name, value in (("step", step), ("own", outs["own"])):
            outs["kept"][name].put(value)
        for kept, link in zip(outs["kept"]["links"], links):
            kept.put(link)
        jacobi(boxes[5], step, links, boxes[0], boxes[1], boxes[5], outs["smooth"])

    smoothed = call(
        first_smooth,
        {
            "smooth": shaped(*shape),
            "own": shaped(7, *shape),
            "kept": {
                "links": [Stored(*boxed), Stored(*boxed), Stored(*boxed)],
                "step": Stored(*boxed),
                "own": Stored(7, *shape),
            },
        },
        (
            far(got),
            Raw(conductance),
            Raw(storage),
            Far(dirichlet),
            Raw(right_side),
            Far(packed["ends"]),
        ),
        [pltpu.SemaphoreType.DMA((6,))] + [vbox] * 10,
        flops=SMOOTH_FLOPS,
    )
    kept = smoothed["kept"]
    own = smoothed["own"]

    def first_direction(smooth, rows, inverse, base, outs):
        smooth, rows = fetch((smooth, rows))
        weights = coarse_weights(inverse.get(), coarse_sum(rows, vecs))
        add_coarse(outs["z"], smooth, base, weights)
        outs["kept"].put(outs["z"])
        pack_faces(outs["faces"], [outs["z"]], sizes, 1)
        outs["tile"][...] = pack_z([outs["z"]])

    directed = call(
        first_direction,
        {
            "z": shaped(*shape),
            "kept": Stored(*shape),
            "faces": face_shapes(shape, sizes, 1, 1),
            "tile": shaped(z_rows(1), nx * ny),
        },
        (smoothed["smooth"], rows_a, Far(coarse_inverse), Far(basis, True)),
    )
    direction, kept_z = directed["z"], directed["kept"]
    got = send_faces(directed["faces"], sizes)
    got_z = send_z(directed["tile"], sizes)

    def apply(field, got, got_z, own, out, vb):
        clear_round(vb, shape)
        field, got, got_z = fetch((field, got, got_z))
        unpack_faces([vb], [field], got["x"], got["y"], sizes, 1)
        vb[3 : 3 + nx, 0:ny, nz : nz + LANES] = halo_lanes(pick_z(got_z, sizes, ends_shape), 0)
        own = own.get()

        def body(x, carry):
            mid = vb[x + 3]
            around = (mid, vb[x + 4], vb[x + 2])
            around += (ahead(mid, 0), behind(mid, 0), ahead(mid, 1), behind(mid, 1))
            total = own[0, x] * mid[0:ny, 0:nz]
            for n in range(1, 7):
                total = total - own[n, x] * around[n][0:ny, 0:nz]
            out[x] = total
            return carry

        loop(0, nx, body)

    def first_image(got, got_z, field, own, rhs, outs, vb):
        image = outs["image"]
        apply(field, got, got_z, own, image, vb)
        outs["kept"].put(image)
        outs["tile"][...] = pack_z([image])
        field, rhs = fetch((field, rhs))
        values = [full_sum(rhs[...] * field[...]), full_sum(field[...] * image[...])]
        outs["sums"][...] = put_scalars(jnp.zeros((1, LANES), F32), vecs, values)

    imaged = call(
        first_image,
        {
            "image": shaped(*shape),
            "kept": Stored(*shape),
            "tile": shaped(z_rows(1), nx * ny),
            "sums": shaped(1, LANES),
        },
        (got, got_z, direction, own, Far(right_side)),
        [vbox],
    )
    got_z = send_z(imaged["tile"], sizes)

    def second_rows(base, field, sums, out):
        row = project(base, field.get()[...]) + sums.get()[...]
        out[...] = jnp.broadcast_to(row, out.shape)

    rows = call(second_rows, row_shape, (Far(basis, True), imaged["image"], imaged["sums"]))
    rows_c = spread(rows)

    def pack_image(got_z, field, rows, outs, ends):
        ends[...] = pick_z(fetch(got_z), sizes, ends_shape)
        outs["ends"].put(ends)
        pack_faces(outs["faces"], [field.get()], sizes, 2, ends)

    packed = call(
        pack_image,
        {"ends": Stored(*ends_shape), "faces": face_shapes(shape, sizes, 1, 2)},
        (got_z, imaged["image"], rows),
        [pltpu.VMEM(ends_shape, F32)],
    )
    got = send_faces(packed["faces"], sizes)

    def second_smooth(got, field, ends, step, links, outs, sem, ga, gb, vb):
        copy = pltpu.make_async_copy(field.get(), own_cells(vb, shape), sem)
        copy.start()
        clear_round(vb, shape)
        got, ends = fetch((got, ends))
        unpack_faces([vb], [None], got["x"], got["y"], sizes, 2, ends[...])
        unpack_xy([vb], shape, got["xy"], sizes)
        copy.wait()
        step, links = fetch((step, links))
        jacobi(vb, step, links, ga, gb, vb, outs["smooth"])

    smoothed = call(
        second_smooth,
        {"smooth": shaped(*shape)},
        (
            got,
            Raw(imaged["kept"]),
            Far(packed["ends"]),
            Far(kept["step"]),
            far(kept["links"]),
        ),
        [pltpu.SemaphoreType.DMA] + [vbox] * 3,
        flops=SMOOTH_FLOPS,
    )

    def second_direction(smooth, rows, inverse, field, rhs, before, base, outs):
        smooth, rows = fetch((smooth, rows))
        norm, curve = scalar_sums(rows, vecs, 2)
        alpha = norm / curve
        weights = coarse_weights(inverse.get(), coarse_sum(rows, vecs))
        field, rhs, before = fetch((field, rhs, before))
        outs["residual"][...] = rhs[...] - alpha * field[...]
        add_coarse(outs["z"], smooth, base, weights)
        outs["z"][...] = before[...] - alpha * outs["z"][...]
        pack_faces(outs["faces"], [outs["z"]], sizes, 1)
        outs["tile"][...] = pack_z([outs["z"]])
        outs["scalars"][...] = jnp.concatenate(
            [jnp.broadcast_to(norm, (8, LANES)), jnp.broadcast_to(curve, (8, LANES))], axis=0
        )

    directed = call(
        second_direction,
        {
            "z": shaped(*shape),
            "residual": shaped(*shape),
            "scalars": shaped(16, LANES),
            "faces": face_shapes(shape, sizes, 1, 1),
            "tile": shaped(z_rows(1), nx * ny),
        },
        (
            smoothed["smooth"],
            rows_c,
            Far(coarse_inverse),
            Far(imaged["kept"]),
            Far(right_side),
            Far(kept_z),
            Far(basis, True),
        ),
    )
    precond, residual = directed["z"], directed["residual"]
    got = send_faces(directed["faces"], sizes)
    got_z = send_z(directed["tile"], sizes)
    image, direction = imaged["kept"], kept_z

    def second_image(got, got_z, field, own, image, residual, outs, vb):
        apply(field, got, got_z, own, outs["image"], vb)
        field, image, residual = fetch((field, image, residual))
        values = [
            full_sum(residual[...] * field[...]),
            full_sum(field[...] * outs["image"][...]),
            full_sum(field[...] * image[...]),
        ]
        row = put_scalars(jnp.zeros((1, LANES), F32), 0, values)
        outs["rows"][...] = jnp.broadcast_to(row, outs["rows"].shape)

    last = call(
        second_image,
        {"image": shaped(*shape), "rows": row_shape},
        (
            got,
            got_z,
            precond,
            Far(kept["own"]),
            image,
            residual,
        ),
        [vbox],
    )
    rows_e = spread(last["rows"])

    def finish(rows, scalars, direction, image, precond, precond_image, residual, outs):
        rows, scalars = fetch((rows, scalars))
        norm = scalars[0:1, 0:1]
        curve = scalars[8:9, 0:1]
        norm_next, curve_z, curve_mixed = scalar_sums(rows, 0, 3)
        alpha = norm / curve
        beta = norm_next / norm
        curve_next = curve_z + 2.0 * beta * curve_mixed + beta * beta * curve
        alpha_next = norm_next / curve_next
        direction, image, precond = fetch((direction, image, precond))
        precond_image, residual = fetch((precond_image, residual))
        outs[0][...] = alpha * direction[...] + alpha_next * (
            precond[...] + beta * direction[...]
        )
        outs[1][...] = residual[...] - alpha_next * (precond_image[...] + beta * image[...])

    return tuple(
        call(
            finish,
            [shaped(*shape), shaped(*shape)],
            (rows_e, directed["scalars"], direction, image, precond, last["image"], residual),
        )
    )


def solution(mesh):
    sizes = tuple(mesh.shape[a] for a in AXES)
    placed = (
        P("gx", "gy", "gz"),
        P(None, "gx", "gy", "gz"),
        P("gx", "gy", "gz"),
        P("gx", "gy", "gz"),
        P(None, "gx", "gy", "gz"),
        P(("gx", "gy", "gz"), None),
    )
    return jax.shard_map(
        functools.partial(shards, sizes),
        mesh=mesh,
        in_specs=placed,
        out_specs=(P("gx", "gy", "gz"), P("gx", "gy", "gz")),
        check_vma=False,
    )
```

```python
import functools
import math

import jax
import jax.numpy as jnp
from jax import lax
from jax.experimental import pallas as pl
from jax.experimental.pallas import tpu as pltpu
from jax.sharding import PartitionSpec as P

SWEEPS = 4
RELAX = 2.0 / 3.0
AXES = ("gx", "gy", "gz")
LANES = 128
VMEM_LIMIT = 24 * 1024 * 1024
F32 = jnp.float32
UNROLL = 16
PARTS = 8
NEAR_FIRST = range(1)
NEAR_SECOND = range(5)
SMOOTH_FLOPS = 10**9


def rounds_of(count):
    return (0, 1)[: 1 if count <= 2 else 2]


def mate(index, odd, count):
    other = index + 1 if index % 2 == odd else index - 1
    return other if 0 <= other < count else None


def swap(value, sizes, along):
    pairs = []
    nx, ny, nz = sizes
    for ix in range(nx):
        for iy in range(ny):
            for iz in range(nz):
                here = [ix, iy, iz]
                there = [
                    mate(here[a], along[a], sizes[a]) if a in along else here[a] for a in range(3)
                ]
                if None in there:
                    if 2 in along:
                        spare = nz - 1 - iz if iz in (0, nz - 1) else None
                    else:
                        spare = iz ^ 1 if nz % 2 == 0 else None
                    if spare is None:
                        continue
                    there = [ix, iy, spare]
                pairs.append(
                    ((ix * ny + iy) * nz + iz, (there[0] * ny + there[1]) * nz + there[2])
                )
    return lax.ppermute(value, AXES, pairs)


def upward(index, odd):
    return lax.rem(index, 2) == odd


def where_am_i():
    return [lax.axis_index(a) for a in AXES]


def lane_iota(shape):
    return lax.broadcasted_iota(jnp.int32, shape, len(shape) - 1)


def pack_x(out, fields, odd, index, width, ends=None):
    nx, _, nz = fields[0].shape
    count = len(fields) * width
    high = upward(index, odd)
    for cond, first in ((high, nx - width), (jnp.logical_not(high), 0)):

        @pl.when(cond)
        def _(first=first):
            for k, field in enumerate(fields):
                out[k * width : (k + 1) * width] = field[first : first + width]
            if ends is not None:
                for i in range(width):
                    out[count, :, LANES * i : LANES * (i + 1)] = ends[first + i]


def pack_y(out, fields, odd, index, width, ends=None):
    _, ny, nz = fields[0].shape
    count = len(fields) * width
    high = upward(index, odd)
    for cond, first in ((high, ny - width), (jnp.logical_not(high), 0)):

        @pl.when(cond)
        def _(first=first):
            for j in range(width):
                for k, field in enumerate(fields):
                    out[k * width + j] = field[:, first + j, :]
                if ends is not None:
                    out[count, :, LANES * j : LANES * (j + 1)] = ends[:, first + j, :]


def pack_xy(out, fields, rx, ry, ix, iy, ends):
    nx, ny, _ = fields[0].shape
    count = len(fields)
    for xhigh in (False, True):
        for yhigh in (False, True):

            @pl.when((upward(ix, rx) == xhigh) & (upward(iy, ry) == yhigh))
            def _(x0=(nx - 2 if xhigh else 0), y0=(ny - 2 if yhigh else 0)):
                for i in range(2):
                    for k, field in enumerate(fields):
                        out[4 * k + 2 * i : 4 * k + 2 * i + 2, :] = field[x0 + i, y0 : y0 + 2, :]
                    out[4 * count + 2 * i : 4 * count + 2 * i + 2, 0:LANES] = ends[
                        x0 + i, y0 : y0 + 2, :
                    ]


def z_rows(count):
    return (4 * count + 7) // 8 * 8


def pack_z(fields):
    nx, ny, nz = fields[0].shape
    lane = lane_iota((nx, ny, LANES))
    total = jnp.zeros((nx, ny, LANES), F32)
    for k, field in enumerate(fields):
        ends = jnp.where(lane < 64, field[:, :, 0:LANES], field[:, :, nz - LANES : nz])
        turned = pltpu.roll(ends, 4 * k + 2, 2)
        total = jnp.where((lane >= 4 * k) & (lane < 4 * k + 4), turned, total)
    return total.reshape(nx * ny, LANES).T[0 : z_rows(len(fields))]


def project(basis, field):
    nx, ny, nz = field.shape
    rows = []
    for piece in basis:
        vectors = piece.get()
        for k in range(vectors.shape[0]):
            prod = jnp.sum(vectors[k] * field, axis=0)
            part = jnp.zeros((8, LANES), F32)
            for y in range(ny // 8):
                for z in range(nz // LANES):
                    part = part + prod[8 * y : 8 * y + 8, LANES * z : LANES * (z + 1)]
            rows.append(jnp.sum(part, axis=0, keepdims=True))
    vecs = len(rows)
    totals = jnp.sum(jnp.concatenate(rows, axis=0), axis=1, keepdims=True)
    row = lax.broadcasted_iota(jnp.int32, (vecs, LANES), 0)
    return jnp.sum(jnp.where(lane_iota((vecs, LANES)) == row, totals, 0.0), axis=0, keepdims=True)


def put_scalars(row, first, values):
    lane = lane_iota(row.shape)
    for i, value in enumerate(values):
        row = jnp.where(lane == first + i, value, row)
    return row


def box_shape(shape):
    nx, ny, nz = shape
    return (nx + 6, ny + 8, nz + LANES)


def clear(box):
    def body(x, carry):
        box[x] = jnp.zeros(box.shape[1:], F32)
        return carry

    loop(0, box.shape[0], body)


def clear_round(box, shape):
    nx, ny, nz = shape
    planes, rows, lanes = box.shape
    for x in (0, 1, 2, planes - 3, planes - 2, planes - 1):
        box[x] = jnp.zeros((rows, lanes), F32)

    def body(x, carry):
        box[x, ny:rows, :] = jnp.zeros((rows - ny, lanes), F32)
        box[x, 0:ny, nz:lanes] = jnp.zeros((ny, lanes - nz), F32)
        return carry

    loop(3, 3 + nx, body)


def own_cells(box, shape):
    nx, ny, nz = shape
    return box.at[3 : 3 + nx, 0:ny, 0:nz]


def each_round(sizes, a, index, act):
    for r in rounds_of(sizes[a]):
        high = upward(index, r)

        @pl.when(high & (index + 1 < sizes[a]))
        def _(r=r):
            act(r, True)

        @pl.when(jnp.logical_not(high) & (index > 0))
        def _(r=r):
            act(r, False)


def unpack_faces(boxes, owns, xs, ys, sizes, width, ends=None):
    nx, ny, nz = boxes[0].shape[0] - 6, boxes[0].shape[1] - 8, boxes[0].shape[2] - LANES
    count = len(boxes) * width
    ix, iy, _ = where_am_i()
    for k, (box, own) in enumerate(zip(boxes, owns)):
        if own is not None:
            box[3 : 3 + nx, 0:ny, 0:nz] = own[...]
        if ends is not None:
            box[3 : 3 + nx, 0:ny, nz : nz + LANES] = halo_lanes(ends, k)

    def put_x(r, above):
        first = 3 + nx if above else 3 - width
        for k, box in enumerate(boxes):
            box[first : first + width, 0:ny, 0:nz] = xs[r][k * width : (k + 1) * width]
            if ends is not None:
                for i in range(width):
                    tile = xs[r][count, :, LANES * i : LANES * (i + 1)]
                    box[first + i, 0:ny, nz : nz + LANES] = halo_lanes(tile, k)

    each_round(sizes, 0, ix, put_x)

    def put_y(r, above):
        first = ny if above else ny + 8 - width
        for k, box in enumerate(boxes):
            for j in range(width):
                box[3 : 3 + nx, first + j, 0:nz] = ys[r][k * width + j]
                if ends is not None:
                    tile = ys[r][count, :, LANES * j : LANES * (j + 1)]
                    box[3 : 3 + nx, first + j, nz : nz + LANES] = halo_lanes(tile, k)

    each_round(sizes, 1, iy, put_y)


def unpack_xy(boxes, shape, xys, sizes):
    nx, ny, nz = shape
    count = len(boxes)
    ix, iy, _ = where_am_i()

    def put(rx, xabove):
        x0 = 3 + nx if xabove else 1

        def inner(ry, yabove):
            y0 = ny if yabove else ny + 6
            rows = xys[(rx, ry)]
            tile = rows[4 * count : 4 * count + 4, 0:LANES]
            for k, box in enumerate(boxes):
                turned = halo_lanes(tile, k)
                for i in range(2):
                    box[x0 + i, y0 : y0 + 2, 0:nz] = rows[4 * k + 2 * i : 4 * k + 2 * i + 2, :]
                    box[x0 + i, y0 : y0 + 2, nz : nz + LANES] = turned[2 * i : 2 * i + 2]

        each_round(sizes, 1, iy, inner)

    each_round(sizes, 0, ix, put)


def pick_z(zs, sizes, shape):
    count = sizes[2]
    iz = lax.axis_index("gz")
    rows, cells = zs[0].shape
    first = lax.rem(lax.broadcasted_iota(jnp.int32, (rows, cells), 0), 4) < 2
    total = jnp.zeros((rows, cells), F32)
    for r in rounds_of(count):
        high = upward(iz, r)
        below = jnp.logical_not(high) & (iz > 0)
        above = high & (iz + 1 < count)
        total = jnp.where((first & below) | (jnp.logical_not(first) & above), zs[r][...], total)
    filled = jnp.concatenate([total, jnp.zeros((LANES - rows, cells), F32)], axis=0)
    return filled.T.reshape(shape)


def halo_lanes(tile, k):
    lane = lane_iota(tile.shape)
    axis = len(tile.shape) - 1
    turned = pltpu.roll(tile, (-(4 * k + 2)) % LANES, axis)
    return jnp.where((lane < 2) | (lane >= LANES - 2), turned, 0.0)


def ahead(plane, axis):
    return pltpu.roll(plane, plane.shape[axis] - 1, axis)


def behind(plane, axis):
    return pltpu.roll(plane, 1, axis)


def neighbours(g, links, x):
    lx, ly, lz = links
    mid = g[x]
    y = ly[x]
    z = lz[x]
    total = lx[x] * g[x + 1] + lx[x - 1] * g[x - 1]
    total = total + y * ahead(mid, 0) + behind(y * mid, 0)
    return total + z * ahead(mid, 1) + behind(z * mid, 1)


def coefficients(fields, links, step, own):
    tx, ty, tz, store, free, _ = fields
    lx, ly, lz = links
    _, nx, ny, nz = own.shape
    last = tx.shape[0] - 1
    for ref in (lx, ly, lz, step):
        ref[0] = jnp.zeros(ref.shape[1:], F32)
        ref[last] = jnp.zeros(ref.shape[1:], F32)

    def body(x, carry, inside):
        f = free[x]
        a, b, c = tx[x], ty[x], tz[x]
        total = store[x] + a + tx[x - 1] + b + behind(b, 0) + c + behind(c, 1)
        d = f * total + (1.0 - f)
        step[x] = RELAX / d
        links_here = (a * f * free[x + 1], b * f * ahead(f, 0), c * f * ahead(f, 1))
        for ref, value in zip(links, links_here):
            ref[x] = value
        if inside:
            x_link, y_link, z_link = links_here
            mine = (
                d,
                x_link,
                lx[x - 1],
                y_link,
                behind(y_link, 0),
                z_link,
                behind(z_link, 1),
            )
            for n, value in enumerate(mine):
                own[n, x - 3] = value[0:ny, 0:nz]
        return carry

    loop(1, 3, functools.partial(body, inside=False))
    loop(3, 3 + nx, functools.partial(body, inside=True))
    loop(3 + nx, last, functools.partial(body, inside=False))


def jacobi(rhs, step, links, ga, gb, source, out):
    planes = rhs.shape[0]
    nx, ny, nz = out.shape
    for g in (ga, gb):
        g[0] = jnp.zeros(g.shape[1:], F32)
        g[planes - 1] = jnp.zeros(g.shape[1:], F32)

    def first(x, carry):
        source[x] = step[x] * rhs[x]
        return carry

    loop(1, planes - 1, first)

    def swept(now, x):
        return (1.0 - RELAX) * now[x] + source[x] + step[x] * neighbours(now, links, x)

    now, then, spare = source, ga, gb
    for sweep in range(1, SWEEPS - 1):
        edge = max(1, 3 - (SWEEPS - 1 - sweep))

        def body(x, carry, now=now, then=then):
            then[x] = swept(now, x)
            return carry

        loop(edge, planes - edge, body)
        now, then, spare = then, spare, then

    def final(x, carry):
        out[x] = swept(now, x + 3)[0:ny, 0:nz]
        return carry

    loop(0, nx, final)


def coarse_sum(rows_ref, vecs):
    count = rows_ref.shape[0]
    per = LANES // vecs
    lane = lane_iota((count, LANES))
    row = lax.broadcasted_iota(jnp.int32, (count, LANES), 0)
    all_rows = rows_ref[...]
    total = jnp.zeros((count, LANES), F32)
    for m in range(per):
        turned = pltpu.roll(all_rows, vecs * m, 1) if m else all_rows
        keep = (lax.rem(row, per) == m) & (lane >= vecs * m) & (lane < vecs * (m + 1))
        total = jnp.where(keep, turned, total)
    return jnp.sum(total.reshape(count // per, per, LANES), axis=1)


def scalar_sums(rows_ref, first, count):
    total = jnp.sum(rows_ref[...], axis=0, keepdims=True)
    return [total[0:1, first + i : first + i + 1] for i in range(count)]


def coarse_weights(inverse_ref, sums):
    total = jnp.zeros((inverse_ref.shape[0], LANES), F32)
    for g in range(sums.shape[0]):
        total = total + inverse_ref[:, LANES * g : LANES * (g + 1)] * sums[g : g + 1, :]
    return jnp.sum(total, axis=1, keepdims=True)


def add_coarse(out, smooth, basis, weights):
    nx, ny, nz = out.shape
    k = 0
    for piece in jax.tree.leaves(basis):
        vectors = piece.get()
        count = vectors.shape[0]
        scale = [jnp.broadcast_to(weights[k + i : k + i + 1, 0:1], (8, LANES)) for i in range(count)]
        scale = [jnp.tile(s, (ny // 8, nz // LANES)) for s in scale]
        source = smooth if k == 0 else out

        def body(x, carry, vectors=vectors, scale=scale, source=source):
            total = source[x]
            for i, s in enumerate(scale):
                total = total + s * vectors[i, x]
            out[x] = total
            return carry

        loop(0, nx, body)
        k += count


def full_sum(value):
    return jnp.sum(value)


class Arriving:
    def __init__(self, buffer, copy=None):
        self.copy = copy
        self.buffer = buffer

    def get(self):
        if self.copy is not None:
            self.copy.wait()
            self.copy = None
        return self.buffer


class Far:
    def __init__(self, value, parts=None):
        self.value, self.parts = value, parts


class Raw(Far):
    pass


class Stored:
    def __init__(self, *shape, near=False):
        self.shape, self.near = shape, near


class Leaving:
    def __init__(self, target, sem):
        self.target, self.sem, self.copy = target, sem, None

    def put(self, source):
        self.copy = pltpu.make_async_copy(source, self.target, self.sem)
        self.copy.start()

    def done(self):
        if self.copy is not None:
            self.copy.wait()
            self.copy = None
        return self.target


def call(kernel, outs, args, scratch=(), flops=0):
    leaves, tree = jax.tree.flatten(list(args), is_leaf=lambda one: isinstance(one, Far))
    out_leaves, out_tree = jax.tree.flatten(outs, is_leaf=lambda one: isinstance(one, Stored))
    count, n_out = len(leaves), len(out_leaves)
    raw = [i for i, a in enumerate(leaves) if isinstance(a, Raw)]
    far = [i for i, a in enumerate(leaves) if isinstance(a, Far) and i not in raw]
    distant = [i for i, a in enumerate(out_leaves) if isinstance(a, Stored) and not a.near]
    stored = [i for i, a in enumerate(out_leaves) if isinstance(a, Stored)]
    parts = {i: leaves[i].parts for i in far if leaves[i].parts is not None}
    leaves = [
        pltpu.with_memory_space_constraint(a.value, pltpu.HBM) if isinstance(a, Far) else a
        for a in leaves
    ]

    def body(*refs):
        sources, results = refs[:count], list(refs[count : count + n_out])
        rest = refs[count + n_out :]
        sems, rest = rest[0], rest[1:]
        coming = [Arriving(a) for a in sources]
        used = 0
        for n, i in enumerate(far):
            pieces = [(sources[i], rest[n])]
            if i in parts:
                pieces = [(sources[i].at[p], rest[n].at[p]) for p in chunks(leaves[i].shape[0], parts[i])]
            arrivals = []
            for source, target in pieces:
                copy = pltpu.make_async_copy(source, target, sems.at[used])
                copy.start()
                arrivals.append(Arriving(target, copy))
                used += 1
            coming[i] = arrivals if i in parts else arrivals[0]
        for n, i in enumerate(stored):
            results[i] = Leaving(results[i], sems.at[used])
            used += 1
        kernel(
            *jax.tree.unflatten(tree, coming),
            jax.tree.unflatten(out_tree, results),
            *rest[len(far) :],
        )
        fetch(coming)
        for i in stored:
            results[i].done()

    n_sems = len(far) - len(parts) + len(stored) + sum(len(p) for p in parts.values())
    size = sum(4 * math.prod(a.shape) for a in leaves + out_leaves)
    given = pl.pallas_call(
        body,
        out_shape=[
            pltpu.HBM(a.shape, F32) if i in distant else shaped(*a.shape)
            for i, a in enumerate(out_leaves)
        ],
        in_specs=[
            pl.BlockSpec(
                memory_space=pltpu.HBM if i in far + raw else pltpu.VMEM
            )
            for i in range(count)
        ],
        out_specs=[
            pl.BlockSpec(memory_space=pltpu.HBM if i in distant else pltpu.VMEM)
            for i in range(n_out)
        ],
        scratch_shapes=[pltpu.SemaphoreType.DMA((max(1, n_sems),))]
        + [pltpu.VMEM(leaves[i].shape, leaves[i].dtype) for i in far]
        + list(scratch),
        compiler_params=pltpu.CompilerParams(vmem_limit_bytes=VMEM_LIMIT),
        cost_estimate=pl.CostEstimate(flops=flops, bytes_accessed=size, transcendentals=0),
    )(*leaves)
    return jax.tree.unflatten(out_tree, given)


def chunks(count, parts):
    each = count // PARTS
    return [pl.ds(p * each, each) for p in parts]


def far(tree):
    return jax.tree.map(Far, tree)


def fetch(tree):
    return jax.tree.map(lambda one: one.get(), tree, is_leaf=lambda one: isinstance(one, Arriving))


def loop(first, last, body):
    lax.fori_loop(first, last, body, 0, unroll=UNROLL)


def shaped(*shape):
    return jax.ShapeDtypeStruct(shape, F32)


def face_shapes(shape, sizes, count, width):
    nx, ny, nz = shape
    blocks = count * width + (1 if width == 2 else 0)
    outs = {
        "x": {r: shaped(blocks, ny, nz) for r in rounds_of(sizes[0])},
        "y": {r: shaped(blocks, nx, nz) for r in rounds_of(sizes[1])},
    }
    if width == 2:
        outs["xy"] = {
            (rx, ry): shaped(4 * count + 4, nz)
            for rx in rounds_of(sizes[0])
            for ry in rounds_of(sizes[1])
        }
    return outs


def pack_faces(out, fields, sizes, width, ends=None):
    ix, iy, _ = where_am_i()
    for r, ref in out["x"].items():
        pack_x(ref, fields, r, ix, width, ends)
    for r, ref in out["y"].items():
        pack_y(ref, fields, r, iy, width, ends)
    for (rx, ry), ref in out.get("xy", {}).items():
        pack_xy(ref, fields, rx, ry, ix, iy, ends)


def send_z(tile, sizes):
    return {r: swap(tile, sizes, {2: r}) for r in rounds_of(sizes[2])}


def send_faces(faces, sizes):
    got = {
        "x": {r: swap(v, sizes, {0: r}) for r, v in faces["x"].items()},
        "y": {r: swap(v, sizes, {1: r}) for r, v in faces["y"].items()},
    }
    if "xy" in faces:
        got["xy"] = {(rx, ry): swap(v, sizes, {0: rx, 1: ry}) for (rx, ry), v in faces["xy"].items()}
    return got


def spread(rows):
    return lax.all_to_all(rows, AXES, 0, 0, tiled=True)


def shards(sizes, right_side, conductance, storage, dirichlet, basis, coarse_inverse):
    shape = right_side.shape
    nx, ny, nz = shape
    vecs = basis.shape[0]
    boxed = box_shape(shape)
    devices = sizes[0] * sizes[1] * sizes[2]
    row_shape = shaped(devices, LANES)
    sum_shape = (devices * vecs // LANES, LANES)
    ends_shape = (nx, ny, LANES)
    vbox = pltpu.VMEM(boxed, F32)
    def pack_first(cond, store, fixed, rhs, outs):
        near, free = outs["near"], outs["free"]
        for target, source in zip(near, (cond, store, rhs)):
            target.put(source.get())
        fixed = fixed.get()
        free[...] = 1.0 - fixed[...].astype(F32)
        cond, store, rhs = [one.done() for one in near]
        outs["tile"][...] = pack_z([cond.at[0], cond.at[1], cond.at[2], store, free, rhs])

    first = call(
        pack_first,
        {
            "near": [Stored(*a.shape, near=True) for a in (conductance, storage, right_side)],
            "free": shaped(*shape),
            "tile": shaped(z_rows(6), nx * ny),
        },
        (Raw(conductance), Raw(storage), Far(dirichlet), Raw(right_side)),
    )
    got_z = send_z(first["tile"], sizes)

    def first_rows(rhs, base, out):
        row = project(base, rhs.get()[...])
        out[...] = jnp.broadcast_to(row, out.shape)

    rows = call(first_rows, row_shape, (Far(right_side), Far(basis, range(PARTS))))
    rows_a = spread(rows)

    def pack_all(got_z, near, free, rows, outs, ends):
        cond, store, rhs = fetch(near)
        fields = [cond.at[0], cond.at[1], cond.at[2], store, free.get(), rhs]
        ends[...] = pick_z(fetch(got_z), sizes, ends_shape)
        pack_faces(outs, fields, sizes, 2, ends)

    packed = call(
        pack_all,
        face_shapes(shape, sizes, 6, 2),
        (got_z, first["near"], first["free"], rows),
        [pltpu.VMEM(ends_shape, F32)],
    )
    got = send_faces(packed, sizes)

    def first_smooth(got, cond, store, fixed, rhs, got_z, base, outs, sems, step, *boxes):
        boxes = list(boxes)
        cond, store, rhs = fetch((cond, store, rhs))
        owns = [cond.at[0], cond.at[1], cond.at[2], store, None, rhs]
        copies = []
        for k, own in enumerate(owns):
            if own is not None:
                copies.append(
                    pltpu.make_async_copy(own, own_cells(boxes[k], shape), sems.at[k])
                )
                copies[-1].start()
        for b in boxes[:6]:
            clear_round(b, shape)
        got, fixed = fetch((got, fixed))
        ends = pick_z(fetch(got_z), sizes, ends_shape)
        boxes[4][3 : 3 + nx, 0:ny, 0:nz] = 1.0 - fixed[...].astype(F32)
        unpack_faces(boxes[:6], [None] * 6, got["x"], got["y"], sizes, 2, ends)
        unpack_xy(boxes[:6], shape, got["xy"], sizes)
        for copy in copies:
            copy.wait()
        for target, piece in zip(outs["base"], chunks(vecs, NEAR_FIRST)):
            target.put(base.get().at[piece])
        links, boxes = boxes[6:], boxes[:6]
        coefficients(boxes, links, step, outs["own"])
        outs["kept"]["step"].put(step)
        for kept, link in zip(outs["kept"]["links"], links):
            kept.put(link)
        jacobi(boxes[5], step, links, boxes[0], boxes[1], boxes[5], outs["smooth"])

    smoothed = call(
        first_smooth,
        {
            "smooth": shaped(*shape),
            "own": shaped(7, *shape),
            "base": [Stored(vecs // PARTS, *shape, near=True) for _ in NEAR_FIRST],
            "kept": {
                "links": [Stored(*boxed), Stored(*boxed), Stored(*boxed)],
                "step": Stored(*boxed),
            },
        },
        (
            got,
            Raw(conductance),
            Raw(storage),
            Far(dirichlet),
            Raw(right_side),
            got_z,
            Raw(basis),
        ),
        [pltpu.SemaphoreType.DMA((6,))] + [vbox] * 10,
        flops=SMOOTH_FLOPS,
    )
    kept = smoothed["kept"]
    own = smoothed["own"]

    def base_rest(smoothed, near):
        return smoothed["base"] + [Far(basis, range(len(near), PARTS))]

    def first_direction(smooth, rows, inverse, base, outs):
        smooth, rows = fetch((smooth, rows))
        weights = coarse_weights(inverse.get(), coarse_sum(rows, vecs))
        add_coarse(outs["z"], smooth, base, weights)
        outs["kept"].put(outs["z"])
        pack_faces(outs["faces"], [outs["z"]], sizes, 1)
        outs["tile"][...] = pack_z([outs["z"]])

    directed = call(
        first_direction,
        {
            "z": shaped(*shape),
            "kept": Stored(*shape),
            "faces": face_shapes(shape, sizes, 1, 1),
            "tile": shaped(z_rows(1), nx * ny),
        },
        (smoothed["smooth"], rows_a, Far(coarse_inverse), base_rest(smoothed, NEAR_FIRST)),
    )
    direction, kept_z = directed["z"], directed["kept"]
    got = send_faces(directed["faces"], sizes)
    got_z = send_z(directed["tile"], sizes)

    def apply(field, got, got_z, own, out, vb):
        clear_round(vb, shape)
        field, got, got_z = fetch((field, got, got_z))
        unpack_faces([vb], [field], got["x"], got["y"], sizes, 1)
        vb[3 : 3 + nx, 0:ny, nz : nz + LANES] = halo_lanes(pick_z(got_z, sizes, ends_shape), 0)
        own = own.get()

        def body(x, carry):
            mid = vb[x + 3]
            around = (mid, vb[x + 4], vb[x + 2])
            around += (ahead(mid, 0), behind(mid, 0), ahead(mid, 1), behind(mid, 1))
            total = own[0, x] * mid[0:ny, 0:nz]
            for n in range(1, 7):
                total = total - own[n, x] * around[n][0:ny, 0:nz]
            out[x] = total
            return carry

        loop(0, nx, body)

    def first_image(got, got_z, field, own, rhs, outs, vb):
        image = outs["image"]
        outs["own"].put(own.get())
        apply(field, got, got_z, own, image, vb)
        outs["kept"].put(image)
        outs["tile"][...] = pack_z([image])
        field, rhs = fetch((field, rhs))
        values = [full_sum(rhs[...] * field[...]), full_sum(field[...] * image[...])]
        outs["sums"][...] = put_scalars(jnp.zeros((1, LANES), F32), vecs, values)

    imaged = call(
        first_image,
        {
            "image": shaped(*shape),
            "kept": Stored(*shape),
            "own": Stored(7, *shape),
            "tile": shaped(z_rows(1), nx * ny),
            "sums": shaped(1, LANES),
        },
        (got, got_z, direction, own, Far(right_side)),
        [vbox],
    )
    got_z = send_z(imaged["tile"], sizes)

    def second_rows(base, field, sums, out):
        row = project(base, field.get()[...]) + sums.get()[...]
        out[...] = jnp.broadcast_to(row, out.shape)

    rows = call(second_rows, row_shape, (Far(basis, range(PARTS)), imaged["image"], imaged["sums"]))
    rows_c = spread(rows)

    def pack_image(got_z, field, rows, outs, ends):
        ends[...] = pick_z(fetch(got_z), sizes, ends_shape)
        pack_faces(outs, [field.get()], sizes, 2, ends)

    packed = call(
        pack_image,
        face_shapes(shape, sizes, 1, 2),
        (got_z, imaged["image"], rows),
        [pltpu.VMEM(ends_shape, F32)],
    )
    got = send_faces(packed, sizes)

    def second_smooth(got, field, got_z, step, links, base, outs, sem, ga, gb, vb):
        copy = pltpu.make_async_copy(field.get(), own_cells(vb, shape), sem)
        copy.start()
        clear_round(vb, shape)
        got = fetch(got)
        ends = pick_z(fetch(got_z), sizes, ends_shape)
        unpack_faces([vb], [None], got["x"], got["y"], sizes, 2, ends)
        unpack_xy([vb], shape, got["xy"], sizes)
        copy.wait()
        step, links = fetch((step, links))
        for target, piece in zip(outs["base"], chunks(vecs, NEAR_SECOND)):
            target.put(base.get().at[piece])
        jacobi(vb, step, links, ga, gb, vb, outs["smooth"])

    smoothed = call(
        second_smooth,
        {
            "smooth": shaped(*shape),
            "base": [Stored(vecs // PARTS, *shape, near=True) for _ in NEAR_SECOND],
        },
        (
            got,
            Raw(imaged["kept"]),
            got_z,
            Far(kept["step"]),
            far(kept["links"]),
            Raw(basis),
        ),
        [pltpu.SemaphoreType.DMA] + [vbox] * 3,
        flops=SMOOTH_FLOPS,
    )

    def second_direction(smooth, rows, inverse, field, rhs, before, base, own, outs):
        smooth, rows = fetch((smooth, rows))
        norm, curve = scalar_sums(rows, vecs, 2)
        alpha = norm / curve
        weights = coarse_weights(inverse.get(), coarse_sum(rows, vecs))
        field, rhs, before = fetch((field, rhs, before))
        outs["own"].put(own.get())
        outs["residual"][...] = rhs[...] - alpha * field[...]
        add_coarse(outs["z"], smooth, base, weights)
        outs["z"][...] = before[...] - alpha * outs["z"][...]
        pack_faces(outs["faces"], [outs["z"]], sizes, 1)
        outs["tile"][...] = pack_z([outs["z"]])
        outs["scalars"][...] = jnp.concatenate(
            [jnp.broadcast_to(norm, (8, LANES)), jnp.broadcast_to(curve, (8, LANES))], axis=0
        )

    directed = call(
        second_direction,
        {
            "z": shaped(*shape),
            "residual": shaped(*shape),
            "own": Stored(7, *shape, near=True),
            "scalars": shaped(16, LANES),
            "faces": face_shapes(shape, sizes, 1, 1),
            "tile": shaped(z_rows(1), nx * ny),
        },
        (
            smoothed["smooth"],
            rows_c,
            Far(coarse_inverse),
            Far(imaged["kept"]),
            Far(right_side),
            Far(kept_z),
            base_rest(smoothed, NEAR_SECOND),
            Raw(imaged["own"]),
        ),
    )
    precond, residual = directed["z"], directed["residual"]
    got = send_faces(directed["faces"], sizes)
    got_z = send_z(directed["tile"], sizes)
    image, direction = imaged["kept"], kept_z

    def second_image(got, got_z, field, own, image, residual, outs, vb):
        apply(field, got, got_z, own, outs["image"], vb)
        field, image, residual = fetch((field, image, residual))
        values = [
            full_sum(residual[...] * field[...]),
            full_sum(field[...] * outs["image"][...]),
            full_sum(field[...] * image[...]),
        ]
        row = put_scalars(jnp.zeros((1, LANES), F32), 0, values)
        outs["rows"][...] = jnp.broadcast_to(row, outs["rows"].shape)

    last = call(
        second_image,
        {"image": shaped(*shape), "rows": row_shape},
        (
            got,
            got_z,
            precond,
            directed["own"],
            image,
            residual,
        ),
        [vbox],
    )
    rows_e = spread(last["rows"])

    def finish(rows, scalars, direction, image, precond, precond_image, residual, outs):
        rows, scalars = fetch((rows, scalars))
        norm = scalars[0:1, 0:1]
        curve = scalars[8:9, 0:1]
        norm_next, curve_z, curve_mixed = scalar_sums(rows, 0, 3)
        alpha = norm / curve
        beta = norm_next / norm
        curve_next = curve_z + 2.0 * beta * curve_mixed + beta * beta * curve
        alpha_next = norm_next / curve_next
        direction, image, precond = fetch((direction, image, precond))
        precond_image, residual = fetch((precond_image, residual))
        outs[0][...] = alpha * direction[...] + alpha_next * (
            precond[...] + beta * direction[...]
        )
        outs[1][...] = residual[...] - alpha_next * (precond_image[...] + beta * image[...])

    return tuple(
        call(
            finish,
            [shaped(*shape), shaped(*shape)],
            (rows_e, directed["scalars"], direction, image, precond, last["image"], residual),
        )
    )


def solution(mesh):
    sizes = tuple(mesh.shape[a] for a in AXES)
    placed = (
        P("gx", "gy", "gz"),
        P(None, "gx", "gy", "gz"),
        P("gx", "gy", "gz"),
        P("gx", "gy", "gz"),
        P(None, "gx", "gy", "gz"),
        P(("gx", "gy", "gz"), None),
    )
    return jax.shard_map(
        functools.partial(shards, sizes),
        mesh=mesh,
        in_specs=placed,
        out_specs=(P("gx", "gy", "gz"), P("gx", "gy", "gz")),
        check_vma=False,
    )
```

```python
import functools
import math

import jax
import jax.numpy as jnp
from jax import lax
from jax.experimental import pallas as pl
from jax.experimental.pallas import tpu as pltpu
from jax.sharding import PartitionSpec as P

SWEEPS = 4
RELAX = 2.0 / 3.0
AXES = ("gx", "gy", "gz")
LANES = 128
VMEM_LIMIT = 24 * 1024 * 1024
F32 = jnp.float32
UNROLL = 16
SWEEP_UNROLL = True
PARTS = 8
NEAR_FIRST = range(1)
NEAR_SECOND = range(5)
SMOOTH_FLOPS = 10**9


def rounds_of(count):
    return (0, 1)[: 1 if count <= 2 else 2]


def mate(index, odd, count):
    other = index + 1 if index % 2 == odd else index - 1
    return other if 0 <= other < count else None


def swap(value, sizes, along):
    pairs = []
    nx, ny, nz = sizes
    for ix in range(nx):
        for iy in range(ny):
            for iz in range(nz):
                here = [ix, iy, iz]
                there = [
                    mate(here[a], along[a], sizes[a]) if a in along else here[a] for a in range(3)
                ]
                if None in there:
                    if 2 in along:
                        spare = nz - 1 - iz if iz in (0, nz - 1) else None
                    else:
                        spare = iz ^ 1 if nz % 2 == 0 else None
                    if spare is None:
                        continue
                    there = [ix, iy, spare]
                pairs.append(
                    ((ix * ny + iy) * nz + iz, (there[0] * ny + there[1]) * nz + there[2])
                )
    return lax.ppermute(value, AXES, pairs)


def upward(index, odd):
    return lax.rem(index, 2) == odd


def where_am_i():
    return [lax.axis_index(a) for a in AXES]


def lane_iota(shape):
    return lax.broadcasted_iota(jnp.int32, shape, len(shape) - 1)


def pack_x(out, fields, odd, index, width, ends=None):
    nx, _, nz = fields[0].shape
    count = len(fields) * width
    high = upward(index, odd)
    for cond, first in ((high, nx - width), (jnp.logical_not(high), 0)):

        @pl.when(cond)
        def _(first=first):
            for k, field in enumerate(fields):
                out[k * width : (k + 1) * width] = field[first : first + width]
            if ends is not None:
                for i in range(width):
                    out[count, :, LANES * i : LANES * (i + 1)] = ends[first + i]


def pack_y(out, fields, odd, index, width, ends=None):
    _, ny, nz = fields[0].shape
    count = len(fields) * width
    high = upward(index, odd)
    for cond, first in ((high, ny - width), (jnp.logical_not(high), 0)):

        @pl.when(cond)
        def _(first=first):
            for j in range(width):
                for k, field in enumerate(fields):
                    out[k * width + j] = field[:, first + j, :]
                if ends is not None:
                    out[count, :, LANES * j : LANES * (j + 1)] = ends[:, first + j, :]


def pack_xy(out, fields, rx, ry, ix, iy, ends):
    nx, ny, _ = fields[0].shape
    count = len(fields)
    for xhigh in (False, True):
        for yhigh in (False, True):

            @pl.when((upward(ix, rx) == xhigh) & (upward(iy, ry) == yhigh))
            def _(x0=(nx - 2 if xhigh else 0), y0=(ny - 2 if yhigh else 0)):
                for i in range(2):
                    for k, field in enumerate(fields):
                        out[4 * k + 2 * i : 4 * k + 2 * i + 2, :] = field[x0 + i, y0 : y0 + 2, :]
                    out[4 * count + 2 * i : 4 * count + 2 * i + 2, 0:LANES] = ends[
                        x0 + i, y0 : y0 + 2, :
                    ]


def z_rows(count):
    return (4 * count + 7) // 8 * 8


def pack_z(fields):
    nx, ny, nz = fields[0].shape
    lane = lane_iota((nx, ny, LANES))
    total = jnp.zeros((nx, ny, LANES), F32)
    for k, field in enumerate(fields):
        ends = jnp.where(lane < 64, field[:, :, 0:LANES], field[:, :, nz - LANES : nz])
        turned = pltpu.roll(ends, 4 * k + 2, 2)
        total = jnp.where((lane >= 4 * k) & (lane < 4 * k + 4), turned, total)
    return total.reshape(nx * ny, LANES).T[0 : z_rows(len(fields))]


def project(basis, field):
    nx, ny, nz = field.shape
    rows = []
    for piece in basis:
        vectors = piece.get()
        for k in range(vectors.shape[0]):
            prod = jnp.sum(vectors[k] * field, axis=0)
            part = jnp.zeros((8, LANES), F32)
            for y in range(ny // 8):
                for z in range(nz // LANES):
                    part = part + prod[8 * y : 8 * y + 8, LANES * z : LANES * (z + 1)]
            rows.append(jnp.sum(part, axis=0, keepdims=True))
    vecs = len(rows)
    totals = jnp.sum(jnp.concatenate(rows, axis=0), axis=1, keepdims=True)
    row = lax.broadcasted_iota(jnp.int32, (vecs, LANES), 0)
    return jnp.sum(jnp.where(lane_iota((vecs, LANES)) == row, totals, 0.0), axis=0, keepdims=True)


def put_scalars(row, first, values):
    lane = lane_iota(row.shape)
    for i, value in enumerate(values):
        row = jnp.where(lane == first + i, value, row)
    return row


def box_shape(shape):
    nx, ny, nz = shape
    return (nx + 6, ny + 8, nz + LANES)


def clear(box):
    def body(x, carry):
        box[x] = jnp.zeros(box.shape[1:], F32)
        return carry

    loop(0, box.shape[0], body)


def clear_round(box, shape):
    nx, ny, nz = shape
    planes, rows, lanes = box.shape
    for x in (0, 1, 2, planes - 3, planes - 2, planes - 1):
        box[x] = jnp.zeros((rows, lanes), F32)

    def body(x, carry):
        box[x, ny:rows, :] = jnp.zeros((rows - ny, lanes), F32)
        box[x, 0:ny, nz:lanes] = jnp.zeros((ny, lanes - nz), F32)
        return carry

    loop(3, 3 + nx, body)


def own_cells(box, shape):
    nx, ny, nz = shape
    return box.at[3 : 3 + nx, 0:ny, 0:nz]


def each_round(sizes, a, index, act):
    for r in rounds_of(sizes[a]):
        high = upward(index, r)

        @pl.when(high & (index + 1 < sizes[a]))
        def _(r=r):
            act(r, True)

        @pl.when(jnp.logical_not(high) & (index > 0))
        def _(r=r):
            act(r, False)


def unpack_faces(boxes, owns, xs, ys, sizes, width, ends=None):
    nx, ny, nz = boxes[0].shape[0] - 6, boxes[0].shape[1] - 8, boxes[0].shape[2] - LANES
    count = len(boxes) * width
    ix, iy, _ = where_am_i()
    for k, (box, own) in enumerate(zip(boxes, owns)):
        if own is not None:
            box[3 : 3 + nx, 0:ny, 0:nz] = own[...]
        if ends is not None:
            box[3 : 3 + nx, 0:ny, nz : nz + LANES] = halo_lanes(ends, k)

    def put_x(r, above):
        first = 3 + nx if above else 3 - width
        for k, box in enumerate(boxes):
            box[first : first + width, 0:ny, 0:nz] = xs[r][k * width : (k + 1) * width]
            if ends is not None:
                for i in range(width):
                    tile = xs[r][count, :, LANES * i : LANES * (i + 1)]
                    box[first + i, 0:ny, nz : nz + LANES] = halo_lanes(tile, k)

    each_round(sizes, 0, ix, put_x)

    def put_y(r, above):
        first = ny if above else ny + 8 - width
        for k, box in enumerate(boxes):
            for j in range(width):
                box[3 : 3 + nx, first + j, 0:nz] = ys[r][k * width + j]
                if ends is not None:
                    tile = ys[r][count, :, LANES * j : LANES * (j + 1)]
                    box[3 : 3 + nx, first + j, nz : nz + LANES] = halo_lanes(tile, k)

    each_round(sizes, 1, iy, put_y)


def unpack_xy(boxes, shape, xys, sizes):
    nx, ny, nz = shape
    count = len(boxes)
    ix, iy, _ = where_am_i()

    def put(rx, xabove):
        x0 = 3 + nx if xabove else 1

        def inner(ry, yabove):
            y0 = ny if yabove else ny + 6
            rows = xys[(rx, ry)]
            tile = rows[4 * count : 4 * count + 4, 0:LANES]
            for k, box in enumerate(boxes):
                turned = halo_lanes(tile, k)
                for i in range(2):
                    box[x0 + i, y0 : y0 + 2, 0:nz] = rows[4 * k + 2 * i : 4 * k + 2 * i + 2, :]
                    box[x0 + i, y0 : y0 + 2, nz : nz + LANES] = turned[2 * i : 2 * i + 2]

        each_round(sizes, 1, iy, inner)

    each_round(sizes, 0, ix, put)


def pick_z(zs, sizes, shape):
    count = sizes[2]
    iz = lax.axis_index("gz")
    rows, cells = zs[0].shape
    first = lax.rem(lax.broadcasted_iota(jnp.int32, (rows, cells), 0), 4) < 2
    total = jnp.zeros((rows, cells), F32)
    for r in rounds_of(count):
        high = upward(iz, r)
        below = jnp.logical_not(high) & (iz > 0)
        above = high & (iz + 1 < count)
        total = jnp.where((first & below) | (jnp.logical_not(first) & above), zs[r][...], total)
    filled = jnp.concatenate([total, jnp.zeros((LANES - rows, cells), F32)], axis=0)
    return filled.T.reshape(shape)


def halo_lanes(tile, k):
    lane = lane_iota(tile.shape)
    axis = len(tile.shape) - 1
    turned = pltpu.roll(tile, (-(4 * k + 2)) % LANES, axis)
    return jnp.where((lane < 2) | (lane >= LANES - 2), turned, 0.0)


def ahead(plane, axis):
    return pltpu.roll(plane, plane.shape[axis] - 1, axis)


def behind(plane, axis):
    return pltpu.roll(plane, 1, axis)


def coefficients(fields, links, step, own):
    tx, ty, tz, store, free, _ = fields
    lx, ly, lz = links
    _, nx, ny, nz = own.shape
    last = tx.shape[0] - 1
    for ref in (lx, ly, lz, step):
        ref[0] = jnp.zeros(ref.shape[1:], F32)
        ref[last] = jnp.zeros(ref.shape[1:], F32)

    def body(x, carry, inside):
        f = free[x]
        a, b, c = tx[x], ty[x], tz[x]
        total = store[x] + a + tx[x - 1] + b + behind(b, 0) + c + behind(c, 1)
        d = f * total + (1.0 - f)
        step[x] = RELAX / d
        links_here = (a * f * free[x + 1], b * f * ahead(f, 0), c * f * ahead(f, 1))
        for ref, value in zip(links, links_here):
            ref[x] = value
        if inside:
            x_link, y_link, z_link = links_here
            mine = (
                d,
                x_link,
                lx[x - 1],
                y_link,
                behind(y_link, 0),
                z_link,
                behind(z_link, 1),
            )
            for n, value in enumerate(mine):
                own[n, x - 3] = value[0:ny, 0:nz]
        return carry

    loop(1, 3, functools.partial(body, inside=False))
    loop(3, 3 + nx, functools.partial(body, inside=True))
    loop(3 + nx, last, functools.partial(body, inside=False))


def jacobi(rhs, step, links, ga, gb, source, out):
    planes = rhs.shape[0]
    nx, ny, nz = out.shape
    for g in (ga, gb):
        g[0] = jnp.zeros(g.shape[1:], F32)
        g[planes - 1] = jnp.zeros(g.shape[1:], F32)

    def first(x, carry):
        source[x] = step[x] * rhs[x]
        return carry

    loop(1, planes - 1, first)

    lx, ly, lz = fetch(links)

    def swept(now, x, carry):
        before, mid, x_before = carry
        after, x_here, y, z = now[x + 1], lx[x], ly[x], lz[x]
        total = x_here * after + x_before * before
        total = total + y * ahead(mid, 0) + behind(y * mid, 0)
        total = total + z * ahead(mid, 1) + behind(z * mid, 1)
        value = (1.0 - RELAX) * mid + source[x] + step[x] * total
        return value, (mid, after, x_here)

    def sweep_planes(now, first, last, put):
        def body(x, carry):
            value, carry = swept(now, x, carry)
            put(x, value)
            return carry

        start = (now[first - 1], now[first], lx[first - 1])
        lax.fori_loop(first, last, body, start, unroll=SWEEP_UNROLL)

    now, then, spare = source, ga, gb
    for sweep in range(1, SWEEPS - 1):
        edge = max(1, 3 - (SWEEPS - 1 - sweep))

        def put(x, value, then=then):
            then[x] = value

        sweep_planes(now, edge, planes - edge, put)
        now, then, spare = then, spare, then

    def put_own(x, value):
        out[x - 3] = value[0:ny, 0:nz]

    sweep_planes(now, 3, 3 + nx, put_own)


def coarse_sum(rows_ref, vecs):
    count = rows_ref.shape[0]
    per = LANES // vecs
    lane = lane_iota((count, LANES))
    row = lax.broadcasted_iota(jnp.int32, (count, LANES), 0)
    all_rows = rows_ref[...]
    total = jnp.zeros((count, LANES), F32)
    for m in range(per):
        turned = pltpu.roll(all_rows, vecs * m, 1) if m else all_rows
        keep = (lax.rem(row, per) == m) & (lane >= vecs * m) & (lane < vecs * (m + 1))
        total = jnp.where(keep, turned, total)
    return jnp.sum(total.reshape(count // per, per, LANES), axis=1)


def scalar_sums(rows_ref, first, count):
    total = jnp.sum(rows_ref[...], axis=0, keepdims=True)
    return [total[0:1, first + i : first + i + 1] for i in range(count)]


def coarse_weights(inverse_ref, sums):
    total = jnp.zeros((inverse_ref.shape[0], LANES), F32)
    for g in range(sums.shape[0]):
        total = total + inverse_ref[:, LANES * g : LANES * (g + 1)] * sums[g : g + 1, :]
    return jnp.sum(total, axis=1, keepdims=True)


def add_coarse(out, smooth, basis, weights):
    nx, ny, nz = out.shape
    k = 0
    for piece in jax.tree.leaves(basis):
        vectors = piece.get()
        count = vectors.shape[0]
        scale = [jnp.broadcast_to(weights[k + i : k + i + 1, 0:1], (8, LANES)) for i in range(count)]
        scale = [jnp.tile(s, (ny // 8, nz // LANES)) for s in scale]
        source = smooth if k == 0 else out

        def body(x, carry, vectors=vectors, scale=scale, source=source):
            total = source[x]
            for i, s in enumerate(scale):
                total = total + s * vectors[i, x]
            out[x] = total
            return carry

        loop(0, nx, body)
        k += count


def full_sum(value):
    return jnp.sum(value)


class Arriving:
    def __init__(self, buffer, copy=None):
        self.copy = copy
        self.buffer = buffer

    def get(self):
        if self.copy is not None:
            self.copy.wait()
            self.copy = None
        return self.buffer


class Far:
    def __init__(self, value, parts=None):
        self.value, self.parts = value, parts


class Raw(Far):
    pass


class Stored:
    def __init__(self, *shape, near=False):
        self.shape, self.near = shape, near


class Leaving:
    def __init__(self, target, sem):
        self.target, self.sem, self.copy = target, sem, None

    def put(self, source):
        self.copy = pltpu.make_async_copy(source, self.target, self.sem)
        self.copy.start()

    def done(self):
        if self.copy is not None:
            self.copy.wait()
            self.copy = None
        return self.target


def call(kernel, outs, args, scratch=(), flops=0):
    leaves, tree = jax.tree.flatten(list(args), is_leaf=lambda one: isinstance(one, Far))
    out_leaves, out_tree = jax.tree.flatten(outs, is_leaf=lambda one: isinstance(one, Stored))
    count, n_out = len(leaves), len(out_leaves)
    raw = [i for i, a in enumerate(leaves) if isinstance(a, Raw)]
    far = [i for i, a in enumerate(leaves) if isinstance(a, Far) and i not in raw]
    distant = [i for i, a in enumerate(out_leaves) if isinstance(a, Stored) and not a.near]
    stored = [i for i, a in enumerate(out_leaves) if isinstance(a, Stored)]
    parts = {i: leaves[i].parts for i in far if leaves[i].parts is not None}
    leaves = [
        pltpu.with_memory_space_constraint(a.value, pltpu.HBM) if isinstance(a, Far) else a
        for a in leaves
    ]

    def body(*refs):
        sources, results = refs[:count], list(refs[count : count + n_out])
        rest = refs[count + n_out :]
        sems, rest = rest[0], rest[1:]
        coming = [Arriving(a) for a in sources]
        used = 0
        for n, i in enumerate(far):
            pieces = [(sources[i], rest[n])]
            if i in parts:
                pieces = [(sources[i].at[p], rest[n].at[p]) for p in chunks(leaves[i].shape[0], parts[i])]
            arrivals = []
            for source, target in pieces:
                copy = pltpu.make_async_copy(source, target, sems.at[used])
                copy.start()
                arrivals.append(Arriving(target, copy))
                used += 1
            coming[i] = arrivals if i in parts else arrivals[0]
        for n, i in enumerate(stored):
            results[i] = Leaving(results[i], sems.at[used])
            used += 1
        kernel(
            *jax.tree.unflatten(tree, coming),
            jax.tree.unflatten(out_tree, results),
            *rest[len(far) :],
        )
        fetch(coming)
        for i in stored:
            results[i].done()

    n_sems = len(far) - len(parts) + len(stored) + sum(len(p) for p in parts.values())
    size = sum(4 * math.prod(a.shape) for a in leaves + out_leaves)
    given = pl.pallas_call(
        body,
        out_shape=[
            pltpu.HBM(a.shape, F32) if i in distant else shaped(*a.shape)
            for i, a in enumerate(out_leaves)
        ],
        in_specs=[
            pl.BlockSpec(
                memory_space=pltpu.HBM if i in far + raw else pltpu.VMEM
            )
            for i in range(count)
        ],
        out_specs=[
            pl.BlockSpec(memory_space=pltpu.HBM if i in distant else pltpu.VMEM)
            for i in range(n_out)
        ],
        scratch_shapes=[pltpu.SemaphoreType.DMA((max(1, n_sems),))]
        + [pltpu.VMEM(leaves[i].shape, leaves[i].dtype) for i in far]
        + list(scratch),
        compiler_params=pltpu.CompilerParams(vmem_limit_bytes=VMEM_LIMIT),
        cost_estimate=pl.CostEstimate(flops=flops, bytes_accessed=size, transcendentals=0),
    )(*leaves)
    return jax.tree.unflatten(out_tree, given)


def chunks(count, parts):
    each = count // PARTS
    return [pl.ds(p * each, each) for p in parts]


def far(tree):
    return jax.tree.map(Far, tree)


def fetch(tree):
    return jax.tree.map(
        lambda one: one.get() if isinstance(one, Arriving) else one,
        tree,
        is_leaf=lambda one: isinstance(one, Arriving),
    )


def loop(first, last, body):
    lax.fori_loop(first, last, body, 0, unroll=UNROLL)


def shaped(*shape):
    return jax.ShapeDtypeStruct(shape, F32)


def face_shapes(shape, sizes, count, width):
    nx, ny, nz = shape
    blocks = count * width + (1 if width == 2 else 0)
    outs = {
        "x": {r: shaped(blocks, ny, nz) for r in rounds_of(sizes[0])},
        "y": {r: shaped(blocks, nx, nz) for r in rounds_of(sizes[1])},
    }
    if width == 2:
        outs["xy"] = {
            (rx, ry): shaped(4 * count + 4, nz)
            for rx in rounds_of(sizes[0])
            for ry in rounds_of(sizes[1])
        }
    return outs


def pack_faces(out, fields, sizes, width, ends=None):
    ix, iy, _ = where_am_i()
    for r, ref in out["x"].items():
        pack_x(ref, fields, r, ix, width, ends)
    for r, ref in out["y"].items():
        pack_y(ref, fields, r, iy, width, ends)
    for (rx, ry), ref in out.get("xy", {}).items():
        pack_xy(ref, fields, rx, ry, ix, iy, ends)


def send_z(tile, sizes):
    return {r: swap(tile, sizes, {2: r}) for r in rounds_of(sizes[2])}


def send_faces(faces, sizes):
    got = {
        "x": {r: swap(v, sizes, {0: r}) for r, v in faces["x"].items()},
        "y": {r: swap(v, sizes, {1: r}) for r, v in faces["y"].items()},
    }
    if "xy" in faces:
        got["xy"] = {(rx, ry): swap(v, sizes, {0: rx, 1: ry}) for (rx, ry), v in faces["xy"].items()}
    return got


def spread(rows):
    return lax.all_to_all(rows, AXES, 0, 0, tiled=True)


def shards(sizes, right_side, conductance, storage, dirichlet, basis, coarse_inverse):
    shape = right_side.shape
    nx, ny, nz = shape
    vecs = basis.shape[0]
    boxed = box_shape(shape)
    devices = sizes[0] * sizes[1] * sizes[2]
    row_shape = shaped(devices, LANES)
    sum_shape = (devices * vecs // LANES, LANES)
    ends_shape = (nx, ny, LANES)
    vbox = pltpu.VMEM(boxed, F32)
    def pack_first(cond, store, fixed, rhs, outs):
        near, free = outs["near"], outs["free"]
        for target, source in zip(near, (cond, store, rhs)):
            target.put(source.get())
        fixed = fixed.get()
        free[...] = 1.0 - fixed[...].astype(F32)
        cond, store, rhs = [one.done() for one in near]
        outs["tile"][...] = pack_z([cond.at[0], cond.at[1], cond.at[2], store, free, rhs])

    first = call(
        pack_first,
        {
            "near": [Stored(*a.shape, near=True) for a in (conductance, storage, right_side)],
            "free": shaped(*shape),
            "tile": shaped(z_rows(6), nx * ny),
        },
        (Raw(conductance), Raw(storage), Far(dirichlet), Raw(right_side)),
    )
    got_z = send_z(first["tile"], sizes)

    def first_rows(rhs, base, out):
        row = project(base, rhs.get()[...])
        out[...] = jnp.broadcast_to(row, out.shape)

    rows = call(first_rows, row_shape, (Far(right_side), Far(basis, range(PARTS))))
    rows_a = spread(rows)

    def pack_all(got_z, near, free, rows, outs, ends):
        cond, store, rhs = fetch(near)
        fields = [cond.at[0], cond.at[1], cond.at[2], store, free.get(), rhs]
        ends[...] = pick_z(fetch(got_z), sizes, ends_shape)
        pack_faces(outs, fields, sizes, 2, ends)

    packed = call(
        pack_all,
        face_shapes(shape, sizes, 6, 2),
        (got_z, first["near"], first["free"], rows),
        [pltpu.VMEM(ends_shape, F32)],
    )
    got = send_faces(packed, sizes)

    def first_smooth(got, cond, store, fixed, rhs, got_z, base, outs, sems, step, *boxes):
        boxes = list(boxes)
        cond, store, rhs = fetch((cond, store, rhs))
        owns = [cond.at[0], cond.at[1], cond.at[2], store, None, rhs]
        copies = []
        for k, own in enumerate(owns):
            if own is not None:
                copies.append(
                    pltpu.make_async_copy(own, own_cells(boxes[k], shape), sems.at[k])
                )
                copies[-1].start()
        for b in boxes[:6]:
            clear_round(b, shape)
        got, fixed = fetch((got, fixed))
        ends = pick_z(fetch(got_z), sizes, ends_shape)
        boxes[4][3 : 3 + nx, 0:ny, 0:nz] = 1.0 - fixed[...].astype(F32)
        unpack_faces(boxes[:6], [None] * 6, got["x"], got["y"], sizes, 2, ends)
        unpack_xy(boxes[:6], shape, got["xy"], sizes)
        for copy in copies:
            copy.wait()
        for target, piece in zip(outs["base"], chunks(vecs, NEAR_FIRST)):
            target.put(base.get().at[piece])
        links, boxes = boxes[6:], boxes[:6]
        coefficients(boxes, links, step, outs["own"])
        outs["kept"]["step"].put(step)
        for kept, link in zip(outs["kept"]["links"], links):
            kept.put(link)
        jacobi(boxes[5], step, links, boxes[0], boxes[1], boxes[5], outs["smooth"])

    smoothed = call(
        first_smooth,
        {
            "smooth": shaped(*shape),
            "own": shaped(7, *shape),
            "base": [Stored(vecs // PARTS, *shape, near=True) for _ in NEAR_FIRST],
            "kept": {
                "links": [Stored(*boxed), Stored(*boxed), Stored(*boxed)],
                "step": Stored(*boxed),
            },
        },
        (
            got,
            Raw(conductance),
            Raw(storage),
            Far(dirichlet),
            Raw(right_side),
            got_z,
            Raw(basis),
        ),
        [pltpu.SemaphoreType.DMA((6,))] + [vbox] * 10,
        flops=SMOOTH_FLOPS,
    )
    kept = smoothed["kept"]
    own = smoothed["own"]

    def base_rest(smoothed, near):
        return smoothed["base"] + [Far(basis, range(len(near), PARTS))]

    def first_direction(smooth, rows, inverse, base, outs):
        smooth, rows = fetch((smooth, rows))
        weights = coarse_weights(inverse.get(), coarse_sum(rows, vecs))
        add_coarse(outs["z"], smooth, base, weights)
        outs["kept"].put(outs["z"])
        pack_faces(outs["faces"], [outs["z"]], sizes, 1)
        outs["tile"][...] = pack_z([outs["z"]])

    directed = call(
        first_direction,
        {
            "z": shaped(*shape),
            "kept": Stored(*shape),
            "faces": face_shapes(shape, sizes, 1, 1),
            "tile": shaped(z_rows(1), nx * ny),
        },
        (smoothed["smooth"], rows_a, Far(coarse_inverse), base_rest(smoothed, NEAR_FIRST)),
    )
    direction, kept_z = directed["z"], directed["kept"]
    got = send_faces(directed["faces"], sizes)
    got_z = send_z(directed["tile"], sizes)

    def apply(field, got, got_z, own, out, vb):
        clear_round(vb, shape)
        field, got, got_z = fetch((field, got, got_z))
        unpack_faces([vb], [field], got["x"], got["y"], sizes, 1)
        vb[3 : 3 + nx, 0:ny, nz : nz + LANES] = halo_lanes(pick_z(got_z, sizes, ends_shape), 0)
        own = own.get()

        def body(x, carry):
            mid = vb[x + 3]
            around = (mid, vb[x + 4], vb[x + 2])
            around += (ahead(mid, 0), behind(mid, 0), ahead(mid, 1), behind(mid, 1))
            total = own[0, x] * mid[0:ny, 0:nz]
            for n in range(1, 7):
                total = total - own[n, x] * around[n][0:ny, 0:nz]
            out[x] = total
            return carry

        loop(0, nx, body)

    def first_image(got, got_z, field, own, rhs, outs, vb):
        image = outs["image"]
        outs["own"].put(own.get())
        apply(field, got, got_z, own, image, vb)
        outs["kept"].put(image)
        outs["tile"][...] = pack_z([image])
        field, rhs = fetch((field, rhs))
        values = [full_sum(rhs[...] * field[...]), full_sum(field[...] * image[...])]
        outs["sums"][...] = put_scalars(jnp.zeros((1, LANES), F32), vecs, values)

    imaged = call(
        first_image,
        {
            "image": shaped(*shape),
            "kept": Stored(*shape),
            "own": Stored(7, *shape),
            "tile": shaped(z_rows(1), nx * ny),
            "sums": shaped(1, LANES),
        },
        (got, got_z, direction, own, Far(right_side)),
        [vbox],
    )
    got_z = send_z(imaged["tile"], sizes)

    def second_rows(base, field, sums, out):
        row = project(base, field.get()[...]) + sums.get()[...]
        out[...] = jnp.broadcast_to(row, out.shape)

    rows = call(second_rows, row_shape, ([basis], imaged["image"], imaged["sums"]))
    rows_c = spread(rows)

    def pack_image(got_z, field, rows, outs, ends):
        ends[...] = pick_z(fetch(got_z), sizes, ends_shape)
        pack_faces(outs, [field.get()], sizes, 2, ends)

    packed = call(
        pack_image,
        face_shapes(shape, sizes, 1, 2),
        (got_z, imaged["image"], rows),
        [pltpu.VMEM(ends_shape, F32)],
    )
    got = send_faces(packed, sizes)

    def second_smooth(got, field, got_z, step, links, base, outs, sem, ga, gb, vb):
        copy = pltpu.make_async_copy(field.get(), own_cells(vb, shape), sem)
        copy.start()
        clear_round(vb, shape)
        got = fetch(got)
        ends = pick_z(fetch(got_z), sizes, ends_shape)
        unpack_faces([vb], [None], got["x"], got["y"], sizes, 2, ends)
        unpack_xy([vb], shape, got["xy"], sizes)
        copy.wait()
        for target, piece in zip(outs["base"], chunks(vecs, NEAR_SECOND)):
            target.put(base.get().at[piece])
        jacobi(vb, step.get(), links, ga, gb, vb, outs["smooth"])

    smoothed = call(
        second_smooth,
        {
            "smooth": shaped(*shape),
            "base": [Stored(vecs // PARTS, *shape, near=True) for _ in NEAR_SECOND],
        },
        (
            got,
            Raw(imaged["kept"]),
            got_z,
            Far(kept["step"]),
            far(kept["links"]),
            Raw(basis),
        ),
        [pltpu.SemaphoreType.DMA] + [vbox] * 3,
        flops=SMOOTH_FLOPS,
    )

    def second_direction(smooth, rows, inverse, field, rhs, before, base, outs):
        smooth, rows = fetch((smooth, rows))
        norm, curve = scalar_sums(rows, vecs, 2)
        alpha = norm / curve
        weights = coarse_weights(inverse.get(), coarse_sum(rows, vecs))
        field, rhs, before = fetch((field, rhs, before))
        outs["residual"][...] = rhs[...] - alpha * field[...]
        add_coarse(outs["z"], smooth, base, weights)
        outs["z"][...] = before[...] - alpha * outs["z"][...]
        pack_faces(outs["faces"], [outs["z"]], sizes, 1)
        outs["tile"][...] = pack_z([outs["z"]])
        outs["scalars"][...] = jnp.concatenate(
            [jnp.broadcast_to(norm, (8, LANES)), jnp.broadcast_to(curve, (8, LANES))], axis=0
        )

    directed = call(
        second_direction,
        {
            "z": shaped(*shape),
            "residual": shaped(*shape),
            "scalars": shaped(16, LANES),
            "faces": face_shapes(shape, sizes, 1, 1),
            "tile": shaped(z_rows(1), nx * ny),
        },
        (
            smoothed["smooth"],
            rows_c,
            Far(coarse_inverse),
            Far(imaged["kept"]),
            Far(right_side),
            Far(kept_z),
            base_rest(smoothed, NEAR_SECOND),
        ),
    )
    precond, residual = directed["z"], directed["residual"]
    got = send_faces(directed["faces"], sizes)
    got_z = send_z(directed["tile"], sizes)
    image, direction = imaged["kept"], kept_z

    def second_image(got, got_z, field, own, image, residual, outs, vb):
        apply(field, got, got_z, own, outs["image"], vb)
        field, image, residual = fetch((field, image, residual))
        values = [
            full_sum(residual[...] * field[...]),
            full_sum(field[...] * outs["image"][...]),
            full_sum(field[...] * image[...]),
        ]
        row = put_scalars(jnp.zeros((1, LANES), F32), 0, values)
        outs["rows"][...] = jnp.broadcast_to(row, outs["rows"].shape)

    last = call(
        second_image,
        {"image": shaped(*shape), "rows": row_shape},
        (
            got,
            got_z,
            precond,
            imaged["own"],
            image,
            residual,
        ),
        [vbox],
    )
    rows_e = spread(last["rows"])

    def finish(rows, scalars, direction, image, precond, precond_image, residual, outs):
        rows, scalars = fetch((rows, scalars))
        norm = scalars[0:1, 0:1]
        curve = scalars[8:9, 0:1]
        norm_next, curve_z, curve_mixed = scalar_sums(rows, 0, 3)
        alpha = norm / curve
        beta = norm_next / norm
        curve_next = curve_z + 2.0 * beta * curve_mixed + beta * beta * curve
        alpha_next = norm_next / curve_next
        direction, image, precond = fetch((direction, image, precond))
        precond_image, residual = fetch((precond_image, residual))
        outs[0][...] = alpha * direction[...] + alpha_next * (
            precond[...] + beta * direction[...]
        )
        outs[1][...] = residual[...] - alpha_next * (precond_image[...] + beta * image[...])

    return tuple(
        call(
            finish,
            [shaped(*shape), shaped(*shape)],
            (rows_e, directed["scalars"], direction, image, precond, last["image"], residual),
        )
    )


def solution(mesh):
    sizes = tuple(mesh.shape[a] for a in AXES)
    placed = (
        P("gx", "gy", "gz"),
        P(None, "gx", "gy", "gz"),
        P("gx", "gy", "gz"),
        P("gx", "gy", "gz"),
        P(None, "gx", "gy", "gz"),
        P(("gx", "gy", "gz"), None),
    )
    return jax.shard_map(
        functools.partial(shards, sizes),
        mesh=mesh,
        in_specs=placed,
        out_specs=(P("gx", "gy", "gz"), P("gx", "gy", "gz")),
        check_vma=False,
    )
```

```python
import functools
import math

import jax
import jax.numpy as jnp
from jax import lax
from jax.experimental import pallas as pl
from jax.experimental.pallas import tpu as pltpu
from jax.sharding import PartitionSpec as P

SWEEPS = 4
RELAX = 2.0 / 3.0
AXES = ("gx", "gy", "gz")
LANES = 128
VMEM_LIMIT = 24 * 1024 * 1024
F32 = jnp.float32
UNROLL = 16
SWEEP_UNROLL = True
PARTS = 8
NEAR_FIRST = range(1)
NEAR_SECOND = range(5)
SMOOTH_FLOPS = 10**9


def rounds_of(count):
    return (0, 1)[: 1 if count <= 2 else 2]


def mate(index, odd, count):
    other = index + 1 if index % 2 == odd else index - 1
    return other if 0 <= other < count else None


def swap(value, sizes, along):
    pairs = []
    nx, ny, nz = sizes
    for ix in range(nx):
        for iy in range(ny):
            for iz in range(nz):
                here = [ix, iy, iz]
                there = [
                    mate(here[a], along[a], sizes[a]) if a in along else here[a] for a in range(3)
                ]
                if None in there:
                    if 2 in along:
                        spare = nz - 1 - iz if iz in (0, nz - 1) else None
                    else:
                        spare = iz ^ 1 if nz % 2 == 0 else None
                    if spare is None:
                        continue
                    there = [ix, iy, spare]
                pairs.append(
                    ((ix * ny + iy) * nz + iz, (there[0] * ny + there[1]) * nz + there[2])
                )
    return lax.ppermute(value, AXES, pairs)


def upward(index, odd):
    return lax.rem(index, 2) == odd


def where_am_i():
    return [lax.axis_index(a) for a in AXES]


def lane_iota(shape):
    return lax.broadcasted_iota(jnp.int32, shape, len(shape) - 1)


def pack_x(out, fields, odd, index, width, ends=None):
    nx, _, nz = fields[0].shape
    count = len(fields) * width
    high = upward(index, odd)
    for cond, first in ((high, nx - width), (jnp.logical_not(high), 0)):

        @pl.when(cond)
        def _(first=first):
            for k, field in enumerate(fields):
                out[k * width : (k + 1) * width] = field[first : first + width]
            if ends is not None:
                for i in range(width):
                    out[count, :, LANES * i : LANES * (i + 1)] = ends[first + i]


def pack_y(out, fields, odd, index, width, ends=None):
    _, ny, nz = fields[0].shape
    count = len(fields) * width
    high = upward(index, odd)
    for cond, first in ((high, ny - width), (jnp.logical_not(high), 0)):

        @pl.when(cond)
        def _(first=first):
            for j in range(width):
                for k, field in enumerate(fields):
                    out[k * width + j] = field[:, first + j, :]
                if ends is not None:
                    out[count, :, LANES * j : LANES * (j + 1)] = ends[:, first + j, :]


def pack_xy(out, fields, rx, ry, ix, iy, ends):
    nx, ny, _ = fields[0].shape
    count = len(fields)
    for xhigh in (False, True):
        for yhigh in (False, True):

            @pl.when((upward(ix, rx) == xhigh) & (upward(iy, ry) == yhigh))
            def _(x0=(nx - 2 if xhigh else 0), y0=(ny - 2 if yhigh else 0)):
                for i in range(2):
                    for k, field in enumerate(fields):
                        out[4 * k + 2 * i : 4 * k + 2 * i + 2, :] = field[x0 + i, y0 : y0 + 2, :]
                    out[4 * count + 2 * i : 4 * count + 2 * i + 2, 0:LANES] = ends[
                        x0 + i, y0 : y0 + 2, :
                    ]


def z_rows(count):
    return (4 * count + 7) // 8 * 8


def pack_z(fields):
    nx, ny, nz = fields[0].shape
    lane = lane_iota((nx, ny, LANES))
    total = jnp.zeros((nx, ny, LANES), F32)
    for k, field in enumerate(fields):
        ends = jnp.where(lane < 64, field[:, :, 0:LANES], field[:, :, nz - LANES : nz])
        turned = pltpu.roll(ends, 4 * k + 2, 2)
        total = jnp.where((lane >= 4 * k) & (lane < 4 * k + 4), turned, total)
    return total.reshape(nx * ny, LANES).T[0 : z_rows(len(fields))]


def project(basis, field):
    nx, ny, nz = field.shape
    rows = []
    for piece in basis:
        vectors = piece.get()
        for k in range(vectors.shape[0]):
            prod = jnp.sum(vectors[k] * field, axis=0)
            part = jnp.zeros((8, LANES), F32)
            for y in range(ny // 8):
                for z in range(nz // LANES):
                    part = part + prod[8 * y : 8 * y + 8, LANES * z : LANES * (z + 1)]
            rows.append(jnp.sum(part, axis=0, keepdims=True))
    vecs = len(rows)
    totals = jnp.sum(jnp.concatenate(rows, axis=0), axis=1, keepdims=True)
    row = lax.broadcasted_iota(jnp.int32, (vecs, LANES), 0)
    return jnp.sum(jnp.where(lane_iota((vecs, LANES)) == row, totals, 0.0), axis=0, keepdims=True)


def put_scalars(row, first, values):
    lane = lane_iota(row.shape)
    for i, value in enumerate(values):
        row = jnp.where(lane == first + i, value, row)
    return row


def box_shape(shape):
    nx, ny, nz = shape
    return (nx + 6, ny + 8, nz + LANES)


def clear(box):
    def body(x, carry):
        box[x] = jnp.zeros(box.shape[1:], F32)
        return carry

    loop(0, box.shape[0], body)


def clear_round(box, shape):
    nx, ny, nz = shape
    planes, rows, lanes = box.shape
    for x in (0, 1, 2, planes - 3, planes - 2, planes - 1):
        box[x] = jnp.zeros((rows, lanes), F32)

    def body(x, carry):
        box[x, ny:rows, :] = jnp.zeros((rows - ny, lanes), F32)
        box[x, 0:ny, nz:lanes] = jnp.zeros((ny, lanes - nz), F32)
        return carry

    loop(3, 3 + nx, body)


def own_cells(box, shape):
    nx, ny, nz = shape
    return box.at[3 : 3 + nx, 0:ny, 0:nz]


def each_round(sizes, a, index, act):
    for r in rounds_of(sizes[a]):
        high = upward(index, r)

        @pl.when(high & (index + 1 < sizes[a]))
        def _(r=r):
            act(r, True)

        @pl.when(jnp.logical_not(high) & (index > 0))
        def _(r=r):
            act(r, False)


def unpack_faces(boxes, owns, xs, ys, sizes, width, ends=None):
    nx, ny, nz = boxes[0].shape[0] - 6, boxes[0].shape[1] - 8, boxes[0].shape[2] - LANES
    count = len(boxes) * width
    ix, iy, _ = where_am_i()
    for k, (box, own) in enumerate(zip(boxes, owns)):
        if own is not None:
            box[3 : 3 + nx, 0:ny, 0:nz] = own[...]
        if ends is not None:
            box[3 : 3 + nx, 0:ny, nz : nz + LANES] = halo_lanes(ends, k)

    def put_x(r, above):
        first = 3 + nx if above else 3 - width
        for k, box in enumerate(boxes):
            box[first : first + width, 0:ny, 0:nz] = xs[r][k * width : (k + 1) * width]
            if ends is not None:
                for i in range(width):
                    tile = xs[r][count, :, LANES * i : LANES * (i + 1)]
                    box[first + i, 0:ny, nz : nz + LANES] = halo_lanes(tile, k)

    each_round(sizes, 0, ix, put_x)

    def put_y(r, above):
        first = ny if above else ny + 8 - width
        for k, box in enumerate(boxes):
            for j in range(width):
                box[3 : 3 + nx, first + j, 0:nz] = ys[r][k * width + j]
                if ends is not None:
                    tile = ys[r][count, :, LANES * j : LANES * (j + 1)]
                    box[3 : 3 + nx, first + j, nz : nz + LANES] = halo_lanes(tile, k)

    each_round(sizes, 1, iy, put_y)


def unpack_xy(boxes, shape, xys, sizes):
    nx, ny, nz = shape
    count = len(boxes)
    ix, iy, _ = where_am_i()

    def put(rx, xabove):
        x0 = 3 + nx if xabove else 1

        def inner(ry, yabove):
            y0 = ny if yabove else ny + 6
            rows = xys[(rx, ry)]
            tile = rows[4 * count : 4 * count + 4, 0:LANES]
            for k, box in enumerate(boxes):
                turned = halo_lanes(tile, k)
                for i in range(2):
                    box[x0 + i, y0 : y0 + 2, 0:nz] = rows[4 * k + 2 * i : 4 * k + 2 * i + 2, :]
                    box[x0 + i, y0 : y0 + 2, nz : nz + LANES] = turned[2 * i : 2 * i + 2]

        each_round(sizes, 1, iy, inner)

    each_round(sizes, 0, ix, put)


def pick_z(zs, sizes, shape):
    count = sizes[2]
    iz = lax.axis_index("gz")
    rows, cells = zs[0].shape
    first = lax.rem(lax.broadcasted_iota(jnp.int32, (rows, cells), 0), 4) < 2
    total = jnp.zeros((rows, cells), F32)
    for r in rounds_of(count):
        high = upward(iz, r)
        below = jnp.logical_not(high) & (iz > 0)
        above = high & (iz + 1 < count)
        total = jnp.where((first & below) | (jnp.logical_not(first) & above), zs[r][...], total)
    filled = jnp.concatenate([total, jnp.zeros((LANES - rows, cells), F32)], axis=0)
    return filled.T.reshape(shape)


def halo_lanes(tile, k):
    lane = lane_iota(tile.shape)
    axis = len(tile.shape) - 1
    turned = pltpu.roll(tile, (-(4 * k + 2)) % LANES, axis)
    return jnp.where((lane < 2) | (lane >= LANES - 2), turned, 0.0)


def ahead(plane, axis):
    return pltpu.roll(plane, plane.shape[axis] - 1, axis)


def behind(plane, axis):
    return pltpu.roll(plane, 1, axis)


def coefficients(fields, links, step, own):
    tx, ty, tz, store, free, _ = fields
    lx, ly, lz = links
    _, nx, ny, nz = own.shape
    last = tx.shape[0] - 1
    for ref in (lx, ly, lz, step):
        ref[0] = jnp.zeros(ref.shape[1:], F32)
        ref[last] = jnp.zeros(ref.shape[1:], F32)

    def body(x, carry, inside):
        f = free[x]
        a, b, c = tx[x], ty[x], tz[x]
        total = store[x] + a + tx[x - 1] + b + behind(b, 0) + c + behind(c, 1)
        d = f * total + (1.0 - f)
        step[x] = RELAX / d
        links_here = (a * f * free[x + 1], b * f * ahead(f, 0), c * f * ahead(f, 1))
        for ref, value in zip(links, links_here):
            ref[x] = value
        if inside:
            x_link, y_link, z_link = links_here
            mine = (
                d,
                x_link,
                lx[x - 1],
                y_link,
                behind(y_link, 0),
                z_link,
                behind(z_link, 1),
            )
            for n, value in enumerate(mine):
                own[n, x - 3] = value[0:ny, 0:nz]
        return carry

    loop(1, 3, functools.partial(body, inside=False))
    loop(3, 3 + nx, functools.partial(body, inside=True))
    loop(3 + nx, last, functools.partial(body, inside=False))


def jacobi(rhs, step, links, ga, gb, source, out):
    planes = rhs.shape[0]
    nx, ny, nz = out.shape
    for g in (ga, gb):
        g[0] = jnp.zeros(g.shape[1:], F32)
        g[planes - 1] = jnp.zeros(g.shape[1:], F32)

    def first(x, carry):
        source[x] = step[x] * rhs[x]
        return carry

    loop(1, planes - 1, first)

    lx, ly, lz = fetch(links)

    def swept(now, x, carry):
        before, mid, x_before = carry
        after, x_here, y, z = now[x + 1], lx[x], ly[x], lz[x]
        total = x_here * after + x_before * before
        total = total + y * ahead(mid, 0) + behind(y * mid, 0)
        total = total + z * ahead(mid, 1) + behind(z * mid, 1)
        value = (1.0 - RELAX) * mid + source[x] + step[x] * total
        return value, (mid, after, x_here)

    def sweep_planes(now, first, last, put):
        def body(x, carry):
            value, carry = swept(now, x, carry)
            put(x, value)
            return carry

        start = (now[first - 1], now[first], lx[first - 1])
        lax.fori_loop(first, last, body, start, unroll=SWEEP_UNROLL)

    now, then, spare = source, ga, gb
    for sweep in range(1, SWEEPS - 1):
        edge = max(1, 3 - (SWEEPS - 1 - sweep))

        def put(x, value, then=then):
            then[x] = value

        sweep_planes(now, edge, planes - edge, put)
        now, then, spare = then, spare, then

    def put_own(x, value):
        out[x - 3] = value[0:ny, 0:nz]

    sweep_planes(now, 3, 3 + nx, put_own)


def coarse_sum(rows_ref, vecs):
    count = rows_ref.shape[0]
    per = LANES // vecs
    lane = lane_iota((count, LANES))
    row = lax.broadcasted_iota(jnp.int32, (count, LANES), 0)
    all_rows = rows_ref[...]
    total = jnp.zeros((count, LANES), F32)
    for m in range(per):
        turned = pltpu.roll(all_rows, vecs * m, 1) if m else all_rows
        keep = (lax.rem(row, per) == m) & (lane >= vecs * m) & (lane < vecs * (m + 1))
        total = jnp.where(keep, turned, total)
    return jnp.sum(total.reshape(count // per, per, LANES), axis=1)


def scalar_sums(rows_ref, first, count):
    total = jnp.sum(rows_ref[...], axis=0, keepdims=True)
    return [total[0:1, first + i : first + i + 1] for i in range(count)]


def coarse_weights(inverse_ref, sums):
    total = jnp.zeros((inverse_ref.shape[0], LANES), F32)
    for g in range(sums.shape[0]):
        total = total + inverse_ref[:, LANES * g : LANES * (g + 1)] * sums[g : g + 1, :]
    return jnp.sum(total, axis=1, keepdims=True)


def add_coarse(out, smooth, basis, weights):
    nx, ny, nz = out.shape
    k = 0
    for piece in jax.tree.leaves(basis):
        vectors = piece.get()
        count = vectors.shape[0]
        scale = [jnp.broadcast_to(weights[k + i : k + i + 1, 0:1], (8, LANES)) for i in range(count)]
        scale = [jnp.tile(s, (ny // 8, nz // LANES)) for s in scale]
        source = smooth if k == 0 else out

        def body(x, carry, vectors=vectors, scale=scale, source=source):
            total = source[x]
            for i, s in enumerate(scale):
                total = total + s * vectors[i, x]
            out[x] = total
            return carry

        loop(0, nx, body)
        k += count


def full_sum(value):
    return jnp.sum(value)


class Arriving:
    def __init__(self, buffer, copy=None):
        self.copy = copy
        self.buffer = buffer

    def get(self):
        if self.copy is not None:
            self.copy.wait()
            self.copy = None
        return self.buffer


class Far:
    def __init__(self, value, parts=None):
        self.value, self.parts = value, parts


class Raw(Far):
    pass


class Stored:
    def __init__(self, *shape, near=False):
        self.shape, self.near = shape, near


class Leaving:
    def __init__(self, target, sem):
        self.target, self.sem, self.copy = target, sem, None

    def put(self, source):
        self.copy = pltpu.make_async_copy(source, self.target, self.sem)
        self.copy.start()

    def done(self):
        if self.copy is not None:
            self.copy.wait()
            self.copy = None
        return self.target


def call(kernel, outs, args, scratch=(), flops=0):
    leaves, tree = jax.tree.flatten(list(args), is_leaf=lambda one: isinstance(one, Far))
    out_leaves, out_tree = jax.tree.flatten(outs, is_leaf=lambda one: isinstance(one, Stored))
    count, n_out = len(leaves), len(out_leaves)
    raw = [i for i, a in enumerate(leaves) if isinstance(a, Raw)]
    far = [i for i, a in enumerate(leaves) if isinstance(a, Far) and i not in raw]
    distant = [i for i, a in enumerate(out_leaves) if isinstance(a, Stored) and not a.near]
    stored = [i for i, a in enumerate(out_leaves) if isinstance(a, Stored)]
    parts = {i: leaves[i].parts for i in far if leaves[i].parts is not None}
    leaves = [
        pltpu.with_memory_space_constraint(a.value, pltpu.HBM) if isinstance(a, Far) else a
        for a in leaves
    ]

    def body(*refs):
        sources, results = refs[:count], list(refs[count : count + n_out])
        rest = refs[count + n_out :]
        sems, rest = rest[0], rest[1:]
        coming = [Arriving(a) for a in sources]
        used = 0
        for n, i in enumerate(far):
            pieces = [(sources[i], rest[n])]
            if i in parts:
                pieces = [(sources[i].at[p], rest[n].at[p]) for p in chunks(leaves[i].shape[0], parts[i])]
            arrivals = []
            for source, target in pieces:
                copy = pltpu.make_async_copy(source, target, sems.at[used])
                copy.start()
                arrivals.append(Arriving(target, copy))
                used += 1
            coming[i] = arrivals if i in parts else arrivals[0]
        for n, i in enumerate(stored):
            results[i] = Leaving(results[i], sems.at[used])
            used += 1
        kernel(
            *jax.tree.unflatten(tree, coming),
            jax.tree.unflatten(out_tree, results),
            *rest[len(far) :],
        )
        fetch(coming)
        for i in stored:
            results[i].done()

    n_sems = len(far) - len(parts) + len(stored) + sum(len(p) for p in parts.values())
    size = sum(4 * math.prod(a.shape) for a in leaves + out_leaves)
    given = pl.pallas_call(
        body,
        out_shape=[
            pltpu.HBM(a.shape, F32) if i in distant else shaped(*a.shape)
            for i, a in enumerate(out_leaves)
        ],
        in_specs=[
            pl.BlockSpec(
                memory_space=pltpu.HBM if i in far + raw else pltpu.VMEM
            )
            for i in range(count)
        ],
        out_specs=[
            pl.BlockSpec(memory_space=pltpu.HBM if i in distant else pltpu.VMEM)
            for i in range(n_out)
        ],
        scratch_shapes=[pltpu.SemaphoreType.DMA((max(1, n_sems),))]
        + [pltpu.VMEM(leaves[i].shape, leaves[i].dtype) for i in far]
        + list(scratch),
        compiler_params=pltpu.CompilerParams(vmem_limit_bytes=VMEM_LIMIT),
        cost_estimate=pl.CostEstimate(flops=flops, bytes_accessed=size, transcendentals=0),
    )(*leaves)
    return jax.tree.unflatten(out_tree, given)


def chunks(count, parts):
    each = count // PARTS
    return [pl.ds(p * each, each) for p in parts]


def far(tree):
    return jax.tree.map(Far, tree)


def fetch(tree):
    return jax.tree.map(
        lambda one: one.get() if isinstance(one, Arriving) else one,
        tree,
        is_leaf=lambda one: isinstance(one, Arriving),
    )


def loop(first, last, body):
    lax.fori_loop(first, last, body, 0, unroll=UNROLL)


def shaped(*shape):
    return jax.ShapeDtypeStruct(shape, F32)


def face_shapes(shape, sizes, count, width):
    nx, ny, nz = shape
    blocks = count * width + (1 if width == 2 else 0)
    outs = {
        "x": {r: shaped(blocks, ny, nz) for r in rounds_of(sizes[0])},
        "y": {r: shaped(blocks, nx, nz) for r in rounds_of(sizes[1])},
    }
    if width == 2:
        outs["xy"] = {
            (rx, ry): shaped(4 * count + 4, nz)
            for rx in rounds_of(sizes[0])
            for ry in rounds_of(sizes[1])
        }
    return outs


def pack_faces(out, fields, sizes, width, ends=None):
    ix, iy, _ = where_am_i()
    for r, ref in out["x"].items():
        pack_x(ref, fields, r, ix, width, ends)
    for r, ref in out["y"].items():
        pack_y(ref, fields, r, iy, width, ends)
    for (rx, ry), ref in out.get("xy", {}).items():
        pack_xy(ref, fields, rx, ry, ix, iy, ends)


def send_z(tile, sizes):
    return {r: swap(tile, sizes, {2: r}) for r in rounds_of(sizes[2])}


def send_faces(faces, sizes):
    got = {
        "x": {r: swap(v, sizes, {0: r}) for r, v in faces["x"].items()},
        "y": {r: swap(v, sizes, {1: r}) for r, v in faces["y"].items()},
    }
    if "xy" in faces:
        got["xy"] = {(rx, ry): swap(v, sizes, {0: rx, 1: ry}) for (rx, ry), v in faces["xy"].items()}
    return got


def spread(rows):
    return lax.all_to_all(rows, AXES, 0, 0, tiled=True)


def shards(sizes, right_side, conductance, storage, dirichlet, basis, coarse_inverse):
    shape = right_side.shape
    nx, ny, nz = shape
    vecs = basis.shape[0]
    boxed = box_shape(shape)
    devices = sizes[0] * sizes[1] * sizes[2]
    row_shape = shaped(devices, LANES)
    sum_shape = (devices * vecs // LANES, LANES)
    ends_shape = (nx, ny, LANES)
    vbox = pltpu.VMEM(boxed, F32)
    def pack_first(cond, store, fixed, rhs, outs):
        near, free = outs["near"], outs["free"]
        for target, source in zip(near, (cond, store, rhs)):
            target.put(source.get())
        fixed = fixed.get()
        free[...] = 1.0 - fixed[...].astype(F32)
        cond, store, rhs = [one.done() for one in near]
        outs["tile"][...] = pack_z([cond.at[0], cond.at[1], cond.at[2], store, free, rhs])

    first = call(
        pack_first,
        {
            "near": [Stored(*a.shape, near=True) for a in (conductance, storage, right_side)],
            "free": shaped(*shape),
            "tile": shaped(z_rows(6), nx * ny),
        },
        (Raw(conductance), Raw(storage), Far(dirichlet), Raw(right_side)),
    )
    got_z = send_z(first["tile"], sizes)

    def first_rows(rhs, base, out):
        row = project(base, rhs.get()[...])
        out[...] = jnp.broadcast_to(row, out.shape)

    rows = call(first_rows, row_shape, (Far(right_side), Far(basis, range(PARTS))))
    rows_a = spread(rows)

    def pack_all(got_z, near, free, rows, outs, ends):
        cond, store, rhs = fetch(near)
        fields = [cond.at[0], cond.at[1], cond.at[2], store, free.get(), rhs]
        ends[...] = pick_z(fetch(got_z), sizes, ends_shape)
        pack_faces(outs, fields, sizes, 2, ends)

    packed = call(
        pack_all,
        face_shapes(shape, sizes, 6, 2),
        (got_z, first["near"], first["free"], rows),
        [pltpu.VMEM(ends_shape, F32)],
    )
    got = send_faces(packed, sizes)

    def first_smooth(got, cond, store, fixed, rhs, got_z, base, outs, sems, step, *boxes):
        boxes = list(boxes)
        cond, store, rhs = fetch((cond, store, rhs))
        owns = [cond.at[0], cond.at[1], cond.at[2], store, None, rhs]
        copies = []
        for k, own in enumerate(owns):
            if own is not None:
                copies.append(
                    pltpu.make_async_copy(own, own_cells(boxes[k], shape), sems.at[k])
                )
                copies[-1].start()
        for b in boxes[:6]:
            clear_round(b, shape)
        got = fetch(got)
        ends = pick_z(fetch(got_z), sizes, ends_shape)
        unpack_faces(boxes[:6], [None] * 6, got["x"], got["y"], sizes, 2, ends)
        unpack_xy(boxes[:6], shape, got["xy"], sizes)
        boxes[4][3 : 3 + nx, 0:ny, 0:nz] = 1.0 - fixed.get()[...].astype(F32)
        for copy in copies:
            copy.wait()
        for target, piece in zip(outs["base"], chunks(vecs, NEAR_FIRST)):
            target.put(base.get().at[piece])
        links, boxes = boxes[6:], boxes[:6]
        coefficients(boxes, links, step, outs["own"])
        outs["kept"]["step"].put(step)
        for kept, link in zip(outs["kept"]["links"], links):
            kept.put(link)
        jacobi(boxes[5], step, links, boxes[0], boxes[1], boxes[5], outs["smooth"])

    smoothed = call(
        first_smooth,
        {
            "smooth": shaped(*shape),
            "own": shaped(7, *shape),
            "base": [Stored(vecs // PARTS, *shape, near=True) for _ in NEAR_FIRST],
            "kept": {
                "links": [Stored(*boxed), Stored(*boxed), Stored(*boxed)],
                "step": Stored(*boxed),
            },
        },
        (
            got,
            Raw(conductance),
            Raw(storage),
            Far(dirichlet),
            Raw(right_side),
            got_z,
            Raw(basis),
        ),
        [pltpu.SemaphoreType.DMA((6,))] + [vbox] * 10,
        flops=SMOOTH_FLOPS,
    )
    kept = smoothed["kept"]
    own = smoothed["own"]

    def base_rest(smoothed, near):
        return smoothed["base"] + [Far(basis, range(len(near), PARTS))]

    def first_direction(smooth, rows, inverse, base, outs):
        smooth, rows = fetch((smooth, rows))
        weights = coarse_weights(inverse.get(), coarse_sum(rows, vecs))
        add_coarse(outs["z"], smooth, base, weights)
        pack_faces(outs["faces"], [outs["z"]], sizes, 1)
        outs["tile"][...] = pack_z([outs["z"]])

    directed = call(
        first_direction,
        {
            "z": shaped(*shape),
            "faces": face_shapes(shape, sizes, 1, 1),
            "tile": shaped(z_rows(1), nx * ny),
        },
        (smoothed["smooth"], rows_a, Far(coarse_inverse), base_rest(smoothed, NEAR_FIRST)),
    )
    direction = directed["z"]
    got = send_faces(directed["faces"], sizes)
    got_z = send_z(directed["tile"], sizes)

    def apply(field, got, got_z, own, out, vb):
        clear_round(vb, shape)
        field, got, got_z = fetch((field, got, got_z))
        unpack_faces([vb], [field], got["x"], got["y"], sizes, 1)
        vb[3 : 3 + nx, 0:ny, nz : nz + LANES] = halo_lanes(pick_z(got_z, sizes, ends_shape), 0)
        own = own.get()

        def body(x, carry):
            mid = vb[x + 3]
            around = (mid, vb[x + 4], vb[x + 2])
            around += (ahead(mid, 0), behind(mid, 0), ahead(mid, 1), behind(mid, 1))
            total = own[0, x] * mid[0:ny, 0:nz]
            for n in range(1, 7):
                total = total - own[n, x] * around[n][0:ny, 0:nz]
            out[x] = total
            return carry

        loop(0, nx, body)

    def first_image(got, got_z, field, own, rhs, outs, vb):
        image = outs["image"]
        outs["own"].put(own.get())
        outs["z"].put(field.get())
        apply(field, got, got_z, own, image, vb)
        outs["kept"].put(image)
        outs["tile"][...] = pack_z([image])
        field, rhs = fetch((field, rhs))
        values = [full_sum(rhs[...] * field[...]), full_sum(field[...] * image[...])]
        outs["sums"][...] = put_scalars(jnp.zeros((1, LANES), F32), vecs, values)

    imaged = call(
        first_image,
        {
            "image": shaped(*shape),
            "kept": Stored(*shape),
            "own": Stored(7, *shape),
            "z": Stored(*shape),
            "tile": shaped(z_rows(1), nx * ny),
            "sums": shaped(1, LANES),
        },
        (got, got_z, direction, own, Far(right_side)),
        [vbox],
    )
    got_z = send_z(imaged["tile"], sizes)
    kept_z = imaged["z"]

    def second_rows(base, field, sums, out):
        row = project(base, field.get()[...]) + sums.get()[...]
        out[...] = jnp.broadcast_to(row, out.shape)

    rows = call(second_rows, row_shape, ([basis], imaged["image"], imaged["sums"]))
    rows_c = spread(rows)

    def pack_image(got_z, field, rows, outs, ends):
        ends[...] = pick_z(fetch(got_z), sizes, ends_shape)
        pack_faces(outs, [field.get()], sizes, 2, ends)

    packed = call(
        pack_image,
        face_shapes(shape, sizes, 1, 2),
        (got_z, imaged["image"], rows),
        [pltpu.VMEM(ends_shape, F32)],
    )
    got = send_faces(packed, sizes)

    def second_smooth(got, field, got_z, step, links, base, outs, sem, ga, gb, vb):
        copy = pltpu.make_async_copy(field.get(), own_cells(vb, shape), sem)
        copy.start()
        clear_round(vb, shape)
        got = fetch(got)
        ends = pick_z(fetch(got_z), sizes, ends_shape)
        unpack_faces([vb], [None], got["x"], got["y"], sizes, 2, ends)
        unpack_xy([vb], shape, got["xy"], sizes)
        copy.wait()
        for target, piece in zip(outs["base"], chunks(vecs, NEAR_SECOND)):
            target.put(base.get().at[piece])
        jacobi(vb, step.get(), links, ga, gb, vb, outs["smooth"])

    smoothed = call(
        second_smooth,
        {
            "smooth": shaped(*shape),
            "base": [Stored(vecs // PARTS, *shape, near=True) for _ in NEAR_SECOND],
        },
        (
            got,
            Raw(imaged["kept"]),
            got_z,
            Far(kept["step"]),
            far(kept["links"]),
            Raw(basis),
        ),
        [pltpu.SemaphoreType.DMA] + [vbox] * 3,
        flops=SMOOTH_FLOPS,
    )

    def second_direction(smooth, rows, inverse, field, rhs, before, base, outs):
        smooth, rows = fetch((smooth, rows))
        norm, curve = scalar_sums(rows, vecs, 2)
        alpha = norm / curve
        weights = coarse_weights(inverse.get(), coarse_sum(rows, vecs))
        field, rhs, before = fetch((field, rhs, before))
        outs["residual"][...] = rhs[...] - alpha * field[...]
        add_coarse(outs["z"], smooth, base, weights)
        outs["z"][...] = before[...] - alpha * outs["z"][...]
        pack_faces(outs["faces"], [outs["z"]], sizes, 1)
        outs["tile"][...] = pack_z([outs["z"]])
        outs["scalars"][...] = jnp.concatenate(
            [jnp.broadcast_to(norm, (8, LANES)), jnp.broadcast_to(curve, (8, LANES))], axis=0
        )

    directed = call(
        second_direction,
        {
            "z": shaped(*shape),
            "residual": shaped(*shape),
            "scalars": shaped(16, LANES),
            "faces": face_shapes(shape, sizes, 1, 1),
            "tile": shaped(z_rows(1), nx * ny),
        },
        (
            smoothed["smooth"],
            rows_c,
            Far(coarse_inverse),
            Far(imaged["kept"]),
            Far(right_side),
            Far(kept_z),
            base_rest(smoothed, NEAR_SECOND),
        ),
    )
    precond, residual = directed["z"], directed["residual"]
    got = send_faces(directed["faces"], sizes)
    got_z = send_z(directed["tile"], sizes)
    image, direction = imaged["kept"], kept_z

    def second_image(got, got_z, field, own, image, residual, outs, vb):
        apply(field, got, got_z, own, outs["image"], vb)
        field, image, residual = fetch((field, image, residual))
        values = [
            full_sum(residual[...] * field[...]),
            full_sum(field[...] * outs["image"][...]),
            full_sum(field[...] * image[...]),
        ]
        row = put_scalars(jnp.zeros((1, LANES), F32), 0, values)
        outs["rows"][...] = jnp.broadcast_to(row, outs["rows"].shape)

    last = call(
        second_image,
        {"image": shaped(*shape), "rows": row_shape},
        (
            got,
            got_z,
            precond,
            imaged["own"],
            image,
            residual,
        ),
        [vbox],
    )
    rows_e = spread(last["rows"])

    def finish(rows, scalars, direction, image, precond, precond_image, residual, outs):
        rows, scalars = fetch((rows, scalars))
        norm = scalars[0:1, 0:1]
        curve = scalars[8:9, 0:1]
        norm_next, curve_z, curve_mixed = scalar_sums(rows, 0, 3)
        alpha = norm / curve
        beta = norm_next / norm
        curve_next = curve_z + 2.0 * beta * curve_mixed + beta * beta * curve
        alpha_next = norm_next / curve_next
        direction, image, precond = fetch((direction, image, precond))
        precond_image, residual = fetch((precond_image, residual))
        outs[0][...] = alpha * direction[...] + alpha_next * (
            precond[...] + beta * direction[...]
        )
        outs[1][...] = residual[...] - alpha_next * (precond_image[...] + beta * image[...])

    return tuple(
        call(
            finish,
            [shaped(*shape), shaped(*shape)],
            (rows_e, directed["scalars"], direction, image, precond, last["image"], residual),
        )
    )


def solution(mesh):
    sizes = tuple(mesh.shape[a] for a in AXES)
    placed = (
        P("gx", "gy", "gz"),
        P(None, "gx", "gy", "gz"),
        P("gx", "gy", "gz"),
        P("gx", "gy", "gz"),
        P(None, "gx", "gy", "gz"),
        P(("gx", "gy", "gz"), None),
    )
    return jax.shard_map(
        functools.partial(shards, sizes),
        mesh=mesh,
        in_specs=placed,
        out_specs=(P("gx", "gy", "gz"), P("gx", "gy", "gz")),
        check_vma=False,
    )
```

```python
import functools
import math

import jax
import jax.numpy as jnp
from jax import lax
from jax.experimental import pallas as pl
from jax.experimental.pallas import tpu as pltpu
from jax.sharding import PartitionSpec as P

SWEEPS = 4
RELAX = 2.0 / 3.0
AXES = ("gx", "gy", "gz")
LANES = 128
VMEM_LIMIT = 24 * 1024 * 1024
F32 = jnp.float32
UNROLL = 16
SWEEP_UNROLL = True
PARTS = 8
NEAR_FIRST = range(1)
NEAR_SECOND = range(5)
SMOOTH_FLOPS = 10**9


def rounds_of(count):
    return (0, 1)[: 1 if count <= 2 else 2]


def mate(index, odd, count):
    other = index + 1 if index % 2 == odd else index - 1
    return other if 0 <= other < count else None


def swap(value, sizes, along):
    pairs = []
    nx, ny, nz = sizes
    for ix in range(nx):
        for iy in range(ny):
            for iz in range(nz):
                here = [ix, iy, iz]
                there = [
                    mate(here[a], along[a], sizes[a]) if a in along else here[a] for a in range(3)
                ]
                if None in there:
                    if 2 in along:
                        spare = nz - 1 - iz if iz in (0, nz - 1) else None
                    else:
                        spare = iz ^ 1 if nz % 2 == 0 else None
                    if spare is None:
                        continue
                    there = [ix, iy, spare]
                pairs.append(
                    ((ix * ny + iy) * nz + iz, (there[0] * ny + there[1]) * nz + there[2])
                )
    return lax.ppermute(value, AXES, pairs)


def upward(index, odd):
    return lax.rem(index, 2) == odd


def where_am_i():
    return [lax.axis_index(a) for a in AXES]


def lane_iota(shape):
    return lax.broadcasted_iota(jnp.int32, shape, len(shape) - 1)


def pack_x(out, fields, odd, index, width, ends=None):
    nx, _, nz = fields[0].shape
    count = len(fields) * width
    high = upward(index, odd)
    for cond, first in ((high, nx - width), (jnp.logical_not(high), 0)):

        @pl.when(cond)
        def _(first=first):
            for k, field in enumerate(fields):
                out[k * width : (k + 1) * width] = field[first : first + width]
            if ends is not None:
                for i in range(width):
                    out[count, :, LANES * i : LANES * (i + 1)] = ends[first + i]


def pack_y(out, fields, odd, index, width, ends=None):
    _, ny, nz = fields[0].shape
    count = len(fields) * width
    high = upward(index, odd)
    for cond, first in ((high, ny - width), (jnp.logical_not(high), 0)):

        @pl.when(cond)
        def _(first=first):
            for j in range(width):
                for k, field in enumerate(fields):
                    out[k * width + j] = field[:, first + j, :]
                if ends is not None:
                    out[count, :, LANES * j : LANES * (j + 1)] = ends[:, first + j, :]


def pack_xy(out, fields, rx, ry, ix, iy, ends):
    nx, ny, _ = fields[0].shape
    count = len(fields)
    for xhigh in (False, True):
        for yhigh in (False, True):

            @pl.when((upward(ix, rx) == xhigh) & (upward(iy, ry) == yhigh))
            def _(x0=(nx - 2 if xhigh else 0), y0=(ny - 2 if yhigh else 0)):
                for i in range(2):
                    for k, field in enumerate(fields):
                        out[4 * k + 2 * i : 4 * k + 2 * i + 2, :] = field[x0 + i, y0 : y0 + 2, :]
                    out[4 * count + 2 * i : 4 * count + 2 * i + 2, 0:LANES] = ends[
                        x0 + i, y0 : y0 + 2, :
                    ]


def z_rows(count):
    return (4 * count + 7) // 8 * 8


def pack_z(fields):
    nx, ny, nz = fields[0].shape
    lane = lane_iota((nx, ny, LANES))
    total = jnp.zeros((nx, ny, LANES), F32)
    for k, field in enumerate(fields):
        ends = jnp.where(lane < 64, field[:, :, 0:LANES], field[:, :, nz - LANES : nz])
        turned = pltpu.roll(ends, 4 * k + 2, 2)
        total = jnp.where((lane >= 4 * k) & (lane < 4 * k + 4), turned, total)
    return total.reshape(nx * ny, LANES).T[0 : z_rows(len(fields))]


def project(basis, field):
    nx, ny, nz = field.shape
    rows = []
    for piece in basis:
        vectors = piece.get()
        for k in range(vectors.shape[0]):
            prod = jnp.sum(vectors[k] * field, axis=0)
            part = jnp.zeros((8, LANES), F32)
            for y in range(ny // 8):
                for z in range(nz // LANES):
                    part = part + prod[8 * y : 8 * y + 8, LANES * z : LANES * (z + 1)]
            rows.append(jnp.sum(part, axis=0, keepdims=True))
    vecs = len(rows)
    totals = jnp.sum(jnp.concatenate(rows, axis=0), axis=1, keepdims=True)
    row = lax.broadcasted_iota(jnp.int32, (vecs, LANES), 0)
    return jnp.sum(jnp.where(lane_iota((vecs, LANES)) == row, totals, 0.0), axis=0, keepdims=True)


def put_scalars(row, first, values):
    lane = lane_iota(row.shape)
    for i, value in enumerate(values):
        row = jnp.where(lane == first + i, value, row)
    return row


def box_shape(shape):
    nx, ny, nz = shape
    return (nx + 6, ny + 8, nz + LANES)


def clear(box):
    def body(x, carry):
        box[x] = jnp.zeros(box.shape[1:], F32)
        return carry

    loop(0, box.shape[0], body)


def clear_round(box, shape):
    nx, ny, nz = shape
    planes, rows, lanes = box.shape
    for x in (0, 1, 2, planes - 3, planes - 2, planes - 1):
        box[x] = jnp.zeros((rows, lanes), F32)

    def body(x, carry):
        box[x, ny:rows, :] = jnp.zeros((rows - ny, lanes), F32)
        box[x, 0:ny, nz:lanes] = jnp.zeros((ny, lanes - nz), F32)
        return carry

    loop(3, 3 + nx, body)


def own_cells(box, shape):
    nx, ny, nz = shape
    return box.at[3 : 3 + nx, 0:ny, 0:nz]


def each_round(sizes, a, index, act):
    for r in rounds_of(sizes[a]):
        high = upward(index, r)

        @pl.when(high & (index + 1 < sizes[a]))
        def _(r=r):
            act(r, True)

        @pl.when(jnp.logical_not(high) & (index > 0))
        def _(r=r):
            act(r, False)


def unpack_faces(boxes, owns, xs, ys, sizes, width, ends=None):
    nx, ny, nz = boxes[0].shape[0] - 6, boxes[0].shape[1] - 8, boxes[0].shape[2] - LANES
    count = len(boxes) * width
    ix, iy, _ = where_am_i()
    for k, (box, own) in enumerate(zip(boxes, owns)):
        if own is not None:
            box[3 : 3 + nx, 0:ny, 0:nz] = own[...]
        if ends is not None:
            box[3 : 3 + nx, 0:ny, nz : nz + LANES] = halo_lanes(ends, k)

    def put_x(r, above):
        first = 3 + nx if above else 3 - width
        for k, box in enumerate(boxes):
            box[first : first + width, 0:ny, 0:nz] = xs[r][k * width : (k + 1) * width]
            if ends is not None:
                for i in range(width):
                    tile = xs[r][count, :, LANES * i : LANES * (i + 1)]
                    box[first + i, 0:ny, nz : nz + LANES] = halo_lanes(tile, k)

    each_round(sizes, 0, ix, put_x)

    def put_y(r, above):
        first = ny if above else ny + 8 - width
        for k, box in enumerate(boxes):
            for j in range(width):
                box[3 : 3 + nx, first + j, 0:nz] = ys[r][k * width + j]
                if ends is not None:
                    tile = ys[r][count, :, LANES * j : LANES * (j + 1)]
                    box[3 : 3 + nx, first + j, nz : nz + LANES] = halo_lanes(tile, k)

    each_round(sizes, 1, iy, put_y)


def unpack_xy(boxes, shape, xys, sizes):
    nx, ny, nz = shape
    count = len(boxes)
    ix, iy, _ = where_am_i()

    def put(rx, xabove):
        x0 = 3 + nx if xabove else 1

        def inner(ry, yabove):
            y0 = ny if yabove else ny + 6
            rows = xys[(rx, ry)]
            tile = rows[4 * count : 4 * count + 4, 0:LANES]
            for k, box in enumerate(boxes):
                turned = halo_lanes(tile, k)
                for i in range(2):
                    box[x0 + i, y0 : y0 + 2, 0:nz] = rows[4 * k + 2 * i : 4 * k + 2 * i + 2, :]
                    box[x0 + i, y0 : y0 + 2, nz : nz + LANES] = turned[2 * i : 2 * i + 2]

        each_round(sizes, 1, iy, inner)

    each_round(sizes, 0, ix, put)


def pick_z(zs, sizes, shape):
    count = sizes[2]
    iz = lax.axis_index("gz")
    rows, cells = zs[0].shape
    first = lax.rem(lax.broadcasted_iota(jnp.int32, (rows, cells), 0), 4) < 2
    total = jnp.zeros((rows, cells), F32)
    for r in rounds_of(count):
        high = upward(iz, r)
        below = jnp.logical_not(high) & (iz > 0)
        above = high & (iz + 1 < count)
        total = jnp.where((first & below) | (jnp.logical_not(first) & above), zs[r][...], total)
    filled = jnp.concatenate([total, jnp.zeros((LANES - rows, cells), F32)], axis=0)
    return filled.T.reshape(shape)


def halo_lanes(tile, k):
    lane = lane_iota(tile.shape)
    axis = len(tile.shape) - 1
    turned = pltpu.roll(tile, (-(4 * k + 2)) % LANES, axis)
    return jnp.where((lane < 2) | (lane >= LANES - 2), turned, 0.0)


def ahead(plane, axis):
    return pltpu.roll(plane, plane.shape[axis] - 1, axis)


def behind(plane, axis):
    return pltpu.roll(plane, 1, axis)


def coefficients(fields, links, step, own):
    tx, ty, tz, store, free, _ = fields
    lx, ly, lz = links
    _, nx, ny, nz = own.shape
    last = tx.shape[0] - 1
    for ref in (lx, ly, lz, step):
        ref[0] = jnp.zeros(ref.shape[1:], F32)
        ref[last] = jnp.zeros(ref.shape[1:], F32)

    def body(x, carry, inside):
        f = free[x]
        a, b, c = tx[x], ty[x], tz[x]
        total = store[x] + a + tx[x - 1] + b + behind(b, 0) + c + behind(c, 1)
        d = f * total + (1.0 - f)
        step[x] = RELAX / d
        links_here = (a * f * free[x + 1], b * f * ahead(f, 0), c * f * ahead(f, 1))
        for ref, value in zip(links, links_here):
            ref[x] = value
        if inside:
            x_link, y_link, z_link = links_here
            mine = (
                d,
                x_link,
                lx[x - 1],
                y_link,
                behind(y_link, 0),
                z_link,
                behind(z_link, 1),
            )
            for n, value in enumerate(mine):
                own[n, x - 3] = value[0:ny, 0:nz]
        return carry

    loop(1, 3, functools.partial(body, inside=False))
    loop(3, 3 + nx, functools.partial(body, inside=True))
    loop(3 + nx, last, functools.partial(body, inside=False))


def jacobi(rhs, step, links, ga, gb, source, out):
    planes = rhs.shape[0]
    nx, ny, nz = out.shape
    for g in (ga, gb):
        g[0] = jnp.zeros(g.shape[1:], F32)
        g[planes - 1] = jnp.zeros(g.shape[1:], F32)

    def first(x, carry):
        source[x] = step[x] * rhs[x]
        return carry

    loop(1, planes - 1, first)

    lx, ly, lz = fetch(links)

    def swept(now, x, carry):
        before, mid, x_before = carry
        after, x_here, y, z = now[x + 1], lx[x], ly[x], lz[x]
        total = x_here * after + x_before * before
        total = total + y * ahead(mid, 0) + behind(y * mid, 0)
        total = total + z * ahead(mid, 1) + behind(z * mid, 1)
        value = (1.0 - RELAX) * mid + source[x] + step[x] * total
        return value, (mid, after, x_here)

    def sweep_planes(now, first, last, put):
        def body(x, carry):
            value, carry = swept(now, x, carry)
            put(x, value)
            return carry

        start = (now[first - 1], now[first], lx[first - 1])
        lax.fori_loop(first, last, body, start, unroll=SWEEP_UNROLL)

    now, then, spare = source, ga, gb
    for sweep in range(1, SWEEPS - 1):
        edge = max(1, 3 - (SWEEPS - 1 - sweep))

        def put(x, value, then=then):
            then[x] = value

        sweep_planes(now, edge, planes - edge, put)
        now, then, spare = then, spare, then

    def put_own(x, value):
        out[x - 3] = value[0:ny, 0:nz]

    sweep_planes(now, 3, 3 + nx, put_own)


def coarse_sum(rows_ref, vecs):
    count = rows_ref.shape[0]
    per = LANES // vecs
    lane = lane_iota((count, LANES))
    row = lax.broadcasted_iota(jnp.int32, (count, LANES), 0)
    all_rows = rows_ref[...]
    total = jnp.zeros((count, LANES), F32)
    for m in range(per):
        turned = pltpu.roll(all_rows, vecs * m, 1) if m else all_rows
        keep = (lax.rem(row, per) == m) & (lane >= vecs * m) & (lane < vecs * (m + 1))
        total = jnp.where(keep, turned, total)
    return jnp.sum(total.reshape(count // per, per, LANES), axis=1)


def scalar_sums(rows_ref, first, count):
    total = jnp.sum(rows_ref[...], axis=0, keepdims=True)
    return [total[0:1, first + i : first + i + 1] for i in range(count)]


def coarse_weights(inverse_ref, sums):
    total = jnp.zeros((inverse_ref.shape[0], LANES), F32)
    for g in range(sums.shape[0]):
        total = total + inverse_ref[:, LANES * g : LANES * (g + 1)] * sums[g : g + 1, :]
    return jnp.sum(total, axis=1, keepdims=True)


def add_coarse(out, smooth, basis, weights):
    nx, ny, nz = out.shape
    k = 0
    for piece in jax.tree.leaves(basis):
        vectors = piece.get()
        count = vectors.shape[0]
        scale = [jnp.broadcast_to(weights[k + i : k + i + 1, 0:1], (8, LANES)) for i in range(count)]
        scale = [jnp.tile(s, (ny // 8, nz // LANES)) for s in scale]
        source = smooth if k == 0 else out

        def body(x, carry, vectors=vectors, scale=scale, source=source):
            total = source[x]
            for i, s in enumerate(scale):
                total = total + s * vectors[i, x]
            out[x] = total
            return carry

        loop(0, nx, body)
        k += count


def full_sum(value):
    return jnp.sum(value)


class Arriving:
    def __init__(self, buffer, copy=None):
        self.copy = copy
        self.buffer = buffer

    def get(self):
        if self.copy is not None:
            self.copy.wait()
            self.copy = None
        return self.buffer


class Far:
    def __init__(self, value, parts=None):
        self.value, self.parts = value, parts


class Raw(Far):
    pass


class Stored:
    def __init__(self, *shape, near=False):
        self.shape, self.near = shape, near


class Leaving:
    def __init__(self, target, sem):
        self.target, self.sem, self.copy = target, sem, None

    def put(self, source):
        self.copy = pltpu.make_async_copy(source, self.target, self.sem)
        self.copy.start()

    def done(self):
        if self.copy is not None:
            self.copy.wait()
            self.copy = None
        return self.target


def call(kernel, outs, args, scratch=(), flops=0):
    leaves, tree = jax.tree.flatten(list(args), is_leaf=lambda one: isinstance(one, Far))
    out_leaves, out_tree = jax.tree.flatten(outs, is_leaf=lambda one: isinstance(one, Stored))
    count, n_out = len(leaves), len(out_leaves)
    raw = [i for i, a in enumerate(leaves) if isinstance(a, Raw)]
    far = [i for i, a in enumerate(leaves) if isinstance(a, Far) and i not in raw]
    distant = [i for i, a in enumerate(out_leaves) if isinstance(a, Stored) and not a.near]
    stored = [i for i, a in enumerate(out_leaves) if isinstance(a, Stored)]
    parts = {i: leaves[i].parts for i in far if leaves[i].parts is not None}
    leaves = [
        pltpu.with_memory_space_constraint(a.value, pltpu.HBM) if isinstance(a, Far) else a
        for a in leaves
    ]

    def body(*refs):
        sources, results = refs[:count], list(refs[count : count + n_out])
        rest = refs[count + n_out :]
        sems, rest = rest[0], rest[1:]
        coming = [Arriving(a) for a in sources]
        used = 0
        for n, i in enumerate(far):
            pieces = [(sources[i], rest[n])]
            if i in parts:
                pieces = [(sources[i].at[p], rest[n].at[p]) for p in chunks(leaves[i].shape[0], parts[i])]
            arrivals = []
            for source, target in pieces:
                copy = pltpu.make_async_copy(source, target, sems.at[used])
                copy.start()
                arrivals.append(Arriving(target, copy))
                used += 1
            coming[i] = arrivals if i in parts else arrivals[0]
        for n, i in enumerate(stored):
            results[i] = Leaving(results[i], sems.at[used])
            used += 1
        kernel(
            *jax.tree.unflatten(tree, coming),
            jax.tree.unflatten(out_tree, results),
            *rest[len(far) :],
        )
        fetch(coming)
        for i in stored:
            results[i].done()

    n_sems = len(far) - len(parts) + len(stored) + sum(len(p) for p in parts.values())
    size = sum(4 * math.prod(a.shape) for a in leaves + out_leaves)
    given = pl.pallas_call(
        body,
        out_shape=[
            pltpu.HBM(a.shape, F32) if i in distant else shaped(*a.shape)
            for i, a in enumerate(out_leaves)
        ],
        in_specs=[
            pl.BlockSpec(
                memory_space=pltpu.HBM if i in far + raw else pltpu.VMEM
            )
            for i in range(count)
        ],
        out_specs=[
            pl.BlockSpec(memory_space=pltpu.HBM if i in distant else pltpu.VMEM)
            for i in range(n_out)
        ],
        scratch_shapes=[pltpu.SemaphoreType.DMA((max(1, n_sems),))]
        + [pltpu.VMEM(leaves[i].shape, leaves[i].dtype) for i in far]
        + list(scratch),
        compiler_params=pltpu.CompilerParams(vmem_limit_bytes=VMEM_LIMIT),
        cost_estimate=pl.CostEstimate(flops=flops, bytes_accessed=size, transcendentals=0),
    )(*leaves)
    return jax.tree.unflatten(out_tree, given)


def chunks(count, parts):
    each = count // PARTS
    return [pl.ds(p * each, each) for p in parts]


def far(tree):
    return jax.tree.map(Far, tree)


def fetch(tree):
    return jax.tree.map(
        lambda one: one.get() if isinstance(one, Arriving) else one,
        tree,
        is_leaf=lambda one: isinstance(one, Arriving),
    )


def loop(first, last, body):
    lax.fori_loop(first, last, body, 0, unroll=UNROLL)


def shaped(*shape):
    return jax.ShapeDtypeStruct(shape, F32)


def face_shapes(shape, sizes, count, width):
    nx, ny, nz = shape
    blocks = count * width + (1 if width == 2 else 0)
    outs = {
        "x": {r: shaped(blocks, ny, nz) for r in rounds_of(sizes[0])},
        "y": {r: shaped(blocks, nx, nz) for r in rounds_of(sizes[1])},
    }
    if width == 2:
        outs["xy"] = {
            (rx, ry): shaped(4 * count + 4, nz)
            for rx in rounds_of(sizes[0])
            for ry in rounds_of(sizes[1])
        }
    return outs


def pack_faces(out, fields, sizes, width, ends=None):
    ix, iy, _ = where_am_i()
    for r, ref in out["x"].items():
        pack_x(ref, fields, r, ix, width, ends)
    for r, ref in out["y"].items():
        pack_y(ref, fields, r, iy, width, ends)
    for (rx, ry), ref in out.get("xy", {}).items():
        pack_xy(ref, fields, rx, ry, ix, iy, ends)


def send_z(tile, sizes):
    return {r: swap(tile, sizes, {2: r}) for r in rounds_of(sizes[2])}


def send_faces(faces, sizes):
    got = {
        "x": {r: swap(v, sizes, {0: r}) for r, v in faces["x"].items()},
        "y": {r: swap(v, sizes, {1: r}) for r, v in faces["y"].items()},
    }
    if "xy" in faces:
        got["xy"] = {(rx, ry): swap(v, sizes, {0: rx, 1: ry}) for (rx, ry), v in faces["xy"].items()}
    return got


def spread(rows):
    return lax.all_to_all(rows, AXES, 0, 0, tiled=True)


def shards(sizes, right_side, conductance, storage, dirichlet, basis, coarse_inverse):
    shape = right_side.shape
    nx, ny, nz = shape
    vecs = basis.shape[0]
    boxed = box_shape(shape)
    devices = sizes[0] * sizes[1] * sizes[2]
    row_shape = shaped(devices, LANES)
    sum_shape = (devices * vecs // LANES, LANES)
    ends_shape = (nx, ny, LANES)
    vbox = pltpu.VMEM(boxed, F32)
    def pack_first(cond, store, fixed, rhs, outs):
        near, free = outs["near"], outs["free"]
        for target, source in zip(near, (cond, store, rhs)):
            target.put(source.get())
        fixed = fixed.get()
        free[...] = 1.0 - fixed[...].astype(F32)
        cond, store, rhs = [one.done() for one in near]
        outs["tile"][...] = pack_z([cond.at[0], cond.at[1], cond.at[2], store, free, rhs])

    first = call(
        pack_first,
        {
            "near": [Stored(*a.shape, near=True) for a in (conductance, storage, right_side)],
            "free": shaped(*shape),
            "tile": shaped(z_rows(6), nx * ny),
        },
        (Raw(conductance), Raw(storage), Far(dirichlet), Raw(right_side)),
    )
    got_z = send_z(first["tile"], sizes)

    def first_rows(rhs, base, out):
        row = project(base, rhs.get()[...])
        out[...] = jnp.broadcast_to(row, out.shape)

    rows = call(first_rows, row_shape, (first["near"][2], Far(basis, range(PARTS))))
    rows_a = spread(rows)

    def pack_all(got_z, near, free, rows, outs, ends):
        cond, store, rhs = fetch(near)
        fields = [cond.at[0], cond.at[1], cond.at[2], store, free.get(), rhs]
        ends[...] = pick_z(fetch(got_z), sizes, ends_shape)
        pack_faces(outs, fields, sizes, 2, ends)

    packed = call(
        pack_all,
        face_shapes(shape, sizes, 6, 2),
        (got_z, first["near"], first["free"], rows),
        [pltpu.VMEM(ends_shape, F32)],
    )
    got = send_faces(packed, sizes)

    def first_smooth(got, cond, store, fixed, rhs, got_z, base, outs, sems, step, *boxes):
        boxes = list(boxes)
        cond, store, rhs = fetch((cond, store, rhs))
        owns = [cond.at[0], cond.at[1], cond.at[2], store, None, rhs]
        copies = []
        for k, own in enumerate(owns):
            if own is not None:
                copies.append(
                    pltpu.make_async_copy(own, own_cells(boxes[k], shape), sems.at[k])
                )
                copies[-1].start()
        for b in boxes[:6]:
            clear_round(b, shape)
        got = fetch(got)
        ends = pick_z(fetch(got_z), sizes, ends_shape)
        unpack_faces(boxes[:6], [None] * 6, got["x"], got["y"], sizes, 2, ends)
        unpack_xy(boxes[:6], shape, got["xy"], sizes)
        boxes[4][3 : 3 + nx, 0:ny, 0:nz] = 1.0 - fixed.get()[...].astype(F32)
        for copy in copies:
            copy.wait()
        for target, piece in zip(outs["base"], chunks(vecs, NEAR_FIRST)):
            target.put(base.get().at[piece])
        links, boxes = boxes[6:], boxes[:6]
        coefficients(boxes, links, step, outs["own"])
        outs["kept"]["step"].put(step)
        for kept, link in zip(outs["kept"]["links"], links):
            kept.put(link)
        jacobi(boxes[5], step, links, boxes[0], boxes[1], boxes[5], outs["smooth"])

    smoothed = call(
        first_smooth,
        {
            "smooth": shaped(*shape),
            "own": shaped(7, *shape),
            "base": [Stored(vecs // PARTS, *shape, near=True) for _ in NEAR_FIRST],
            "kept": {
                "links": [Stored(*boxed), Stored(*boxed), Stored(*boxed)],
                "step": Stored(*boxed),
            },
        },
        (
            got,
            Raw(conductance),
            Raw(storage),
            Far(dirichlet),
            Raw(right_side),
            got_z,
            Raw(basis),
        ),
        [pltpu.SemaphoreType.DMA((6,))] + [vbox] * 10,
        flops=SMOOTH_FLOPS,
    )
    kept = smoothed["kept"]
    own = smoothed["own"]

    def base_rest(smoothed, near):
        return smoothed["base"] + [Far(basis, range(len(near), PARTS))]

    def first_direction(smooth, rows, inverse, base, outs):
        smooth, rows = fetch((smooth, rows))
        weights = coarse_weights(inverse.get(), coarse_sum(rows, vecs))
        add_coarse(outs["z"], smooth, base, weights)
        pack_faces(outs["faces"], [outs["z"]], sizes, 1)
        outs["tile"][...] = pack_z([outs["z"]])

    directed = call(
        first_direction,
        {
            "z": shaped(*shape),
            "faces": face_shapes(shape, sizes, 1, 1),
            "tile": shaped(z_rows(1), nx * ny),
        },
        (smoothed["smooth"], rows_a, Far(coarse_inverse), base_rest(smoothed, NEAR_FIRST)),
    )
    direction = directed["z"]
    got = send_faces(directed["faces"], sizes)
    got_z = send_z(directed["tile"], sizes)

    def apply(field, got, got_z, own, out, vb):
        clear_round(vb, shape)
        field, got, got_z = fetch((field, got, got_z))
        unpack_faces([vb], [field], got["x"], got["y"], sizes, 1)
        vb[3 : 3 + nx, 0:ny, nz : nz + LANES] = halo_lanes(pick_z(got_z, sizes, ends_shape), 0)
        own = own.get()

        def body(x, carry):
            mid = vb[x + 3]
            around = (mid, vb[x + 4], vb[x + 2])
            around += (ahead(mid, 0), behind(mid, 0), ahead(mid, 1), behind(mid, 1))
            total = own[0, x] * mid[0:ny, 0:nz]
            for n in range(1, 7):
                total = total - own[n, x] * around[n][0:ny, 0:nz]
            out[x] = total
            return carry

        loop(0, nx, body)

    def first_image(got, got_z, field, own, rhs, outs, vb):
        image = outs["image"]
        outs["own"].put(own.get())
        outs["z"].put(field.get())
        apply(field, got, got_z, own, image, vb)
        outs["kept"].put(image)
        outs["tile"][...] = pack_z([image])
        field, rhs = fetch((field, rhs))
        values = [full_sum(rhs[...] * field[...]), full_sum(field[...] * image[...])]
        outs["sums"][...] = put_scalars(jnp.zeros((1, LANES), F32), vecs, values)

    imaged = call(
        first_image,
        {
            "image": shaped(*shape),
            "kept": Stored(*shape),
            "own": Stored(7, *shape),
            "z": Stored(*shape),
            "tile": shaped(z_rows(1), nx * ny),
            "sums": shaped(1, LANES),
        },
        (got, got_z, direction, own, right_side),
        [vbox],
    )
    got_z = send_z(imaged["tile"], sizes)
    kept_z = imaged["z"]

    def second_rows(base, field, sums, out):
        row = project(base, field.get()[...]) + sums.get()[...]
        out[...] = jnp.broadcast_to(row, out.shape)

    rows = call(second_rows, row_shape, ([basis], imaged["image"], imaged["sums"]))
    rows_c = spread(rows)

    def pack_image(got_z, field, rows, outs, ends):
        ends[...] = pick_z(fetch(got_z), sizes, ends_shape)
        pack_faces(outs, [field.get()], sizes, 2, ends)

    packed = call(
        pack_image,
        face_shapes(shape, sizes, 1, 2),
        (got_z, imaged["image"], rows),
        [pltpu.VMEM(ends_shape, F32)],
    )
    got = send_faces(packed, sizes)

    def second_smooth(got, field, got_z, step, links, base, outs, sem, ga, gb, vb):
        copy = pltpu.make_async_copy(field.get(), own_cells(vb, shape), sem)
        copy.start()
        clear_round(vb, shape)
        got = fetch(got)
        ends = pick_z(fetch(got_z), sizes, ends_shape)
        unpack_faces([vb], [None], got["x"], got["y"], sizes, 2, ends)
        unpack_xy([vb], shape, got["xy"], sizes)
        copy.wait()
        for target, piece in zip(outs["base"], chunks(vecs, NEAR_SECOND)):
            target.put(base.get().at[piece])
        jacobi(vb, step.get(), links, ga, gb, vb, outs["smooth"])

    smoothed = call(
        second_smooth,
        {
            "smooth": shaped(*shape),
            "base": [Stored(vecs // PARTS, *shape, near=True) for _ in NEAR_SECOND],
        },
        (
            got,
            Raw(imaged["kept"]),
            got_z,
            Far(kept["step"]),
            far(kept["links"]),
            Raw(basis),
        ),
        [pltpu.SemaphoreType.DMA] + [vbox] * 3,
        flops=SMOOTH_FLOPS,
    )

    def second_direction(smooth, rows, inverse, field, rhs, before, base, outs):
        smooth, rows = fetch((smooth, rows))
        norm, curve = scalar_sums(rows, vecs, 2)
        alpha = norm / curve
        weights = coarse_weights(inverse.get(), coarse_sum(rows, vecs))
        field, rhs, before = fetch((field, rhs, before))
        outs["residual"][...] = rhs[...] - alpha * field[...]
        add_coarse(outs["z"], smooth, base, weights)
        outs["z"][...] = before[...] - alpha * outs["z"][...]
        pack_faces(outs["faces"], [outs["z"]], sizes, 1)
        outs["tile"][...] = pack_z([outs["z"]])
        outs["scalars"][...] = jnp.concatenate(
            [jnp.broadcast_to(norm, (8, LANES)), jnp.broadcast_to(curve, (8, LANES))], axis=0
        )

    directed = call(
        second_direction,
        {
            "z": shaped(*shape),
            "residual": shaped(*shape),
            "scalars": shaped(16, LANES),
            "faces": face_shapes(shape, sizes, 1, 1),
            "tile": shaped(z_rows(1), nx * ny),
        },
        (
            smoothed["smooth"],
            rows_c,
            Far(coarse_inverse),
            Far(imaged["kept"]),
            Far(right_side),
            Far(kept_z),
            base_rest(smoothed, NEAR_SECOND),
        ),
    )
    precond, residual = directed["z"], directed["residual"]
    got = send_faces(directed["faces"], sizes)
    got_z = send_z(directed["tile"], sizes)
    image, direction = imaged["kept"], kept_z

    def second_image(got, got_z, field, own, image, residual, outs, vb):
        apply(field, got, got_z, own, outs["image"], vb)
        field, image, residual = fetch((field, image, residual))
        values = [
            full_sum(residual[...] * field[...]),
            full_sum(field[...] * outs["image"][...]),
            full_sum(field[...] * image[...]),
        ]
        row = put_scalars(jnp.zeros((1, LANES), F32), 0, values)
        outs["rows"][...] = jnp.broadcast_to(row, outs["rows"].shape)

    last = call(
        second_image,
        {"image": shaped(*shape), "rows": row_shape},
        (
            got,
            got_z,
            precond,
            imaged["own"],
            image,
            residual,
        ),
        [vbox],
    )
    rows_e = spread(last["rows"])

    def finish(rows, scalars, direction, image, precond, precond_image, residual, outs):
        rows, scalars = fetch((rows, scalars))
        norm = scalars[0:1, 0:1]
        curve = scalars[8:9, 0:1]
        norm_next, curve_z, curve_mixed = scalar_sums(rows, 0, 3)
        alpha = norm / curve
        beta = norm_next / norm
        curve_next = curve_z + 2.0 * beta * curve_mixed + beta * beta * curve
        alpha_next = norm_next / curve_next
        direction, image, precond = fetch((direction, image, precond))
        precond_image, residual = fetch((precond_image, residual))
        outs[0][...] = alpha * direction[...] + alpha_next * (
            precond[...] + beta * direction[...]
        )
        outs[1][...] = residual[...] - alpha_next * (precond_image[...] + beta * image[...])

    return tuple(
        call(
            finish,
            [shaped(*shape), shaped(*shape)],
            (rows_e, directed["scalars"], direction, image, precond, last["image"], residual),
        )
    )


def solution(mesh):
    sizes = tuple(mesh.shape[a] for a in AXES)
    placed = (
        P("gx", "gy", "gz"),
        P(None, "gx", "gy", "gz"),
        P("gx", "gy", "gz"),
        P("gx", "gy", "gz"),
        P(None, "gx", "gy", "gz"),
        P(("gx", "gy", "gz"), None),
    )
    return jax.shard_map(
        functools.partial(shards, sizes),
        mesh=mesh,
        in_specs=placed,
        out_specs=(P("gx", "gy", "gz"), P("gx", "gy", "gz")),
        check_vma=False,
    )
```

```python
import functools
import math

import jax
import jax.numpy as jnp
from jax import lax
from jax.experimental import pallas as pl
from jax.experimental.pallas import tpu as pltpu
from jax.sharding import PartitionSpec as P

SWEEPS = 4
RELAX = 2.0 / 3.0
AXES = ("gx", "gy", "gz")
LANES = 128
VMEM_LIMIT = 24 * 1024 * 1024
F32 = jnp.float32
UNROLL = 16
SWEEP_UNROLL = True
PARTS = 16
NEAR_FIRST = range(2)
NEAR_SECOND = range(10)
SMOOTH_FLOPS = 10**9


def rounds_of(count):
    return (0, 1)[: 1 if count <= 2 else 2]


def mate(index, odd, count):
    other = index + 1 if index % 2 == odd else index - 1
    return other if 0 <= other < count else None


def swap(value, sizes, along):
    pairs = []
    nx, ny, nz = sizes
    for ix in range(nx):
        for iy in range(ny):
            for iz in range(nz):
                here = [ix, iy, iz]
                there = [
                    mate(here[a], along[a], sizes[a]) if a in along else here[a] for a in range(3)
                ]
                if None in there:
                    if 2 in along:
                        spare = nz - 1 - iz if iz in (0, nz - 1) else None
                    else:
                        spare = iz ^ 1 if nz % 2 == 0 else None
                    if spare is None:
                        continue
                    there = [ix, iy, spare]
                pairs.append(
                    ((ix * ny + iy) * nz + iz, (there[0] * ny + there[1]) * nz + there[2])
                )
    return lax.ppermute(value, AXES, pairs)


def upward(index, odd):
    return lax.rem(index, 2) == odd


def where_am_i():
    return [lax.axis_index(a) for a in AXES]


def lane_iota(shape):
    return lax.broadcasted_iota(jnp.int32, shape, len(shape) - 1)


def pack_x(out, fields, odd, index, width, ends=None):
    nx, _, nz = fields[0].shape
    count = len(fields) * width
    high = upward(index, odd)
    for cond, first in ((high, nx - width), (jnp.logical_not(high), 0)):

        @pl.when(cond)
        def _(first=first):
            for k, field in enumerate(fields):
                out[k * width : (k + 1) * width] = field[first : first + width]
            if ends is not None:
                for i in range(width):
                    out[count, :, LANES * i : LANES * (i + 1)] = ends[first + i]


def pack_y(out, fields, odd, index, width, ends=None):
    _, ny, nz = fields[0].shape
    count = len(fields) * width
    high = upward(index, odd)
    for cond, first in ((high, ny - width), (jnp.logical_not(high), 0)):

        @pl.when(cond)
        def _(first=first):
            for j in range(width):
                for k, field in enumerate(fields):
                    out[k * width + j] = field[:, first + j, :]
                if ends is not None:
                    out[count, :, LANES * j : LANES * (j + 1)] = ends[:, first + j, :]


def pack_xy(out, fields, rx, ry, ix, iy, ends):
    nx, ny, _ = fields[0].shape
    count = len(fields)
    for xhigh in (False, True):
        for yhigh in (False, True):

            @pl.when((upward(ix, rx) == xhigh) & (upward(iy, ry) == yhigh))
            def _(x0=(nx - 2 if xhigh else 0), y0=(ny - 2 if yhigh else 0)):
                for i in range(2):
                    for k, field in enumerate(fields):
                        out[4 * k + 2 * i : 4 * k + 2 * i + 2, :] = field[x0 + i, y0 : y0 + 2, :]
                    out[4 * count + 2 * i : 4 * count + 2 * i + 2, 0:LANES] = ends[
                        x0 + i, y0 : y0 + 2, :
                    ]


def z_rows(count):
    return (4 * count + 7) // 8 * 8


def pack_z(fields):
    nx, ny, nz = fields[0].shape
    lane = lane_iota((nx, ny, LANES))
    total = jnp.zeros((nx, ny, LANES), F32)
    for k, field in enumerate(fields):
        ends = jnp.where(lane < 64, field[:, :, 0:LANES], field[:, :, nz - LANES : nz])
        turned = pltpu.roll(ends, 4 * k + 2, 2)
        total = jnp.where((lane >= 4 * k) & (lane < 4 * k + 4), turned, total)
    return total.reshape(nx * ny, LANES).T[0 : z_rows(len(fields))]


def project(basis, field):
    nx, ny, nz = field.shape
    rows = []
    for piece in basis:
        vectors = piece.get()
        for k in range(vectors.shape[0]):
            prod = jnp.sum(vectors[k] * field, axis=0)
            part = jnp.zeros((8, LANES), F32)
            for y in range(ny // 8):
                for z in range(nz // LANES):
                    part = part + prod[8 * y : 8 * y + 8, LANES * z : LANES * (z + 1)]
            rows.append(jnp.sum(part, axis=0, keepdims=True))
    vecs = len(rows)
    totals = jnp.sum(jnp.concatenate(rows, axis=0), axis=1, keepdims=True)
    row = lax.broadcasted_iota(jnp.int32, (vecs, LANES), 0)
    return jnp.sum(jnp.where(lane_iota((vecs, LANES)) == row, totals, 0.0), axis=0, keepdims=True)


def put_scalars(row, first, values):
    lane = lane_iota(row.shape)
    for i, value in enumerate(values):
        row = jnp.where(lane == first + i, value, row)
    return row


def box_shape(shape):
    nx, ny, nz = shape
    return (nx + 6, ny + 8, nz + LANES)


def clear(box):
    def body(x, carry):
        box[x] = jnp.zeros(box.shape[1:], F32)
        return carry

    loop(0, box.shape[0], body)


def clear_round(box, shape):
    nx, ny, nz = shape
    planes, rows, lanes = box.shape
    for x in (0, 1, 2, planes - 3, planes - 2, planes - 1):
        box[x] = jnp.zeros((rows, lanes), F32)

    def body(x, carry):
        box[x, ny:rows, :] = jnp.zeros((rows - ny, lanes), F32)
        box[x, 0:ny, nz:lanes] = jnp.zeros((ny, lanes - nz), F32)
        return carry

    loop(3, 3 + nx, body)


def own_cells(box, shape):
    nx, ny, nz = shape
    return box.at[3 : 3 + nx, 0:ny, 0:nz]


def each_round(sizes, a, index, act):
    for r in rounds_of(sizes[a]):
        high = upward(index, r)

        @pl.when(high & (index + 1 < sizes[a]))
        def _(r=r):
            act(r, True)

        @pl.when(jnp.logical_not(high) & (index > 0))
        def _(r=r):
            act(r, False)


def unpack_faces(boxes, owns, xs, ys, sizes, width, ends=None):
    nx, ny, nz = boxes[0].shape[0] - 6, boxes[0].shape[1] - 8, boxes[0].shape[2] - LANES
    count = len(boxes) * width
    ix, iy, _ = where_am_i()
    for k, (box, own) in enumerate(zip(boxes, owns)):
        if own is not None:
            box[3 : 3 + nx, 0:ny, 0:nz] = own[...]
        if ends is not None:
            box[3 : 3 + nx, 0:ny, nz : nz + LANES] = halo_lanes(ends, k)

    def put_x(r, above):
        first = 3 + nx if above else 3 - width
        for k, box in enumerate(boxes):
            box[first : first + width, 0:ny, 0:nz] = xs[r][k * width : (k + 1) * width]
            if ends is not None:
                for i in range(width):
                    tile = xs[r][count, :, LANES * i : LANES * (i + 1)]
                    box[first + i, 0:ny, nz : nz + LANES] = halo_lanes(tile, k)

    each_round(sizes, 0, ix, put_x)

    def put_y(r, above):
        first = ny if above else ny + 8 - width
        for k, box in enumerate(boxes):
            for j in range(width):
                box[3 : 3 + nx, first + j, 0:nz] = ys[r][k * width + j]
                if ends is not None:
                    tile = ys[r][count, :, LANES * j : LANES * (j + 1)]
                    box[3 : 3 + nx, first + j, nz : nz + LANES] = halo_lanes(tile, k)

    each_round(sizes, 1, iy, put_y)


def unpack_xy(boxes, shape, xys, sizes):
    nx, ny, nz = shape
    count = len(boxes)
    ix, iy, _ = where_am_i()

    def put(rx, xabove):
        x0 = 3 + nx if xabove else 1

        def inner(ry, yabove):
            y0 = ny if yabove else ny + 6
            rows = xys[(rx, ry)]
            tile = rows[4 * count : 4 * count + 4, 0:LANES]
            for k, box in enumerate(boxes):
                turned = halo_lanes(tile, k)
                for i in range(2):
                    box[x0 + i, y0 : y0 + 2, 0:nz] = rows[4 * k + 2 * i : 4 * k + 2 * i + 2, :]
                    box[x0 + i, y0 : y0 + 2, nz : nz + LANES] = turned[2 * i : 2 * i + 2]

        each_round(sizes, 1, iy, inner)

    each_round(sizes, 0, ix, put)


def pick_z(zs, sizes, shape):
    count = sizes[2]
    iz = lax.axis_index("gz")
    rows, cells = zs[0].shape
    first = lax.rem(lax.broadcasted_iota(jnp.int32, (rows, cells), 0), 4) < 2
    total = jnp.zeros((rows, cells), F32)
    for r in rounds_of(count):
        high = upward(iz, r)
        below = jnp.logical_not(high) & (iz > 0)
        above = high & (iz + 1 < count)
        total = jnp.where((first & below) | (jnp.logical_not(first) & above), zs[r][...], total)
    filled = jnp.concatenate([total, jnp.zeros((LANES - rows, cells), F32)], axis=0)
    return filled.T.reshape(shape)


def halo_lanes(tile, k):
    lane = lane_iota(tile.shape)
    axis = len(tile.shape) - 1
    turned = pltpu.roll(tile, (-(4 * k + 2)) % LANES, axis)
    return jnp.where((lane < 2) | (lane >= LANES - 2), turned, 0.0)


def ahead(plane, axis):
    return pltpu.roll(plane, plane.shape[axis] - 1, axis)


def behind(plane, axis):
    return pltpu.roll(plane, 1, axis)


def coefficients(fields, links, step, own):
    tx, ty, tz, store, free, _ = fields
    lx, ly, lz = links
    _, nx, ny, nz = own.shape
    last = tx.shape[0] - 1
    for ref in (lx, ly, lz, step):
        ref[0] = jnp.zeros(ref.shape[1:], F32)
        ref[last] = jnp.zeros(ref.shape[1:], F32)

    def body(x, carry, inside):
        f = free[x]
        a, b, c = tx[x], ty[x], tz[x]
        total = store[x] + a + tx[x - 1] + b + behind(b, 0) + c + behind(c, 1)
        d = f * total + (1.0 - f)
        step[x] = RELAX / d
        links_here = (a * f * free[x + 1], b * f * ahead(f, 0), c * f * ahead(f, 1))
        for ref, value in zip(links, links_here):
            ref[x] = value
        if inside:
            x_link, y_link, z_link = links_here
            mine = (
                d,
                x_link,
                lx[x - 1],
                y_link,
                behind(y_link, 0),
                z_link,
                behind(z_link, 1),
            )
            for n, value in enumerate(mine):
                own[n, x - 3] = value[0:ny, 0:nz]
        return carry

    loop(1, 3, functools.partial(body, inside=False))
    loop(3, 3 + nx, functools.partial(body, inside=True))
    loop(3 + nx, last, functools.partial(body, inside=False))


def jacobi(rhs, step, links, ga, gb, source, out):
    planes = rhs.shape[0]
    nx, ny, nz = out.shape
    for g in (ga, gb):
        g[0] = jnp.zeros(g.shape[1:], F32)
        g[planes - 1] = jnp.zeros(g.shape[1:], F32)

    def first(x, carry):
        source[x] = step[x] * rhs[x]
        return carry

    loop(1, planes - 1, first)

    lx, ly, lz = fetch(links)

    def swept(now, x, carry):
        before, mid, x_before = carry
        after, x_here, y, z = now[x + 1], lx[x], ly[x], lz[x]
        total = x_here * after + x_before * before
        total = total + y * ahead(mid, 0) + behind(y * mid, 0)
        total = total + z * ahead(mid, 1) + behind(z * mid, 1)
        value = (1.0 - RELAX) * mid + source[x] + step[x] * total
        return value, (mid, after, x_here)

    def sweep_planes(now, first, last, put):
        def body(x, carry):
            value, carry = swept(now, x, carry)
            put(x, value)
            return carry

        start = (now[first - 1], now[first], lx[first - 1])
        lax.fori_loop(first, last, body, start, unroll=SWEEP_UNROLL)

    now, then, spare = source, ga, gb
    for sweep in range(1, SWEEPS - 1):
        edge = max(1, 3 - (SWEEPS - 1 - sweep))

        def put(x, value, then=then):
            then[x] = value

        sweep_planes(now, edge, planes - edge, put)
        now, then, spare = then, spare, then

    def put_own(x, value):
        out[x - 3] = value[0:ny, 0:nz]

    sweep_planes(now, 3, 3 + nx, put_own)


def coarse_sum(rows_ref, vecs):
    count = rows_ref.shape[0]
    per = LANES // vecs
    lane = lane_iota((count, LANES))
    row = lax.broadcasted_iota(jnp.int32, (count, LANES), 0)
    all_rows = rows_ref[...]
    total = jnp.zeros((count, LANES), F32)
    for m in range(per):
        turned = pltpu.roll(all_rows, vecs * m, 1) if m else all_rows
        keep = (lax.rem(row, per) == m) & (lane >= vecs * m) & (lane < vecs * (m + 1))
        total = jnp.where(keep, turned, total)
    return jnp.sum(total.reshape(count // per, per, LANES), axis=1)


def scalar_sums(rows_ref, first, count):
    total = jnp.sum(rows_ref[...], axis=0, keepdims=True)
    return [total[0:1, first + i : first + i + 1] for i in range(count)]


def coarse_weights(inverse_ref, sums):
    total = jnp.zeros((inverse_ref.shape[0], LANES), F32)
    for g in range(sums.shape[0]):
        total = total + inverse_ref[:, LANES * g : LANES * (g + 1)] * sums[g : g + 1, :]
    return jnp.sum(total, axis=1, keepdims=True)


def add_coarse(out, smooth, basis, weights):
    nx, ny, nz = out.shape
    k = 0
    for piece in jax.tree.leaves(basis):
        vectors = piece.get()
        count = vectors.shape[0]
        scale = [jnp.broadcast_to(weights[k + i : k + i + 1, 0:1], (8, LANES)) for i in range(count)]
        scale = [jnp.tile(s, (ny // 8, nz // LANES)) for s in scale]
        source = smooth if k == 0 else out

        def body(x, carry, vectors=vectors, scale=scale, source=source):
            total = source[x]
            for i, s in enumerate(scale):
                total = total + s * vectors[i, x]
            out[x] = total
            return carry

        loop(0, nx, body)
        k += count


def full_sum(value):
    return jnp.sum(value)


class Arriving:
    def __init__(self, buffer, copy=None):
        self.copy = copy
        self.buffer = buffer

    def get(self):
        if self.copy is not None:
            self.copy.wait()
            self.copy = None
        return self.buffer


class Far:
    def __init__(self, value, parts=None):
        self.value, self.parts = value, parts


class Raw(Far):
    pass


class Stored:
    def __init__(self, *shape, near=False):
        self.shape, self.near = shape, near


class Leaving:
    def __init__(self, target, sem):
        self.target, self.sem, self.copy = target, sem, None

    def put(self, source):
        self.copy = pltpu.make_async_copy(source, self.target, self.sem)
        self.copy.start()

    def done(self):
        if self.copy is not None:
            self.copy.wait()
            self.copy = None
        return self.target


def call(kernel, outs, args, scratch=(), flops=0):
    leaves, tree = jax.tree.flatten(list(args), is_leaf=lambda one: isinstance(one, Far))
    out_leaves, out_tree = jax.tree.flatten(outs, is_leaf=lambda one: isinstance(one, Stored))
    count, n_out = len(leaves), len(out_leaves)
    raw = [i for i, a in enumerate(leaves) if isinstance(a, Raw)]
    far = [i for i, a in enumerate(leaves) if isinstance(a, Far) and i not in raw]
    distant = [i for i, a in enumerate(out_leaves) if isinstance(a, Stored) and not a.near]
    stored = [i for i, a in enumerate(out_leaves) if isinstance(a, Stored)]
    parts = {i: leaves[i].parts for i in far if leaves[i].parts is not None}
    leaves = [
        pltpu.with_memory_space_constraint(a.value, pltpu.HBM) if isinstance(a, Far) else a
        for a in leaves
    ]

    def body(*refs):
        sources, results = refs[:count], list(refs[count : count + n_out])
        rest = refs[count + n_out :]
        sems, rest = rest[0], rest[1:]
        coming = [Arriving(a) for a in sources]
        used = 0
        for n, i in enumerate(far):
            pieces = [(sources[i], rest[n])]
            if i in parts:
                pieces = [(sources[i].at[p], rest[n].at[p]) for p in chunks(leaves[i].shape[0], parts[i])]
            arrivals = []
            for source, target in pieces:
                copy = pltpu.make_async_copy(source, target, sems.at[used])
                copy.start()
                arrivals.append(Arriving(target, copy))
                used += 1
            coming[i] = arrivals if i in parts else arrivals[0]
        for n, i in enumerate(stored):
            results[i] = Leaving(results[i], sems.at[used])
            used += 1
        kernel(
            *jax.tree.unflatten(tree, coming),
            jax.tree.unflatten(out_tree, results),
            *rest[len(far) :],
        )
        fetch(coming)
        for i in stored:
            results[i].done()

    n_sems = len(far) - len(parts) + len(stored) + sum(len(p) for p in parts.values())
    size = sum(4 * math.prod(a.shape) for a in leaves + out_leaves)
    given = pl.pallas_call(
        body,
        out_shape=[
            pltpu.HBM(a.shape, F32) if i in distant else shaped(*a.shape)
            for i, a in enumerate(out_leaves)
        ],
        in_specs=[
            pl.BlockSpec(
                memory_space=pltpu.HBM if i in far + raw else pltpu.VMEM
            )
            for i in range(count)
        ],
        out_specs=[
            pl.BlockSpec(memory_space=pltpu.HBM if i in distant else pltpu.VMEM)
            for i in range(n_out)
        ],
        scratch_shapes=[pltpu.SemaphoreType.DMA((max(1, n_sems),))]
        + [pltpu.VMEM(leaves[i].shape, leaves[i].dtype) for i in far]
        + list(scratch),
        compiler_params=pltpu.CompilerParams(vmem_limit_bytes=VMEM_LIMIT),
        cost_estimate=pl.CostEstimate(flops=flops, bytes_accessed=size, transcendentals=0),
    )(*leaves)
    return jax.tree.unflatten(out_tree, given)


def chunks(count, parts):
    each = count // PARTS
    return [pl.ds(p * each, each) for p in parts]


def far(tree):
    return jax.tree.map(Far, tree)


def fetch(tree):
    return jax.tree.map(
        lambda one: one.get() if isinstance(one, Arriving) else one,
        tree,
        is_leaf=lambda one: isinstance(one, Arriving),
    )


def loop(first, last, body):
    lax.fori_loop(first, last, body, 0, unroll=UNROLL)


def shaped(*shape):
    return jax.ShapeDtypeStruct(shape, F32)


def face_shapes(shape, sizes, count, width):
    nx, ny, nz = shape
    blocks = count * width + (1 if width == 2 else 0)
    outs = {
        "x": {r: shaped(blocks, ny, nz) for r in rounds_of(sizes[0])},
        "y": {r: shaped(blocks, nx, nz) for r in rounds_of(sizes[1])},
    }
    if width == 2:
        outs["xy"] = {
            (rx, ry): shaped(4 * count + 4, nz)
            for rx in rounds_of(sizes[0])
            for ry in rounds_of(sizes[1])
        }
    return outs


def pack_faces(out, fields, sizes, width, ends=None):
    ix, iy, _ = where_am_i()
    for r, ref in out["x"].items():
        pack_x(ref, fields, r, ix, width, ends)
    for r, ref in out["y"].items():
        pack_y(ref, fields, r, iy, width, ends)
    for (rx, ry), ref in out.get("xy", {}).items():
        pack_xy(ref, fields, rx, ry, ix, iy, ends)


def send_z(tile, sizes):
    return {r: swap(tile, sizes, {2: r}) for r in rounds_of(sizes[2])}


def send_faces(faces, sizes):
    got = {
        "x": {r: swap(v, sizes, {0: r}) for r, v in faces["x"].items()},
        "y": {r: swap(v, sizes, {1: r}) for r, v in faces["y"].items()},
    }
    if "xy" in faces:
        got["xy"] = {(rx, ry): swap(v, sizes, {0: rx, 1: ry}) for (rx, ry), v in faces["xy"].items()}
    return got


def spread(rows):
    return lax.all_to_all(rows, AXES, 0, 0, tiled=True)


def shards(sizes, right_side, conductance, storage, dirichlet, basis, coarse_inverse):
    shape = right_side.shape
    nx, ny, nz = shape
    vecs = basis.shape[0]
    boxed = box_shape(shape)
    devices = sizes[0] * sizes[1] * sizes[2]
    row_shape = shaped(devices, LANES)
    sum_shape = (devices * vecs // LANES, LANES)
    ends_shape = (nx, ny, LANES)
    vbox = pltpu.VMEM(boxed, F32)
    def pack_first(cond, store, fixed, rhs, outs):
        near, free = outs["near"], outs["free"]
        for target, source in zip(near, (cond, store, rhs)):
            target.put(source.get())
        fixed = fixed.get()
        free[...] = 1.0 - fixed[...].astype(F32)
        cond, store, rhs = [one.done() for one in near]
        outs["tile"][...] = pack_z([cond.at[0], cond.at[1], cond.at[2], store, free, rhs])

    first = call(
        pack_first,
        {
            "near": [Stored(*a.shape, near=True) for a in (conductance, storage, right_side)],
            "free": shaped(*shape),
            "tile": shaped(z_rows(6), nx * ny),
        },
        (Raw(conductance), Raw(storage), Far(dirichlet), Raw(right_side)),
    )
    got_z = send_z(first["tile"], sizes)

    def first_rows(rhs, base, out):
        row = project(base, rhs.get()[...])
        out[...] = jnp.broadcast_to(row, out.shape)

    rows = call(first_rows, row_shape, (first["near"][2], Far(basis, range(PARTS))))
    rows_a = spread(rows)

    def pack_all(got_z, near, free, rows, outs, ends):
        cond, store, rhs = fetch(near)
        fields = [cond.at[0], cond.at[1], cond.at[2], store, free.get(), rhs]
        ends[...] = pick_z(fetch(got_z), sizes, ends_shape)
        pack_faces(outs, fields, sizes, 2, ends)

    packed = call(
        pack_all,
        face_shapes(shape, sizes, 6, 2),
        (got_z, first["near"], first["free"], rows),
        [pltpu.VMEM(ends_shape, F32)],
    )
    got = send_faces(packed, sizes)

    def first_smooth(got, cond, store, fixed, rhs, got_z, base, outs, sems, step, *boxes):
        boxes = list(boxes)
        cond, store, rhs = fetch((cond, store, rhs))
        owns = [cond.at[0], cond.at[1], cond.at[2], store, None, rhs]
        copies = []
        for k, own in enumerate(owns):
            if own is not None:
                copies.append(
                    pltpu.make_async_copy(own, own_cells(boxes[k], shape), sems.at[k])
                )
                copies[-1].start()
        for b in boxes[:6]:
            clear_round(b, shape)
        got = fetch(got)
        ends = pick_z(fetch(got_z), sizes, ends_shape)
        unpack_faces(boxes[:6], [None] * 6, got["x"], got["y"], sizes, 2, ends)
        unpack_xy(boxes[:6], shape, got["xy"], sizes)
        boxes[4][3 : 3 + nx, 0:ny, 0:nz] = 1.0 - fixed.get()[...].astype(F32)
        for copy in copies:
            copy.wait()
        for target, piece in zip(outs["base"], chunks(vecs, NEAR_FIRST)):
            target.put(base.get().at[piece])
        links, boxes = boxes[6:], boxes[:6]
        coefficients(boxes, links, step, outs["own"])
        outs["kept"]["step"].put(step)
        for kept, link in zip(outs["kept"]["links"], links):
            kept.put(link)
        jacobi(boxes[5], step, links, boxes[0], boxes[1], boxes[5], outs["smooth"])

    smoothed = call(
        first_smooth,
        {
            "smooth": shaped(*shape),
            "own": shaped(7, *shape),
            "base": [Stored(vecs // PARTS, *shape, near=True) for _ in NEAR_FIRST],
            "kept": {
                "links": [Stored(*boxed), Stored(*boxed), Stored(*boxed)],
                "step": Stored(*boxed),
            },
        },
        (
            got,
            Raw(conductance),
            Raw(storage),
            Far(dirichlet),
            Raw(right_side),
            got_z,
            Raw(basis),
        ),
        [pltpu.SemaphoreType.DMA((6,))] + [vbox] * 10,
        flops=SMOOTH_FLOPS,
    )
    kept = smoothed["kept"]
    own = smoothed["own"]

    def base_rest(smoothed, near):
        return smoothed["base"] + [Far(basis, range(len(near), PARTS))]

    def first_direction(smooth, rows, inverse, base, outs):
        smooth, rows = fetch((smooth, rows))
        weights = coarse_weights(inverse.get(), coarse_sum(rows, vecs))
        add_coarse(outs["z"], smooth, base, weights)
        pack_faces(outs["faces"], [outs["z"]], sizes, 1)
        outs["tile"][...] = pack_z([outs["z"]])

    directed = call(
        first_direction,
        {
            "z": shaped(*shape),
            "faces": face_shapes(shape, sizes, 1, 1),
            "tile": shaped(z_rows(1), nx * ny),
        },
        (smoothed["smooth"], rows_a, Far(coarse_inverse), base_rest(smoothed, NEAR_FIRST)),
    )
    direction = directed["z"]
    got = send_faces(directed["faces"], sizes)
    got_z = send_z(directed["tile"], sizes)

    def apply(field, got, got_z, own, out, vb):
        clear_round(vb, shape)
        field, got, got_z = fetch((field, got, got_z))
        unpack_faces([vb], [field], got["x"], got["y"], sizes, 1)
        vb[3 : 3 + nx, 0:ny, nz : nz + LANES] = halo_lanes(pick_z(got_z, sizes, ends_shape), 0)
        own = own.get()

        def body(x, carry):
            mid = vb[x + 3]
            around = (mid, vb[x + 4], vb[x + 2])
            around += (ahead(mid, 0), behind(mid, 0), ahead(mid, 1), behind(mid, 1))
            total = own[0, x] * mid[0:ny, 0:nz]
            for n in range(1, 7):
                total = total - own[n, x] * around[n][0:ny, 0:nz]
            out[x] = total
            return carry

        loop(0, nx, body)

    def first_image(got, got_z, field, own, rhs, outs, vb):
        image = outs["image"]
        outs["own"].put(own.get())
        outs["z"].put(field.get())
        apply(field, got, got_z, own, image, vb)
        outs["kept"].put(image)
        outs["tile"][...] = pack_z([image])
        field, rhs = fetch((field, rhs))
        values = [full_sum(rhs[...] * field[...]), full_sum(field[...] * image[...])]
        outs["sums"][...] = put_scalars(jnp.zeros((1, LANES), F32), vecs, values)

    imaged = call(
        first_image,
        {
            "image": shaped(*shape),
            "kept": Stored(*shape),
            "own": Stored(7, *shape),
            "z": Stored(*shape),
            "tile": shaped(z_rows(1), nx * ny),
            "sums": shaped(1, LANES),
        },
        (got, got_z, direction, own, right_side),
        [vbox],
    )
    got_z = send_z(imaged["tile"], sizes)
    kept_z = imaged["z"]

    def second_rows(base, field, sums, out):
        row = project(base, field.get()[...]) + sums.get()[...]
        out[...] = jnp.broadcast_to(row, out.shape)

    rows = call(second_rows, row_shape, ([basis], imaged["image"], imaged["sums"]))
    rows_c = spread(rows)

    def pack_image(got_z, field, rows, outs, ends):
        ends[...] = pick_z(fetch(got_z), sizes, ends_shape)
        pack_faces(outs, [field.get()], sizes, 2, ends)

    packed = call(
        pack_image,
        face_shapes(shape, sizes, 1, 2),
        (got_z, imaged["image"], rows),
        [pltpu.VMEM(ends_shape, F32)],
    )
    got = send_faces(packed, sizes)

    def second_smooth(got, field, got_z, step, links, base, outs, sem, ga, gb, vb):
        copy = pltpu.make_async_copy(field.get(), own_cells(vb, shape), sem)
        copy.start()
        clear_round(vb, shape)
        got = fetch(got)
        ends = pick_z(fetch(got_z), sizes, ends_shape)
        unpack_faces([vb], [None], got["x"], got["y"], sizes, 2, ends)
        unpack_xy([vb], shape, got["xy"], sizes)
        copy.wait()
        for target, piece in zip(outs["base"], chunks(vecs, NEAR_SECOND)):
            target.put(base.get().at[piece])
        jacobi(vb, step.get(), links, ga, gb, vb, outs["smooth"])

    smoothed = call(
        second_smooth,
        {
            "smooth": shaped(*shape),
            "base": [Stored(vecs // PARTS, *shape, near=True) for _ in NEAR_SECOND],
        },
        (
            got,
            Raw(imaged["kept"]),
            got_z,
            Far(kept["step"]),
            far(kept["links"]),
            Raw(basis),
        ),
        [pltpu.SemaphoreType.DMA] + [vbox] * 3,
        flops=SMOOTH_FLOPS,
    )

    def second_direction(smooth, rows, inverse, field, rhs, before, base, outs):
        smooth, rows = fetch((smooth, rows))
        norm, curve = scalar_sums(rows, vecs, 2)
        alpha = norm / curve
        weights = coarse_weights(inverse.get(), coarse_sum(rows, vecs))
        field, rhs, before = fetch((field, rhs, before))
        outs["residual"][...] = rhs[...] - alpha * field[...]
        add_coarse(outs["z"], smooth, base, weights)
        outs["z"][...] = before[...] - alpha * outs["z"][...]
        pack_faces(outs["faces"], [outs["z"]], sizes, 1)
        outs["tile"][...] = pack_z([outs["z"]])
        outs["scalars"][...] = jnp.concatenate(
            [jnp.broadcast_to(norm, (8, LANES)), jnp.broadcast_to(curve, (8, LANES))], axis=0
        )

    directed = call(
        second_direction,
        {
            "z": shaped(*shape),
            "residual": shaped(*shape),
            "scalars": shaped(16, LANES),
            "faces": face_shapes(shape, sizes, 1, 1),
            "tile": shaped(z_rows(1), nx * ny),
        },
        (
            smoothed["smooth"],
            rows_c,
            Far(coarse_inverse),
            Far(imaged["kept"]),
            Far(right_side),
            Far(kept_z),
            base_rest(smoothed, NEAR_SECOND),
        ),
    )
    precond, residual = directed["z"], directed["residual"]
    got = send_faces(directed["faces"], sizes)
    got_z = send_z(directed["tile"], sizes)
    image, direction = imaged["kept"], kept_z

    def second_image(got, got_z, field, own, image, residual, outs, vb):
        apply(field, got, got_z, own, outs["image"], vb)
        field, image, residual = fetch((field, image, residual))
        values = [
            full_sum(residual[...] * field[...]),
            full_sum(field[...] * outs["image"][...]),
            full_sum(field[...] * image[...]),
        ]
        row = put_scalars(jnp.zeros((1, LANES), F32), 0, values)
        outs["rows"][...] = jnp.broadcast_to(row, outs["rows"].shape)

    last = call(
        second_image,
        {"image": shaped(*shape), "rows": row_shape},
        (
            got,
            got_z,
            precond,
            imaged["own"],
            image,
            residual,
        ),
        [vbox],
    )
    rows_e = spread(last["rows"])

    def finish(rows, scalars, direction, image, precond, precond_image, residual, outs):
        rows, scalars = fetch((rows, scalars))
        norm = scalars[0:1, 0:1]
        curve = scalars[8:9, 0:1]
        norm_next, curve_z, curve_mixed = scalar_sums(rows, 0, 3)
        alpha = norm / curve
        beta = norm_next / norm
        curve_next = curve_z + 2.0 * beta * curve_mixed + beta * beta * curve
        alpha_next = norm_next / curve_next
        direction, image, precond = fetch((direction, image, precond))
        precond_image, residual = fetch((precond_image, residual))
        outs[0][...] = alpha * direction[...] + alpha_next * (
            precond[...] + beta * direction[...]
        )
        outs[1][...] = residual[...] - alpha_next * (precond_image[...] + beta * image[...])

    return tuple(
        call(
            finish,
            [shaped(*shape), shaped(*shape)],
            (rows_e, directed["scalars"], direction, image, precond, last["image"], residual),
        )
    )


def solution(mesh):
    sizes = tuple(mesh.shape[a] for a in AXES)
    placed = (
        P("gx", "gy", "gz"),
        P(None, "gx", "gy", "gz"),
        P("gx", "gy", "gz"),
        P("gx", "gy", "gz"),
        P(None, "gx", "gy", "gz"),
        P(("gx", "gy", "gz"), None),
    )
    return jax.shard_map(
        functools.partial(shards, sizes),
        mesh=mesh,
        in_specs=placed,
        out_specs=(P("gx", "gy", "gz"), P("gx", "gy", "gz")),
        check_vma=False,
    )
```
